32 devices in a mesh: ctx: 4 (over y, x), shard: 8 (over z, core).
Axes of the slice: x: 2, y: 2, z: 4, core: 2. Of those that a mesh axis runs over, the one named last changes fastest.
Arguments:
- tokens: bfloat16 [8, 1024, 1536], P('shard', 'ctx'), may hold values from -6 to 6
- cotangent: bfloat16 [8, 1024, 1536], P('shard', 'ctx'), may hold values from -6 to 6
- routes: int32 [2, 8, 1024, 4], P(None, 'shard', 'ctx'), may hold values from 0 to 7, all different within a row; in each aligned block of 256 rows (0 to 255, 256 to 511, ..., all dimensions but the last counted through in order) at most 160 rows name the same one
- gate_weights: float32 [2, 8, 1024, 4], P(None, 'shard', 'ctx'), may hold values from 0.1 to 0.4
- lengths: int32 [8, 3], P('shard'), may hold values from 1 to 768, 1024 in all within a row
- block_map: int32 [8], replicated, may hold values from 0 to 7, each once
- w_qkv: float32 [2, 1536, 2048], P(None, ('ctx', 'shard')), may hold values from -0.15625 to 0.15625
- w_out: float32 [2, 1536, 1536], P(None, ('ctx', 'shard')), may hold values from -3 to 3
- w_gateup: float32 [2, 8, 1536, 1536], P(None, None, ('ctx', 'shard')), may hold values from -0.15625 to 0.15625
- w_down: float32 [2, 8, 768, 1536], P(None, None, ('ctx', 'shard')), may hold values from -0.625 to 0.625
- gains: float32 [2, 2, 1536], P(None, None, ('ctx', 'shard')), may hold values from 0.5 to 1.5
- m_qkv: float32 [2, 1536, 2048], P(None, ('ctx', 'shard')), may hold values from -64 to 64
- v_qkv: float32 [2, 1536, 2048], P(None, ('ctx', 'shard')), may hold values from 409.6 to 1638.4
- m_out: float32 [2, 1536, 1536], P(None, ('ctx', 'shard')), may hold values from -6 to 6
- v_out: float32 [2, 1536, 1536], P(None, ('ctx', 'shard')), may hold values from 1.6 to 6.4
- m_gateup: float32 [2, 8, 1536, 1536], P(None, None, ('ctx', 'shard')), may hold values from -16 to 16
- v_gateup: float32 [2, 8, 1536, 1536], P(None, None, ('ctx', 'shard')), may hold values from 24.576 to 98.304
- m_down: float32 [2, 8, 768, 1536], P(None, None, ('ctx', 'shard')), may hold values from -6 to 6
- v_down: float32 [2, 8, 768, 1536], P(None, None, ('ctx', 'shard')), may hold values from 4.096 to 16.384
- m_gains: float32 [2, 2, 1536], P(None, None, ('ctx', 'shard')), may hold values from -64 to 64
- v_gains: float32 [2, 2, 1536], P(None, None, ('ctx', 'shard')), may hold values from 409.6 to 1638.4
Outputs:
- output: bfloat16 [8, 1024, 1536], P('shard', 'ctx')
- input_grad: float32 [8, 1024, 1536], P('shard', 'ctx')
- new_qkv: float32 [2, 1536, 2048], P(None, ('ctx', 'shard'))
- moment_qkv: float32 [2, 1536, 2048], P(None, ('ctx', 'shard'))
- second_qkv: float32 [2, 1536, 2048], P(None, ('ctx', 'shard'))
- new_out: float32 [2, 1536, 1536], P(None, ('ctx', 'shard'))
- moment_out: float32 [2, 1536, 1536], P(None, ('ctx', 'shard'))
- second_out: float32 [2, 1536, 1536], P(None, ('ctx', 'shard'))
- new_gateup: float32 [2, 8, 1536, 1536], P(None, None, ('ctx', 'shard'))
- moment_gateup: float32 [2, 8, 1536, 1536], P(None, None, ('ctx', 'shard'))
- second_gateup: float32 [2, 8, 1536, 1536], P(None, None, ('ctx', 'shard'))
- new_down: float32 [2, 8, 768, 1536], P(None, None, ('ctx', 'shard'))
- moment_down: float32 [2, 8, 768, 1536], P(None, None, ('ctx', 'shard'))
- second_down: float32 [2, 8, 768, 1536], P(None, None, ('ctx', 'shard'))
- new_gains: float32 [2, 2, 1536], P(None, None, ('ctx', 'shard'))
- moment_gains: float32 [2, 2, 1536], P(None, None, ('ctx', 'shard'))
- second_gains: float32 [2, 2, 1536], P(None, None, ('ctx', 'shard'))
The draws below stay inside these ranges and needn't reach their ends.
Inputs may be any that keep to these rules, and one draw needn't show every extreme that they name: `routes`: each row names 4 different experts; among the 256 rows of one device (aligned blocks along the length) no expert is named by more than 160 rows. `block_map`: A permutation; the rows of ctx index i hold the stored blocks 2 i and 2 i + 1, each of 128 positions. `lengths`: the 3 documents of each sequence in position order; they sum to 1024.
All inputs are finite; a program needn't handle non-finite values.
Results may differ from the reference program's by a relative error of at most 0.02.
The reference program's roundings to bfloat16 on the way count: a program that leaves them out, or rounds other values in their place, can miss the bound.
Values may be sent and summed in bfloat16 or wider, within the bound.
A program may use at most 576 MiB of HBM per device.

```python
import math
import jax
import jax.numpy as jnp
import numpy as np
from jax import lax

D = 1536
H = 12
KVH = 2
HD = 128
F = 768
TOP = 4
EXPERTS = 8
LAYERS = 2
STEP = 10
DOCS = 3
TOK_DEV = 256
LENGTH = 1024
SEQS = 8
TOKENS = 8192
BLK = 128
CAP = 160
N_CTX = 4


def levels(own_key, dims, split, low, largest):
    def one(dim, shards_of):
        steps = jax.random.uniform(jax.random.fold_in(jax.random.fold_in(own_key, 6), dim), (shards_of,), jnp.float32, low / len(split), largest / len(split))
        return jnp.repeat(jnp.exp(steps), dims[dim] // shards_of).reshape((-1,) + (1,) * (len(dims) - dim - 1))

    level = one(*split[0])
    for cut in split[1:]:
        level = level * one(*cut)
    return level


def length_profile(amount, total, bound, lean):
    portions = [(1 << 20) // math.isqrt(grade ** lean) + 1 for grade in range(2, amount + 1)]
    surplus, given = total - bound - (amount - 1), [1] * (amount - 1)
    while surplus > 0:
        free = [i for i in range(amount - 1) if given[i] < bound]
        mass, remaining = sum([portions[i] for i in free]), surplus
        for i in free:
            extra = min(bound - given[i], max(1, remaining * portions[i] // mass), surplus)
            given[i] = given[i] + extra
            surplus = surplus - extra
    return np.array([bound] + given)


def uneven(own_key, number_of, total, reach, slope):
    if number_of == 2:
        one = jax.random.randint(own_key, (), max(1, total - reach), min(reach, total - 1) + 1)
        return jnp.stack([one, total - one])
    sizes = jnp.asarray(length_profile(number_of, total, reach, slope), jnp.int32)
    couples = (number_of - 1) // 2
    source_of, taker = sizes[1:1 + 2 * couples:2], sizes[2:2 + 2 * couples:2]
    margin = jnp.minimum(source_of - 1, reach - taker)
    moved = jax.random.randint(jax.random.fold_in(own_key, 1), (couples,), 0, 1 << 20) % (margin + 1)
    sizes = sizes.at[1:1 + 2 * couples:2].set(source_of - moved).at[2:2 + 2 * couples:2].set(taker + moved)
    return sizes[jax.random.permutation(jax.random.fold_in(own_key, 2), number_of)]


def assign_block(key, own, number, rows, amount, top, reach, skew):
    order = jax.random.permutation(key, amount)
    heavy_load, common = shares(amount, rows * top, reach, skew, True), shares(amount, rows * top, reach, skew, False)
    places = jnp.arange(amount)

    def named(tallies, turn):
        used = int((tallies > 0).sum())
        fixed = max(1, used // 4)
        passed = fixed + (places - fixed + turn * (used - fixed)) % max(1, amount - fixed)
        return jnp.zeros((amount,), jnp.int32).at[order[jnp.where(places < fixed, places, passed)]].set(jnp.asarray(tallies, jnp.int32))

    tallies = jnp.where(number % 4 == 0, named(heavy_load, number // 4), named(common, number - number // 4 - 1))
    mixed = jax.random.permutation(jax.random.fold_in(own, 3), amount)
    giver, taker = mixed[0:amount // 2 * 2:2], mixed[1:amount // 2 * 2:2]
    margin = jnp.minimum(tallies[giver] - 1, reach - tallies[taker]) // 2
    margin = jnp.where((giver == order[0]) | (taker == order[0]) | (tallies[taker] == 0), 0, jnp.maximum(margin, 0))
    passed = jax.random.randint(jax.random.fold_in(own, 4), (amount // 2,), 0, 1 << 20) % (margin + 1)
    tallies = tallies.at[giver].add(-passed).at[taker].add(passed)
    members = jnp.searchsorted(jnp.cumsum(tallies), jnp.arange(rows * top), side="right").astype(jnp.int32)
    grid = members.reshape(top, rows).T
    grid = grid[jax.random.permutation(jax.random.fold_in(own, 1), rows)]
    turn = jax.random.randint(jax.random.fold_in(own, 2), (rows, 1), 0, top)
    return jnp.take_along_axis(grid, (jnp.arange(top)[None, :] + turn) % top, axis=1)


def shares(count, total, reach, lean, full):
    loads = [(1 << 20) // math.isqrt(rank ** lean) + 1 for rank in range(1, count + 1)]
    largest = reach if full else min(reach, max(-(-total // count), total * loads[0] // sum(loads)))
    least = 1 if total - largest >= count - 1 else 0
    given, spare = [largest] + [least] * (count - 1), total - largest - least * (count - 1)
    while spare > 0:
        movable = [i for i in range(1, count) if given[i] < largest] or [i for i in range(1, count) if given[i] < reach]
        pool, budget = sum([loads[i] for i in movable]), spare
        for i in movable:
            extra = min(reach - given[i], max(1, budget * loads[i] // pool), spare)
            given[i] = given[i] + extra
            spare = spare - extra
    return np.array(given)


def noise(rng, extent, width, most, cuts=(), held_as=jnp.bfloat16):
    gain = levels(rng, extent, cuts, -0.22, 0.18) if cuts else 1.0
    entries = jax.random.normal(rng, extent, jnp.float32) * width * gain
    return jnp.minimum(jnp.maximum(entries, -most), most).astype(held_as)


def setup_inputs(seed: int = 0) -> dict:
    streams_of = jax.random.split(jax.random.key(seed), 22)
    tokens = noise(streams_of[0], (SEQS, LENGTH, D), 1.0, 6.0, ((0, 8), (1, 4)))
    cotangent = noise(streams_of[1], (SEQS, LENGTH, D), 1.0, 6.0, ((0, 8), (1, 4)))
    routes_keys = jax.random.split(jax.random.fold_in(streams_of[2], 1), LAYERS * SEQS * LENGTH // TOK_DEV)
    routes_turns = jax.random.permutation(jax.random.fold_in(streams_of[2], 3), LAYERS * SEQS * LENGTH // TOK_DEV)
    routes = jax.vmap(lambda own, number: assign_block(jax.random.fold_in(streams_of[2], 2), own, number, TOK_DEV, EXPERTS, TOP, CAP, 1))(routes_keys, routes_turns).reshape((LAYERS, SEQS, LENGTH, TOP))
    gate_weights = jnp.clip(jnp.exp(math.log(0.4) - 1.3862944 * jax.random.uniform(streams_of[3], (LAYERS, SEQS, LENGTH, TOP), jnp.float32) ** levels(streams_of[3], (LAYERS, SEQS, LENGTH, TOP), ((1, 8), (2, 4)), -0.2, 0.2)), 0.1, 0.4)
    lengths = jax.vmap(lambda own: uneven(own, DOCS, LENGTH, LENGTH - 2 * BLK, 0))(jax.random.split(streams_of[4], SEQS)).reshape((SEQS, DOCS)).astype(jnp.int32)
    block_map = jax.random.permutation(streams_of[5], 2 * N_CTX).astype(jnp.int32)
    w_qkv = noise(streams_of[6], (LAYERS, D, (H + 2 * KVH) * HD), D ** -0.5, 0.15625, ((1, 32),), jnp.float32)
    w_out = noise(streams_of[7], (LAYERS, H * HD, D), 4 ** -0.5, 3.0, ((1, 32),), jnp.float32)
    w_gateup = noise(streams_of[8], (LAYERS, EXPERTS, D, 2 * F), D ** -0.5, 0.15625, ((2, 32),), jnp.float32)
    w_down = noise(streams_of[9], (LAYERS, EXPERTS, F, D), (F // 8) ** -0.5, 0.625, ((2, 32),), jnp.float32)
    gains = jnp.clip(1.0 + 0.1 * jax.random.normal(streams_of[10], (LAYERS, 2, D), jnp.float32), 0.5, 1.5)
    m_qkv = noise(streams_of[11], (LAYERS, D, (H + 2 * KVH) * HD), (0.11 * TOKENS ** 0.5), 64.0, ((1, 32),), jnp.float32)
    v_qkv = jnp.clip(jnp.exp(math.log(1638.4) - 1.3862944 * jax.random.uniform(streams_of[12], (LAYERS, D, (H + 2 * KVH) * HD), jnp.float32) ** levels(streams_of[12], (LAYERS, D, (H + 2 * KVH) * HD), ((1, 32),), -0.2, 0.2)), 409.6, 1638.4)
    m_out = noise(streams_of[13], (LAYERS, H * HD, D), (0.22 * SEQS ** 0.5), 6.0, ((1, 32),), jnp.float32)
    v_out = jnp.clip(jnp.exp(math.log(6.4) - 1.3862944 * jax.random.uniform(streams_of[14], (LAYERS, H * HD, D), jnp.float32) ** levels(streams_of[14], (LAYERS, H * HD, D), ((1, 32),), -0.2, 0.2)), 1.6, 6.4)
    m_gateup = noise(streams_of[15], (LAYERS, EXPERTS, D, 2 * F), (0.028 * TOKENS ** 0.5), 16.0, ((2, 32),), jnp.float32)
    v_gateup = jnp.clip(jnp.exp(math.log(98.304) - 1.3862944 * jax.random.uniform(streams_of[16], (LAYERS, EXPERTS, D, 2 * F), jnp.float32) ** levels(streams_of[16], (LAYERS, EXPERTS, D, 2 * F), ((2, 32),), -0.2, 0.2)), 24.576, 98.304)
    m_down = noise(streams_of[17], (LAYERS, EXPERTS, F, D), (0.011 * TOKENS ** 0.5), 6.0, ((2, 32),), jnp.float32)
    v_down = jnp.clip(jnp.exp(math.log(16.384) - 1.3862944 * jax.random.uniform(streams_of[18], (LAYERS, EXPERTS, F, D), jnp.float32) ** levels(streams_of[18], (LAYERS, EXPERTS, F, D), ((2, 32),), -0.2, 0.2)), 4.096, 16.384)
    m_gains = noise(streams_of[19], (LAYERS, 2, D), (0.11 * TOKENS ** 0.5), 64.0, ((2, 32),), jnp.float32)
    v_gains = jnp.clip(jnp.exp(math.log(1638.4) - 1.3862944 * jax.random.uniform(streams_of[20], (LAYERS, 2, D), jnp.float32) ** levels(streams_of[20], (LAYERS, 2, D), ((2, 32),), -0.2, 0.2)), 409.6, 1638.4)
    return {"tokens": tokens, "cotangent": cotangent, "routes": routes, "gate_weights": gate_weights, "lengths": lengths, "block_map": block_map, "w_qkv": w_qkv, "w_out": w_out, "w_gateup": w_gateup, "w_down": w_down, "gains": gains, "m_qkv": m_qkv, "v_qkv": v_qkv, "m_out": m_out, "v_out": v_out, "m_gateup": m_gateup, "v_gateup": v_gateup, "m_down": m_down, "v_down": v_down, "m_gains": m_gains, "v_gains": v_gains}


NORM_EPS = 1e-06
ROPE_BASE = 1000000.0
BETA_ONE = 0.9
BETA_TWO = 0.95
ADAM_EPS = 1e-08
DECAY = 0.1
MASKED = -1e+30

@jax.custom_vjp
def low(v):
    return lax.optimization_barrier(v.astype(jnp.bfloat16)).astype(jnp.float32)

@jax.custom_vjp
def low_back(v):
    return v

def low_keep(v):
    return (low(v), None)

def low_pass(kept, grad):
    return (grad,)

def back_keep(v):
    return (v, None)

def back_low(kept, grad):
    return (low(grad),)
low.defvjp(low_keep, low_pass)
low_back.defvjp(back_keep, back_low)

def rope_tables(positions):
    half_width = HD // 2
    frequency = ROPE_BASE ** (-(jnp.arange(half_width, dtype=jnp.float32) * 2.0 / HD))
    angles = positions.astype(jnp.float32)[:, None] * frequency[None, :]
    return (jnp.cos(angles)[:, None, :], jnp.sin(angles)[:, None, :])

def rotate(vectors, cosine_table, sine_table):
    half_width = vectors.shape[-1] // 2
    first_half = vectors[..., :half_width]
    second_half = vectors[..., half_width:]
    return jnp.concatenate([first_half * cosine_table - second_half * sine_table, second_half * cosine_table + first_half * sine_table], axis=-1)

def dispatch(route_rows, gate_rows):
    row_count = route_rows.shape[0]
    flat_routes = route_rows.reshape(-1)
    onehot = (flat_routes[:, None] == jnp.arange(EXPERTS, dtype=jnp.int32)[None, :]).astype(jnp.int32)
    slot_rank = lax.optimization_barrier(jnp.sum((jnp.cumsum(onehot, axis=0) - onehot) * onehot, axis=1))
    owners = jnp.arange(flat_routes.shape[0], dtype=jnp.int32) // TOP
    slot_rows = jnp.full((EXPERTS, CAP), row_count, jnp.int32).at[flat_routes, slot_rank].set(owners)
    slot_gates = jnp.zeros((EXPERTS, CAP), jnp.float32).at[flat_routes, slot_rank].set(gate_rows.reshape(-1))
    return (slot_rows, slot_gates)

def adamw(parameter, moment, second, gradient, step_rate, decay_rate):
    moment = BETA_ONE * moment + (1.0 - BETA_ONE) * gradient
    second = BETA_TWO * second + (1.0 - BETA_TWO) * gradient * gradient
    direction = moment / (1.0 - BETA_ONE ** STEP) / (jnp.sqrt(second / (1.0 - BETA_TWO ** STEP)) + ADAM_EPS)
    return (parameter - step_rate * (direction + decay_rate * parameter), moment, second)

def block_layer(values, qkv_w, out_w, gateup_w, down_w, gain_w, slot_index, slot_gates, allowed, cosine_table, sine_table):
    highest = lax.Precision.HIGHEST
    row_count = values.shape[0]
    group_size = H // KVH
    normed = values * lax.rsqrt(lax.optimization_barrier(jnp.mean(values * values, axis=-1, keepdims=True)) + NORM_EPS) * gain_w[0]
    projected = low_back(jnp.dot(low(normed), qkv_w, precision=highest))
    queries = low(rotate(projected[:, :H * HD].reshape(row_count, H, HD), cosine_table, sine_table))
    queries = queries.reshape(row_count, KVH, group_size, HD)
    keys_rot = low(rotate(projected[:, H * HD:(H + KVH) * HD].reshape(row_count, KVH, HD), cosine_table, sine_table))
    values_head = low(projected[:, (H + KVH) * HD:].reshape(row_count, KVH, HD))
    scores = low_back(HD ** (-0.5) * jnp.einsum('tgjd,kgd->gjtk', queries, keys_rot, precision=highest))
    scores = jnp.where(allowed[None, None], scores, MASKED)
    row_max = lax.optimization_barrier(jnp.max(scores, axis=-1, keepdims=True))
    exponent = jnp.exp(scores - row_max)
    probabilities = low(exponent / lax.optimization_barrier(jnp.sum(exponent, axis=-1, keepdims=True)))
    attended = jnp.einsum('gjtk,kgd->tgjd', probabilities, values_head, precision=highest).reshape(row_count, H * HD)
    values = values + low_back(jnp.dot(low_back(low(attended)), out_w, precision=highest))
    normed_two = values * lax.rsqrt(lax.optimization_barrier(jnp.mean(values * values, axis=-1, keepdims=True)) + NORM_EPS) * gain_w[1]
    padded = jnp.concatenate([low(normed_two), jnp.zeros((1, D), jnp.float32)], axis=0)
    slot_in = padded[slot_index]
    gate_up = low_back(jnp.einsum('necd,edf->necf', slot_in, gateup_w, precision=highest))
    middle = low(jax.nn.gelu(gate_up[..., :F], approximate=False) * gate_up[..., F:])
    result = low_back(low(jnp.einsum('necf,efd->necd', middle, down_w, precision=highest)))
    weighted = (result * slot_gates[..., None]).reshape(-1, D)
    merged = jnp.zeros((row_count + 1, D), jnp.float32).at[slot_index.reshape(-1)].add(weighted)
    return values + merged[:row_count]

def reference(tokens, cotangent, routes, gate_weights, lengths, block_map, w_qkv, w_out, w_gateup, w_down, gains, m_qkv, v_qkv, m_out, v_out, m_gateup, v_gateup, m_down, v_down, m_gains, v_gains):
    block_rows = LENGTH // (2 * N_CTX)
    positions = (block_map[:, None] * block_rows + jnp.arange(block_rows, dtype=jnp.int32)[None, :]).reshape(-1)
    cosine_table, sine_table = rope_tables(positions)
    causal = positions[None, :] <= positions[:, None]
    bounds = jnp.cumsum(lengths, axis=1)
    documents = lax.optimization_barrier(jnp.sum((positions[None, :, None] >= bounds[:, None, :]).astype(jnp.int32), axis=2))
    span_routes = routes.reshape(LAYERS, SEQS, N_CTX, TOK_DEV, TOP)
    span_gates = gate_weights.reshape(LAYERS, SEQS, N_CTX, TOK_DEV, TOP)
    slot_rows, slot_gates = jax.vmap(jax.vmap(jax.vmap(dispatch)))(span_routes, span_gates)
    offsets = (jnp.arange(N_CTX, dtype=jnp.int32) * TOK_DEV)[:, None, None]
    slot_index = jnp.where(slot_rows == TOK_DEV, LENGTH, slot_rows + offsets).astype(jnp.int32)
    slot_index = slot_index.transpose(1, 0, 2, 3, 4)
    slot_gates = slot_gates.transpose(1, 0, 2, 3, 4)

    def forward(inputs, qkv_all, out_all, gateup_all, down_all, gain_all):
        qkv_all = low(qkv_all)
        out_all = low(out_all)
        gateup_all = low(gateup_all)
        down_all = low(down_all)
        gain_all = low(gain_all)

        def sequence(pieces):
            values, seq_docs, seq_index, seq_gates = pieces
            allowed = causal & (seq_docs[:, None] == seq_docs[None, :])
            for layer_index in range(LAYERS):
                values = block_layer(values, qkv_all[layer_index], out_all[layer_index], gateup_all[layer_index], down_all[layer_index], gain_all[layer_index], seq_index[layer_index], seq_gates[layer_index], allowed, cosine_table, sine_table)
            return values
        return lax.map(jax.checkpoint(sequence), (inputs, documents, slot_index, slot_gates))
    inputs = tokens.astype(jnp.float32)
    result, pull = jax.vjp(forward, inputs, w_qkv, w_out, w_gateup, w_down, gains)
    grads_all = pull(cotangent.astype(jnp.float32))
    rates = (D ** (-0.5), 0.5, D ** (-0.5), (F // 8) ** (-0.5), 1.0)
    decays = (DECAY, DECAY, DECAY, DECAY, 0.0)
    params = (w_qkv, w_out, w_gateup, w_down, gains)
    firsts = (m_qkv, m_out, m_gateup, m_down, m_gains)
    seconds = (v_qkv, v_out, v_gateup, v_down, v_gains)
    updated = []
    for which in range(5):
        updated.extend(adamw(params[which], firsts[which], seconds[which], grads_all[which + 1], rates[which], decays[which]))
    return (result.astype(jnp.bfloat16), grads_all[0], updated[0], updated[1], updated[2], updated[3], updated[4], updated[5], updated[6], updated[7], updated[8], updated[9], updated[10], updated[11], updated[12], updated[13], updated[14])
```

```python
import functools

import jax
import jax.numpy as jnp
from jax import lax
from jax.experimental import pallas as pl
from jax.experimental.pallas import tpu as pltpu
from jax.sharding import Mesh
from jax.sharding import PartitionSpec as P

D = 1536
H = 12
KVH = 2
HD = 128
F = 768
TOP = 4
EXPERTS = 8
LAYERS = 2
STEP = 10
CAP = 160


NORM_EPS = 1e-06
ROPE_BASE = 1000000.0
BETA_ONE = 0.9
BETA_TWO = 0.95
ADAM_EPS = 1e-08
DECAY = 0.1
MASKED = -1e30


def rope_tables(positions):
    half_width = HD // 2
    frequency = ROPE_BASE ** (-(jnp.arange(half_width, dtype=jnp.float32) * 2.0 / HD))
    angles = positions.astype(jnp.float32)[:, None] * frequency[None, :]
    return (jnp.cos(angles)[:, None, :], jnp.sin(angles)[:, None, :])


def rotate(vectors, cosine_table, sine_table):
    half_width = vectors.shape[-1] // 2
    first_half = vectors[..., :half_width]
    second_half = vectors[..., half_width:]
    return jnp.concatenate(
        [
            first_half * cosine_table - second_half * sine_table,
            second_half * cosine_table + first_half * sine_table,
        ],
        axis=-1,
    )


def rotate_back(gradient, cosine_table, sine_table):
    half_width = gradient.shape[-1] // 2
    first_half = gradient[..., :half_width]
    second_half = gradient[..., half_width:]
    return jnp.concatenate(
        [
            first_half * cosine_table + second_half * sine_table,
            second_half * cosine_table - first_half * sine_table,
        ],
        axis=-1,
    )


def normalize(values, gain_row):
    row_scale = lax.rsqrt(jnp.mean(values * values, axis=-1, keepdims=True) + NORM_EPS)
    return (values * row_scale * gain_row, row_scale)


def normalize_back(gradient, values, row_scale, gain_row):
    unit_rows = values * row_scale
    inner_grad = gradient * gain_row
    input_grad = row_scale * (
        inner_grad - unit_rows * jnp.mean(inner_grad * unit_rows, axis=-1, keepdims=True)
    )
    return (input_grad, jnp.sum(gradient * unit_rows, axis=0))


def adamw(parameter, moment, second, gradient, step_rate, decay_rate):
    moment = BETA_ONE * moment + (1.0 - BETA_ONE) * gradient
    second = BETA_TWO * second + (1.0 - BETA_TWO) * gradient * gradient
    direction = (
        moment / (1.0 - BETA_ONE**STEP) / (jnp.sqrt(second / (1.0 - BETA_TWO**STEP)) + ADAM_EPS)
    )
    return (parameter - step_rate * (direction + decay_rate * parameter), moment, second)


def glu_value(gate_input, up_input):
    return jax.nn.gelu(gate_input, approximate=False) * up_input


def attention_forward(queries, keys_all, values_all, allowed):
    group_size = H // KVH
    score_scale = HD ** (-0.5)
    outputs = []
    totals = []
    for head_group in range(KVH):
        query_part = queries[:, head_group * group_size : (head_group + 1) * group_size, :]
        scores = (
            jnp.einsum(
                "tjd,kd->jtk",
                query_part,
                keys_all[:, head_group, :],
                preferred_element_type=jnp.float32,
            )
            * score_scale
        )
        scores = jnp.where(allowed[None], scores, MASKED)
        row_max = jnp.max(scores, axis=-1, keepdims=True)
        exponent = jnp.exp(scores - row_max)
        row_total = jnp.sum(exponent, axis=-1, keepdims=True)
        probabilities = (exponent / row_total).astype(jnp.bfloat16)
        outputs.append(
            jnp.einsum(
                "jtk,kd->tjd",
                probabilities,
                values_all[:, head_group, :],
                preferred_element_type=jnp.float32,
            )
        )
        totals.append(row_max + jnp.log(row_total))
    return (jnp.concatenate(outputs, axis=1), totals)


def attention_backward(queries, keys_all, values_all, allowed, totals, grad_attended):
    group_size = H // KVH
    score_scale = HD ** (-0.5)
    grad_queries = []
    grad_keys = []
    grad_values = []
    for head_group in range(KVH):
        query_part = queries[:, head_group * group_size : (head_group + 1) * group_size, :]
        grad_part = grad_attended[:, head_group * group_size : (head_group + 1) * group_size, :]
        keys_part = keys_all[:, head_group, :]
        scores = (
            jnp.einsum("tjd,kd->jtk", query_part, keys_part, preferred_element_type=jnp.float32)
            * score_scale
        )
        probabilities = jnp.where(allowed[None], jnp.exp(scores - totals[head_group]), 0.0)
        grad_probs = jnp.einsum(
            "tjd,kd->jtk",
            grad_part,
            values_all[:, head_group, :],
            preferred_element_type=jnp.float32,
        )
        grad_scores = probabilities * (
            grad_probs - jnp.sum(probabilities * grad_probs, axis=-1, keepdims=True)
        )
        grad_scores = grad_scores.astype(jnp.bfloat16)
        grad_queries.append(
            jnp.einsum("jtk,kd->tjd", grad_scores, keys_part, preferred_element_type=jnp.float32)
            * score_scale
        )
        grad_keys.append(
            jnp.einsum("jtk,tjd->kd", grad_scores, query_part, preferred_element_type=jnp.float32)
            * score_scale
        )
        grad_values.append(
            jnp.einsum(
                "jtk,tjd->kd",
                probabilities.astype(jnp.bfloat16),
                grad_part,
                preferred_element_type=jnp.float32,
            )
        )
    return (
        jnp.concatenate(grad_queries, axis=1),
        jnp.stack(grad_keys, axis=1),
        jnp.stack(grad_values, axis=1),
    )


CTX = ("yo", "xi")
SHARD = ("zo", "zi", "core")
ALL = CTX + SHARD
GROUP = ("xi", "zi")
REPLICAS = ("yo", "zo", "core")


def flat_index(axes):
    index = 0
    for axis in axes:
        index = index * lax.axis_size(axis) + lax.axis_index(axis)
    return index


def shift_permutation(axes, offsets, back=False):
    sizes = [lax.axis_size(axis) for axis in axes]
    pairs = []
    for first in range(sizes[0]):
        for second in range(sizes[1]):
            target = ((first + offsets[0]) % sizes[0], (second + offsets[1]) % sizes[1])
            here = first * sizes[1] + second
            there = target[0] * sizes[1] + target[1]
            pairs.append((there, here) if back else (here, there))
    return pairs


def offsets_of(axes):
    sizes = [lax.axis_size(axis) for axis in axes]
    return [(a, b) for a in range(sizes[0]) for b in range(sizes[1])]


def send(value, axes, offsets, back=False):
    if offsets == (0, 0):
        return value
    return lax.ppermute(value, axes, shift_permutation(axes, offsets, back))


def source_index(axes, offsets):
    sizes = [lax.axis_size(axis) for axis in axes]
    return lax.rem(lax.axis_index(axes[0]) - offsets[0] + sizes[0], sizes[0]) * sizes[1] + lax.rem(
        lax.axis_index(axes[1]) - offsets[1] + sizes[1], sizes[1]
    )


def target_index(axes, offsets):
    sizes = [lax.axis_size(axis) for axis in axes]
    return lax.rem(lax.axis_index(axes[0]) + offsets[0], sizes[0]) * sizes[1] + lax.rem(
        lax.axis_index(axes[1]) + offsets[1], sizes[1]
    )


def positions_docs(block_map, lengths_row, ctx_index, block_rows):
    blocks = lax.dynamic_slice_in_dim(block_map, 2 * ctx_index, 2)
    offsets = jnp.arange(block_rows, dtype=jnp.int32)
    positions = (blocks[:, None] * block_rows + offsets[None, :]).reshape(-1)
    bounds = jnp.cumsum(lengths_row)
    documents = jnp.sum((positions[:, None] >= bounds[None, :]).astype(jnp.int32), axis=1)
    return (positions, documents)


def dispatch_tables(routes, gates):
    rows = routes.shape[0]
    hits = (routes[None] == jnp.arange(EXPERTS, dtype=jnp.int32)[:, None, None]).astype(jnp.float32)
    member = jnp.sum(hits, axis=-1)
    gate = jnp.sum(hits * gates[None], axis=-1)
    before = (jnp.arange(rows)[:, None] < jnp.arange(rows)[None, :]).astype(jnp.float32)
    rank = jnp.dot(member, before, preferred_element_type=jnp.float32)
    return jnp.stack([jnp.where(member > 0, rank, -1.0), gate], axis=1)


def selection(ranks):
    slots = jnp.arange(CAP, dtype=jnp.float32)
    return (ranks[:, None, :] == slots[None, :, None]).astype(jnp.bfloat16)


MESH = pl.DeviceIdType.MESH
QKV = (H + 2 * KVH) * HD


class Place:
    def __init__(self, sizes):
        self.yo_size, self.zo_size = sizes
        self.yo, self.xi, self.zo, self.zi, self.core = [lax.axis_index(axis) for axis in ALL]
        self.y_steps = range(1, self.yo_size)
        self.z_steps = range(1, self.zo_size)
        self.column = [(a, b) for a in range(self.zo_size) for b in range(2)]

    def at(self, y=0, x=0, z=0, w=0, core=0):
        return (
            lax.rem(self.yo + y, self.yo_size),
            1 - self.xi if x else self.xi,
            lax.rem(self.zo + z, self.zo_size),
            1 - self.zi if w else self.zi,
            1 - self.core if core else self.core,
        )

    def chip(self, y=0, x=0, z=0, w=0):
        yo, xi, zo, zi, core = self.at(y, x, z, w)
        return ((yo * 2 + xi) * self.zo_size + zo) * 2 + zi

    def back_y(self, y):
        return (self.yo_size - y) % self.yo_size

    def back_z(self, z):
        return (self.zo_size - z) % self.zo_size


class Wires:
    def __init__(self, send_sems, recv_sems):
        self.send_sems, self.recv_sems = send_sems, recv_sems
        self.started = []

    def send(self, source, target, name, device):
        copy = pltpu.make_async_remote_copy(
            src_ref=source,
            dst_ref=target,
            send_sem=self.send_sems.at[len(self.started)],
            recv_sem=self.recv_sems.at[name],
            device_id=device,
            device_id_type=MESH,
        )
        copy.start()
        self.started.append(copy)

    def arrive(self, target, name, device):
        pltpu.make_async_remote_copy(
            src_ref=target,
            dst_ref=target,
            send_sem=self.send_sems.at[0],
            recv_sem=self.recv_sems.at[name],
            device_id=device,
            device_id_type=MESH,
        ).wait_recv()

    def drain(self):
        for copy in self.started:
            copy.wait_send()


def greet(partners):
    barrier = pltpu.get_barrier_semaphore()
    for partner in partners:
        pl.semaphore_signal(barrier, inc=1, device_id=partner, device_id_type=MESH)
    pl.semaphore_wait(barrier, len(partners))


def mesh_sizes():
    return lax.axis_size("yo"), lax.axis_size("zo")


def add_rows(target, *parts):
    def step(index, carry):
        rows = pl.ds(pl.multiple_of(index * 16, 16), 16)
        total = target[rows, :].astype(jnp.float32)
        for part in parts:
            total = total + part[rows, :].astype(jnp.float32)
        target[rows, :] = total.astype(target.dtype)
        return carry

    lax.fori_loop(0, target.shape[0] // 16, step, 0)


def gather_attention_kernel(sizes, q_ref, o_ref, q_out, o_out, send_sems, recv_sems):
    here = Place(sizes)
    wires = Wires(send_sems, recv_sems)
    shards, wholes = (q_ref, o_ref), (q_out, o_out)
    far = [offset for offset in here.column if offset != (0, 0)]
    greet(
        [here.at(z=z, w=w) for z, w in far]
        + [here.at(x=1), here.at(core=1)]
        + [here.at(y=y) for y in here.y_steps]
    )
    mine = here.chip() * 2 + here.core

    def block(**offsets):
        return here.chip(**offsets) * 2 + here.core

    def name(kind, y, x, z, w):
        return ((((kind * here.yo_size + y) * 2 + x) * here.zo_size + z) * 2 + w) * 2

    for z, w in far:
        for part in range(2):
            wires.send(
                shards[part],
                wholes[part].at[mine],
                name(0, 0, 0, here.back_z(z), w) + part,
                here.at(z=z, w=w),
            )

    def pass_on(source, y, x, z, w, part, to_x, to_y):
        index = block(y=y, x=x, z=z, w=w)
        target = wholes[part].at[index]
        if to_x:
            wires.send(source, target, name(0, y, 1 - x, z, w) + part, here.at(x=1))
        for step in here.y_steps if to_y else ():
            wires.send(
                source,
                target,
                name(0, (y + here.back_y(step)) % here.yo_size, x, z, w) + part,
                here.at(y=step),
            )
        wires.send(source, target, name(1, y, x, z, w) + part, here.at(core=1))

    for z, w in here.column:
        for part in range(2):
            if (z, w) == (0, 0):
                pass_on(shards[part], 0, 0, 0, 0, part, True, True)
                wholes[part][mine] = shards[part][...]
            else:
                source = wholes[part].at[block(z=z, w=w)]
                wires.arrive(source, name(0, 0, 0, z, w) + part, here.at(core=1))
                pass_on(source, 0, 0, z, w, part, True, True)
    for z, w in here.column:
        for part in range(2):
            source = wholes[part].at[block(x=1, z=z, w=w)]
            wires.arrive(source, name(0, 0, 1, z, w) + part, here.at(core=1))
            pass_on(source, 0, 1, z, w, part, False, part == 1)
            for y in here.y_steps:
                source = wholes[part].at[block(y=y, z=z, w=w)]
                wires.arrive(source, name(0, y, 0, z, w) + part, here.at(core=1))
                pass_on(source, y, 0, z, w, part, part == 0, False)
    for z, w in here.column:
        for part in range(2):
            for y in here.y_steps:
                source = wholes[part].at[block(y=y, x=1, z=z, w=w)]
                wires.arrive(source, name(0, y, 1, z, w) + part, here.at(core=1))
                pass_on(source, y, 1, z, w, part, False, False)
    for y in range(here.yo_size):
        for x in range(2):
            for z, w in here.column:
                for part in range(2):
                    index = here.chip(y=y, x=x, z=z, w=w) * 2 + 1 - here.core
                    wires.arrive(
                        wholes[part].at[index], name(1, y, x, z, w) + part, here.at(core=1)
                    )
    wires.drain()


def gather_attention(q_shard, o_shard):
    sizes = mesh_sizes()
    devices = sizes[0] * sizes[1] * 8
    chips = devices // 2
    columns = sizes[1] * 2
    sends = 2 * (columns - 1) + 2 * columns * (sizes[0] + 1) + 4 * columns * (sizes[0] + 1) * 2
    return pl.pallas_call(
        functools.partial(gather_attention_kernel, sizes),
        out_shape=[
            jax.ShapeDtypeStruct((devices,) + shard.shape, shard.dtype)
            for shard in (q_shard, o_shard)
        ],
        in_specs=[pl.BlockSpec(memory_space=pltpu.VMEM)] * 2,
        out_specs=[pl.BlockSpec(memory_space=pltpu.VMEM)] * 2,
        scratch_shapes=[
            pltpu.SemaphoreType.DMA((sends,)),
            pltpu.SemaphoreType.DMA((4 * chips,)),
        ],
        compiler_params=pltpu.CompilerParams(
            collective_id=0, has_side_effects=True, vmem_limit_bytes=40 * 1024 * 1024
        ),
    )(q_shard, o_shard)


def gather_experts_kernel(sizes, u_ref, v_ref, u_out, v_out, send_sems, recv_sems):
    here = Place(sizes)
    wires = Wires(send_sems, recv_sems)
    shards, wholes = (u_ref, v_ref), (u_out, v_out)
    group = [(0, 0), (1, 0), (0, 1), (1, 1)]
    greet(
        [here.at(x=x, w=w) for x, w in group[1:]]
        + [here.at(z=z) for z in here.z_steps]
        + [here.at(y=y) for y in here.y_steps]
        + [here.at(core=1)]
    )

    def name(kind, y, x, z, w):
        return ((((kind * here.yo_size + y) * 2 + x) * here.zo_size + z) * 2 + w) * 2

    def member(x, w):
        yo, xi, zo, zi, core = here.at(x=x, w=w)
        return xi * 2 + zi

    for x, w in group[1:]:
        for part in range(2):
            wires.send(
                shards[part].at[member(x, w)],
                wholes[part].at[0, here.chip()],
                name(0, 0, x, 0, w) + part,
                here.at(x=x, w=w),
            )

    def pass_on(source, y, x, z, w, part, to_z, to_y):
        index = here.chip(y=y, x=x, z=z, w=w)
        for step in here.z_steps if to_z else ():
            wires.send(
                source,
                wholes[part].at[0, index],
                name(0, y, x, (z + here.back_z(step)) % here.zo_size, w) + part,
                here.at(z=step),
            )
        for step in here.y_steps if to_y else ():
            wires.send(
                source,
                wholes[part].at[0, index],
                name(0, (y + here.back_y(step)) % here.yo_size, x, z, w) + part,
                here.at(y=step),
            )
        wires.send(
            source, wholes[part].at[1, index], name(1, y, x, z, w) + part, here.at(core=1)
        )

    for x, w in group:
        for part in range(2):
            if (x, w) == (0, 0):
                pass_on(shards[part].at[member(0, 0)], 0, 0, 0, 0, part, True, True)
                wholes[part][0, here.chip()] = shards[part][member(0, 0)]
            else:
                source = wholes[part].at[0, here.chip(x=x, w=w)]
                wires.arrive(source, name(0, 0, x, 0, w) + part, here.at(core=1))
                pass_on(source, 0, x, 0, w, part, True, True)
    for x, w in group:
        for part in range(2):
            for z in here.z_steps:
                source = wholes[part].at[0, here.chip(x=x, w=w, z=z)]
                wires.arrive(source, name(0, 0, x, z, w) + part, here.at(core=1))
                pass_on(source, 0, x, z, w, part, False, True)
    for z in range(here.zo_size):
        for x, w in group:
            for part in range(2):
                for y in here.y_steps:
                    source = wholes[part].at[0, here.chip(y=y, x=x, w=w, z=z)]
                    wires.arrive(source, name(0, y, x, z, w) + part, here.at(core=1))
                    pass_on(source, y, x, z, w, part, False, False)
    for y in range(here.yo_size):
        for z in range(here.zo_size):
            for x, w in group:
                for part in range(2):
                    target = wholes[part].at[1, here.chip(y=y, x=x, w=w, z=z)]
                    wires.arrive(target, name(1, y, x, z, w) + part, here.at(core=1))
    wires.drain()


def gather_experts(u_parts, v_parts):
    sizes = mesh_sizes()
    chips = sizes[0] * sizes[1] * 4
    sends = 6 + 8 * (sizes[0] + sizes[1] - 1) + 8 * (sizes[1] - 1) * sizes[0] + 2 * chips
    return pl.pallas_call(
        functools.partial(gather_experts_kernel, sizes),
        out_shape=[
            jax.ShapeDtypeStruct((2, chips) + part.shape[1:], part.dtype)
            for part in (u_parts, v_parts)
        ],
        in_specs=[pl.BlockSpec(memory_space=pltpu.VMEM)] * 2,
        out_specs=[pl.BlockSpec(memory_space=pltpu.VMEM)] * 2,
        scratch_shapes=[
            pltpu.SemaphoreType.DMA((sends,)),
            pltpu.SemaphoreType.DMA((4 * chips,)),
        ],
        compiler_params=pltpu.CompilerParams(
            collective_id=1, has_side_effects=True, vmem_limit_bytes=40 * 1024 * 1024
        ),
    )(u_parts, v_parts)


def sum_experts_kernel(sizes, u_ref, v_ref, u_out, v_out, u1, v1, u2, v2, u3, v3, send_sems, recv_sems):
    here = Place(sizes)
    wires = Wires(send_sems, recv_sems)
    group = [(0, 0), (1, 0), (0, 1), (1, 1)]
    whole, outs, first, second, third = (u_ref, v_ref), (u_out, v_out), (u1, v1), (u2, v2), (u3, v3)
    greet(
        [here.at(x=x, w=w) for x, w in group[1:]]
        + [here.at(z=z) for z in here.z_steps]
        + [here.at(y=y) for y in here.y_steps]
        + [here.at(core=1)]
    )
    chips = here.yo_size * here.zo_size * 4

    def place(y, z, member):
        return (y * here.zo_size + z) * 4 + member

    def name(kind, index, part):
        return (kind * chips + index) * 2 + part

    order = [
        (y, z, member)
        for y in list(here.y_steps) + [0]
        for z in list(here.z_steps) + [0]
        for member in range(4)
    ]
    other = here.at(core=1)
    for y, z, member in order:
        x, w = group[member]
        index = here.chip(y=y, x=x, z=z, w=w)
        for part in range(2):
            wires.send(
                whole[part].at[1, index],
                first[part].at[place(y, z, member)],
                name(0, place(y, z, member), part),
                other,
            )
    for y, z, member in order:
        x, w = group[member]
        index = here.chip(y=y, x=x, z=z, w=w)
        for part in range(2):
            spot = place(y, z, member)
            total = first[part].at[spot]
            wires.arrive(total, name(0, spot, part), other)
            if y:
                add_rows(total, whole[part].at[0, index])
                landing = place(here.back_y(y), z, member)
                wires.send(
                    total, second[part].at[landing], name(1, landing, part), here.at(y=y)
                )
                continue
            parts = [whole[part].at[0, index]]
            for step in here.y_steps:
                arrived = second[part].at[place(step, z, member)]
                wires.arrive(arrived, name(1, place(step, z, member), part), other)
                parts.append(arrived)
            if z:
                add_rows(total, *parts)
                landing = here.back_z(z) * 4 + member
                wires.send(total, third[part].at[landing], name(2, landing, part), here.at(z=z))
                continue
            for step in here.z_steps:
                arrived = third[part].at[step * 4 + member]
                wires.arrive(arrived, name(2, step * 4 + member, part), other)
                parts.append(arrived)
            add_rows(total, *parts)
            slot = here.xi * 2 + here.zi
            if member:
                wires.send(
                    total, outs[part].at[slot], name(3, member, part), here.at(x=x, w=w)
                )
            else:
                outs[part][slot] = total[...]
    for member in range(1, 4):
        x, w = group[member]
        yo, xi, zo, zi, core = here.at(x=x, w=w)
        for part in range(2):
            wires.arrive(outs[part].at[xi * 2 + zi], name(3, member, part), other)
    wires.drain()


def sum_experts(u_grads, v_grads):
    sizes = mesh_sizes()
    chips = sizes[0] * sizes[1] * 4
    rows = [grads.shape[1] // chips for grads in (u_grads, v_grads)]
    blocks = [grads.reshape(2, chips, -1, D) for grads in (u_grads, v_grads)]

    def buffers(count):
        return [pltpu.VMEM((count, part, D), jnp.bfloat16) for part in rows]

    return pl.pallas_call(
        functools.partial(sum_experts_kernel, sizes),
        out_shape=[jax.ShapeDtypeStruct((4, part, D), jnp.bfloat16) for part in rows],
        in_specs=[pl.BlockSpec(memory_space=pltpu.VMEM)] * 2,
        out_specs=[pl.BlockSpec(memory_space=pltpu.VMEM)] * 2,
        scratch_shapes=buffers(chips)
        + buffers(chips)
        + buffers(sizes[1] * 4)
        + [
            pltpu.SemaphoreType.DMA((6 * chips,)),
            pltpu.SemaphoreType.DMA((8 * chips,)),
        ],
        compiler_params=pltpu.CompilerParams(
            collective_id=2, has_side_effects=True, vmem_limit_bytes=56 * 1024 * 1024
        ),
    )(*blocks)


def sum_attention_kernel(
    sizes, q_ref, o_ref, q_out, o_out, q1, o1, q2, o2, q3, o3, q4, o4, send_sems, recv_sems
):
    here = Place(sizes)
    wires = Wires(send_sems, recv_sems)
    whole, outs = (q_ref, o_ref), (q_out, o_out)
    first, second, third, fourth = (q1, o1), (q2, o2), (q3, o3), (q4, o4)
    columns = here.column
    far = [offset for offset in columns if offset != (0, 0)]
    other = here.at(core=1)
    greet(
        [here.at(z=z, w=w) for z, w in far]
        + [here.at(x=1), other]
        + [here.at(y=y) for y in here.y_steps]
    )
    chips = here.yo_size * 2 * len(columns)

    def place(y, x, column):
        return (y * 2 + x) * len(columns) + column

    def name(kind, index, part):
        return (kind * chips + index) * 2 + part

    plane = [(y, x) for y in list(here.y_steps) + [0] for x in (1, 0)]
    rounds = [
        (y, x, (column + 1) % len(columns), part)
        for y, x in plane
        for column in range(len(columns))
        for part in range(2)
    ]
    rounds.sort(key=lambda item: (bool(item[0]) + item[1] != 2, not (item[1] if item[3] == 0 else item[0]), not (item[0] or item[1])))
    for y, x, column, part in rounds:
        z, w = columns[column]
        index = here.chip(y=y, x=x, z=z, w=w)
        spot = place(y, x, column)
        wires.send(
            whole[part].at[index, 1 - here.core],
            first[part].at[spot],
            name(0, spot, part),
            other,
        )
    for y, x, column, part in rounds:
        z, w = columns[column]
        index = here.chip(y=y, x=x, z=z, w=w)
        spot = place(y, x, column)
        total = first[part].at[spot]
        wires.arrive(total, name(0, spot, part), other)
        parts = [whole[part].at[index, here.core]]
        if part == 0:
            if x:
                add_rows(total, *parts)
                landing = place(y, 0, column)
                wires.send(total, second[0].at[landing], name(1, landing, 0), here.at(x=1))
                continue
            arrived = second[0].at[place(y, 0, column)]
            wires.arrive(arrived, name(1, place(y, 0, column), 0), other)
            parts.append(arrived)
            if y:
                add_rows(total, *parts)
                landing = place(here.back_y(y), 0, column)
                wires.send(total, third[0].at[landing], name(2, landing, 0), here.at(y=y))
                continue
            for step in here.y_steps:
                arrived = third[0].at[place(step, 0, column)]
                wires.arrive(arrived, name(2, place(step, 0, column), 0), other)
                parts.append(arrived)
        else:
            if y:
                add_rows(total, *parts)
                landing = place(here.back_y(y), x, column)
                wires.send(total, second[1].at[landing], name(1, landing, 1), here.at(y=y))
                continue
            for step in here.y_steps:
                arrived = second[1].at[place(step, x, column)]
                wires.arrive(arrived, name(1, place(step, x, column), 1), other)
                parts.append(arrived)
            if x:
                add_rows(total, *parts)
                landing = place(0, 0, column)
                wires.send(total, third[1].at[landing], name(2, landing, 1), here.at(x=1))
                continue
            arrived = third[1].at[place(0, 0, column)]
            wires.arrive(arrived, name(2, place(0, 0, column), 1), other)
            parts.append(arrived)
        if column:
            add_rows(total, *parts)
            landing = columns.index((here.back_z(z), w))
            wires.send(
                total, fourth[part].at[landing], name(3, landing, part), here.at(z=z, w=w)
            )
            continue
        for step in range(1, len(columns)):
            arrived = fourth[part].at[step]
            wires.arrive(arrived, name(3, step, part), other)
            parts.append(arrived)
        add_rows(total, *parts)
        outs[part][...] = total[...]
    wires.drain()


def sum_attention(q_grads, o_grads):
    sizes = mesh_sizes()
    chips = sizes[0] * sizes[1] * 4
    rows = q_grads.shape[0] // (2 * chips)
    widths = [grads.shape[1] for grads in (q_grads, o_grads)]
    blocks = [grads.reshape(chips, 2, rows, -1) for grads in (q_grads, o_grads)]

    def buffers(count):
        return [pltpu.VMEM((count, rows, width), jnp.bfloat16) for width in widths]

    return pl.pallas_call(
        functools.partial(sum_attention_kernel, sizes),
        out_shape=[jax.ShapeDtypeStruct((rows, width), jnp.bfloat16) for width in widths],
        in_specs=[pl.BlockSpec(memory_space=pltpu.VMEM)] * 2,
        out_specs=[pl.BlockSpec(memory_space=pltpu.VMEM)] * 2,
        scratch_shapes=buffers(chips)
        + buffers(chips)
        + buffers(chips)
        + buffers(sizes[1] * 2)
        + [
            pltpu.SemaphoreType.DMA((6 * chips,)),
            pltpu.SemaphoreType.DMA((8 * chips,)),
        ],
        compiler_params=pltpu.CompilerParams(
            collective_id=3, has_side_effects=True, vmem_limit_bytes=56 * 1024 * 1024
        ),
    )(*blocks)


def swap(value, axis):
    return lax.ppermute(value, axis, [(0, 1), (1, 0)])


def pick(value, index, axis=0):
    return lax.dynamic_index_in_dim(value, index, axis, keepdims=False)


def by_core(mine, theirs, axis):
    core = lax.axis_index("core")
    return jnp.where(
        core == 0, jnp.stack([mine, theirs], axis), jnp.stack([theirs, mine], axis)
    )


def all_gains(gains):
    whole = lax.all_gather(gains.astype(jnp.bfloat16), ALL, axis=2, tiled=True)
    return whole.astype(jnp.float32)


def attention_weights_direct(w_qkv, w_out, layer):
    q_whole, o_whole = gather_attention(
        w_qkv[layer].astype(jnp.bfloat16), w_out[layer].astype(jnp.bfloat16)
    )
    return q_whole.reshape(D, QKV), o_whole.reshape(D, D)


def expert_weights_direct(w_gateup, w_down, layer):
    core = lax.axis_index("core")
    parts = []
    for shard in (w_gateup[layer], w_down[layer]):
        shard = shard.astype(jnp.bfloat16)
        shard = shard.reshape((4, 2) + shard.shape[1:])
        theirs = swap(pick(shard, 1 - core, 1), "core")
        parts.append(by_core(pick(shard, core, 1), theirs, 1).reshape(4, -1, D))
    up, down = gather_experts(*parts)
    return up.reshape(2, D, 2 * F), down.reshape(2, F, D)


def expert_grads_direct(grad_up, grad_down):
    core = lax.axis_index("core")
    result = []
    for part in sum_experts(grad_up.astype(jnp.bfloat16), grad_down.astype(jnp.bfloat16)):
        part = part.reshape(4, 2, -1, D)
        theirs = swap(pick(part, 1 - core, 1), "core")
        pair = by_core(pick(part, core, 1), theirs, 1)
        result.append(pair.reshape(EXPERTS, -1, D).astype(jnp.float32))
    return result


def attention_grads_direct(grad_qkv, grad_out):
    sums = sum_attention(grad_qkv.astype(jnp.bfloat16), grad_out.astype(jnp.bfloat16))
    return [part.astype(jnp.float32) for part in sums]


def attention_weights(w_qkv, w_out, layer):
    packed = jnp.concatenate(
        [w_qkv[layer].astype(jnp.bfloat16), w_out[layer].astype(jnp.bfloat16)], axis=1
    )
    whole = lax.all_gather(packed, ALL, axis=0, tiled=True)
    return whole[:, :QKV], whole[:, QKV:]


def relative_order(axes, back=False):
    pick = target_index if back else source_index
    return jnp.stack([pick(axes, offsets) for offsets in offsets_of(axes)])


def to_absolute(pieces, axes):
    stacked = jnp.stack(pieces)
    order = relative_order(axes)
    return stacked[order]


def expert_weights(w_gateup, w_down, layer):
    packed = jnp.concatenate(
        [w_gateup[layer].astype(jnp.bfloat16), w_down[layer].astype(jnp.bfloat16)], axis=1
    )
    rows_up = w_gateup.shape[2]
    pieces = []
    for offsets in offsets_of(GROUP):
        mine = lax.dynamic_slice_in_dim(packed, 2 * target_index(GROUP, offsets), 2)
        pieces.append(send(mine, GROUP, offsets))
    by_source = to_absolute(pieces, GROUP)
    whole = lax.all_gather(by_source, REPLICAS, axis=0)
    yo, zo = lax.axis_size("yo"), lax.axis_size("zo")
    whole = whole.reshape((yo, zo, 2, 2, 2, 2) + by_source.shape[2:])
    whole = whole.transpose(5, 0, 3, 1, 4, 2, 6, 7)
    up = whole[..., :rows_up, :].reshape(2, D, 2 * F)
    down = whole[..., rows_up:, :].reshape(2, F, D)
    return up, down


def expert_grads(grad_up, grad_down):
    yo, zo = lax.axis_size("yo"), lax.axis_size("zo")

    def split(whole):
        blocks = whole.astype(jnp.bfloat16).reshape((2, yo, 2, zo, 2, 2, -1) + whole.shape[2:])
        return blocks.transpose(1, 3, 5, 2, 4, 0, 6, 7)

    packed = jnp.concatenate([split(grad_up), split(grad_down)], axis=6)
    rows = packed.shape[6]
    packed = packed.reshape((yo * zo * 2, 4, 2, rows, D))
    summed = lax.psum_scatter(packed, REPLICAS, scatter_dimension=0, tiled=False)
    pieces = []
    for offsets in offsets_of(GROUP):
        theirs = lax.dynamic_index_in_dim(summed, target_index(GROUP, offsets), 0, keepdims=False)
        pieces.append(send(theirs, GROUP, offsets))
    by_source = to_absolute(pieces, GROUP).reshape(EXPERTS, rows, D).astype(jnp.float32)
    rows_up = rows * 2 // 3
    return by_source[:, :rows_up], by_source[:, rows_up:]


def attention_grads(grad_qkv, grad_out):
    packed = jnp.concatenate(
        [grad_qkv.astype(jnp.bfloat16), grad_out.astype(jnp.bfloat16)], axis=1
    )
    summed = lax.psum_scatter(packed, ALL, scatter_dimension=0, tiled=True).astype(jnp.float32)
    return summed[:, :QKV], summed[:, QKV:]


def experts_forward(chunk, table, weights):
    up_w, down_w = weights
    select = selection(table[:, 0])
    slot_in = jnp.einsum("jst,td->jsd", select, chunk, preferred_element_type=jnp.float32)
    slot_in = slot_in.astype(jnp.bfloat16)
    gate_up = jnp.einsum("jsd,jdf->jsf", slot_in, up_w, preferred_element_type=jnp.float32)
    activated = glu_value(gate_up[..., :F], gate_up[..., F:]).astype(jnp.bfloat16)
    result = jnp.einsum("jsf,jfd->jsd", activated, down_w, preferred_element_type=jnp.float32)
    result = result.astype(jnp.bfloat16)
    spread = jnp.einsum("jst,jsd->jtd", select, result, preferred_element_type=jnp.float32)
    merged = jnp.sum(spread * table[:, 1, :, None], axis=0)
    return merged, (slot_in, gate_up, activated)


def experts_backward(gradient, table, weights, kept):
    up_w, down_w = weights
    slot_in, gate_up, activated = kept
    select = selection(table[:, 0])
    weighted = (table[:, 1, :, None] * gradient.astype(jnp.float32)[None]).astype(jnp.bfloat16)
    slot_grad = jnp.einsum("jst,jtd->jsd", select, weighted, preferred_element_type=jnp.float32)
    slot_grad = slot_grad.astype(jnp.bfloat16)
    grad_act = jnp.einsum("jsd,jfd->jsf", slot_grad, down_w, preferred_element_type=jnp.float32)
    unused, pull = jax.vjp(glu_value, gate_up[..., :F], gate_up[..., F:])
    grad_gate, grad_up = pull(grad_act)
    grad_glu = jnp.concatenate([grad_gate, grad_up], axis=-1).astype(jnp.bfloat16)
    grad_slots = jnp.einsum("jsf,jdf->jsd", grad_glu, up_w, preferred_element_type=jnp.float32)
    grad_rows = jnp.einsum(
        "jst,jsd->td", select, grad_slots.astype(jnp.bfloat16), preferred_element_type=jnp.float32
    )
    return grad_rows, (slot_grad, grad_glu)


def moe_forward(expert_in, tables, weights):
    total = None
    kept = []
    for place, offsets in enumerate(offsets_of(GROUP)):
        chunk = send(expert_in, GROUP, offsets)
        merged, record = experts_forward(chunk, tables[place], weights)
        kept.append(record)
        if offsets != (0, 0):
            merged = send(merged.astype(jnp.bfloat16), GROUP, offsets, back=True)
            merged = merged.astype(jnp.float32)
        total = merged if total is None else total + merged
    return total, kept


def moe_backward(gradient, tables, weights, kept):
    low = gradient.astype(jnp.bfloat16)
    total = None
    parts = []
    for place, offsets in enumerate(offsets_of(GROUP)):
        chunk = gradient if offsets == (0, 0) else send(low, GROUP, offsets)
        rows, record = experts_backward(chunk, tables[place], weights, kept[place])
        parts.append(record)
        if offsets != (0, 0):
            rows = send(rows.astype(jnp.bfloat16), GROUP, offsets, back=True).astype(jnp.float32)
        total = rows if total is None else total + rows
    slot_grad = jnp.concatenate([part[0] for part in parts], axis=1)
    grad_glu = jnp.concatenate([part[1] for part in parts], axis=1)
    slot_in = jnp.concatenate([record[0] for record in kept], axis=1)
    activated = jnp.concatenate([record[2] for record in kept], axis=1)
    grad_down = jnp.einsum("jsf,jsd->jfd", activated, slot_grad, preferred_element_type=jnp.float32)
    grad_up = jnp.einsum("jsd,jsf->jdf", slot_in, grad_glu, preferred_element_type=jnp.float32)
    return total, grad_up, grad_down


def layer_forward(stream, attn_w, expert_w, tables, allowed, cosine_table, sine_table):
    qkv_w, out_w, gain_full = attn_w
    row_count = stream.shape[0]
    normed, scale_one = normalize(stream, gain_full[0])
    attn_in = normed.astype(jnp.bfloat16)
    projected = jnp.dot(attn_in, qkv_w, preferred_element_type=jnp.float32)
    queries = rotate(
        projected[:, : H * HD].reshape(row_count, H, HD), cosine_table, sine_table
    ).astype(jnp.bfloat16)
    keys_local = rotate(
        projected[:, H * HD : (H + KVH) * HD].reshape(row_count, KVH, HD), cosine_table, sine_table
    ).astype(jnp.bfloat16)
    values_local = projected[:, (H + KVH) * HD :].reshape(row_count, KVH, HD).astype(jnp.bfloat16)
    both = jnp.concatenate([keys_local, values_local], axis=1)
    both_all = jnp.concatenate([send(both, CTX, offsets) for offsets in offsets_of(CTX)], axis=0)
    keys_all, values_all = both_all[:, :KVH], both_all[:, KVH:]
    attended, totals = attention_forward(queries, keys_all, values_all, allowed)
    attended_low = attended.reshape(row_count, H * HD).astype(jnp.bfloat16)
    middle_stream = stream + jnp.dot(attended_low, out_w, preferred_element_type=jnp.float32)
    normed_two, scale_two = normalize(middle_stream, gain_full[1])
    expert_in = normed_two.astype(jnp.bfloat16)
    merged, kept = moe_forward(expert_in, tables, expert_w)
    record = {
        "stream": stream,
        "scale_one": scale_one,
        "attn_in": attn_in,
        "queries": queries,
        "keys_all": keys_all,
        "values_all": values_all,
        "totals": totals,
        "attended": attended_low,
        "middle": middle_stream,
        "scale_two": scale_two,
        "kept": kept,
    }
    return (record, middle_stream + merged)


def layer_backward(gradient, record, attn_w, expert_w, tables, allowed, cosine_table, sine_table):
    qkv_w, out_w, gain_full = attn_w
    row_count = gradient.shape[0]
    grad_normed, grad_up, grad_down = moe_backward(gradient, tables, expert_w, record["kept"])
    grad_in_two, grad_gain_two = normalize_back(
        grad_normed, record["middle"], record["scale_two"], gain_full[1]
    )
    grad_middle = gradient + grad_in_two
    grad_middle_low = grad_middle.astype(jnp.bfloat16)
    grad_out = jnp.dot(record["attended"].T, grad_middle_low, preferred_element_type=jnp.float32)
    grad_attended = jnp.dot(grad_middle_low, out_w.T, preferred_element_type=jnp.float32)
    grad_attended = grad_attended.astype(jnp.bfloat16).reshape(row_count, H, HD)
    grad_queries, grad_keys_all, grad_values_all = attention_backward(
        record["queries"],
        record["keys_all"],
        record["values_all"],
        allowed,
        record["totals"],
        grad_attended,
    )
    both_all = jnp.concatenate([grad_keys_all, grad_values_all], axis=1)
    both = None
    for place, offsets in enumerate(offsets_of(CTX)):
        part = both_all[place * row_count : (place + 1) * row_count]
        if offsets != (0, 0):
            part = send(part.astype(jnp.bfloat16), CTX, offsets, back=True).astype(jnp.float32)
        both = part if both is None else both + part
    grad_keys, grad_values = both[:, :KVH], both[:, KVH:]
    grad_projected = jnp.concatenate(
        [
            rotate_back(grad_queries, cosine_table, sine_table).reshape(row_count, H * HD),
            rotate_back(grad_keys, cosine_table, sine_table).reshape(row_count, KVH * HD),
            grad_values.reshape(row_count, KVH * HD),
        ],
        axis=1,
    ).astype(jnp.bfloat16)
    grad_qkv = jnp.dot(record["attn_in"].T, grad_projected, preferred_element_type=jnp.float32)
    grad_normed_one = jnp.dot(grad_projected, qkv_w.T, preferred_element_type=jnp.float32)
    grad_in_one, grad_gain_one = normalize_back(
        grad_normed_one, record["stream"], record["scale_one"], gain_full[0]
    )
    grad_gains = jnp.stack([grad_gain_one, grad_gain_two])
    return (grad_middle + grad_in_one, (grad_qkv, grad_out, grad_up, grad_down, grad_gains))


def on_device(
    tokens,
    cotangent,
    routes,
    gate_weights,
    lengths,
    block_map,
    w_qkv,
    w_out,
    w_gateup,
    w_down,
    gains,
    m_qkv,
    v_qkv,
    m_out,
    v_out,
    m_gateup,
    v_gateup,
    m_down,
    v_down,
    m_gains,
    v_gains,
):
    row_count = tokens.shape[1]
    block_rows = row_count // 2
    own_pos, own_doc = positions_docs(block_map, lengths[0], flat_index(CTX), block_rows)
    places = [
        positions_docs(block_map, lengths[0], source_index(CTX, offsets), block_rows)
        for offsets in offsets_of(CTX)
    ]
    key_pos = jnp.concatenate([place[0] for place in places])
    key_doc = jnp.concatenate([place[1] for place in places])
    allowed = (own_doc[:, None] == key_doc[None, :]) & (key_pos[None, :] <= own_pos[:, None])
    cosine_table, sine_table = rope_tables(own_pos)
    own_tables = jnp.stack(
        [dispatch_tables(routes[layer, 0], gate_weights[layer, 0]) for layer in range(LAYERS)]
    )
    core = lax.axis_index("core")
    group_tables = []
    for offsets in offsets_of(GROUP):
        theirs = lax.dynamic_slice_in_dim(own_tables, 2 * target_index(GROUP, offsets), 2, axis=1)
        theirs = jnp.stack([jnp.where(core == 0, theirs[0], theirs[0, ::-1]), theirs[1]])
        group_tables.append(send(theirs, GROUP, offsets))
    stream = tokens[0].astype(jnp.float32)
    records = []
    gains_full = all_gains(gains)
    attn_w = [
        attention_weights_direct(w_qkv, w_out, 0) + (gains_full[0],),
        attention_weights(w_qkv, w_out, 1) + (gains_full[1],),
    ]
    expert_w = [
        expert_weights_direct(w_gateup, w_down, 0),
        expert_weights(w_gateup, w_down, 1),
    ]
    for layer_index in range(LAYERS):
        record, stream = layer_forward(
            stream,
            attn_w[layer_index],
            expert_w[layer_index],
            [table[layer_index] for table in group_tables],
            allowed,
            cosine_table,
            sine_table,
        )
        records.append(record)
    output = stream.astype(jnp.bfloat16)[None]
    gradient = cotangent[0].astype(jnp.float32)
    rates = (D ** (-0.5), 0.5, D ** (-0.5), (F // 8) ** (-0.5), 1.0)
    decays = (DECAY, DECAY, DECAY, DECAY, 0.0)
    params = (w_qkv, w_out, w_gateup, w_down, gains)
    firsts = (m_qkv, m_out, m_gateup, m_down, m_gains)
    seconds = (v_qkv, v_out, v_gateup, v_down, v_gains)
    updated = [[None] * LAYERS for which in range(15)]
    for layer_index in reversed(range(LAYERS)):
        gradient, layer_grads = layer_backward(
            gradient,
            records[layer_index],
            attn_w[layer_index],
            expert_w[layer_index],
            [table[layer_index] for table in group_tables],
            allowed,
            cosine_table,
            sine_table,
        )
        gain = lax.psum_scatter(layer_grads[4].T, ALL, scatter_dimension=0, tiled=True).T
        if layer_index:
            up, down = expert_grads(layer_grads[2], layer_grads[3])
            qkv, out = attention_grads(layer_grads[0], layer_grads[1])
        else:
            up, down = expert_grads_direct(layer_grads[2], layer_grads[3])
            qkv, out = attention_grads_direct(layer_grads[0], layer_grads[1])
        reduced = (qkv, out, up, down, gain)
        for which in range(5):
            fresh = adamw(
                params[which][layer_index],
                firsts[which][layer_index],
                seconds[which][layer_index],
                reduced[which],
                rates[which],
                decays[which],
            )
            updated[3 * which][layer_index] = fresh[0]
            updated[3 * which + 1][layer_index] = fresh[1]
            updated[3 * which + 2][layer_index] = fresh[2]
    stacked = [jnp.stack(pieces) for pieces in updated]
    return (output, gradient[None], *stacked)


def solution(mesh):
    ctx_size, shard_size = mesh.shape["ctx"], mesh.shape["shard"]
    fine = Mesh(mesh.devices.reshape(ctx_size // 2, 2, shard_size // 4, 2, 2), ALL)
    tokens = P(SHARD, CTX, None)
    routed = P(None, SHARD, CTX, None)
    rows_two = P(None, ALL, None)
    rows_three = P(None, None, ALL, None)
    gain = P(None, None, ALL)
    weights = (rows_two, rows_two, rows_three, rows_three, gain)
    states = tuple(spec for spec in weights for which in range(2))
    return jax.shard_map(
        on_device,
        mesh=fine,
        in_specs=(tokens, tokens, routed, routed, P(SHARD, None), P()) + weights + states,
        out_specs=(tokens, tokens) + tuple(spec for spec in weights for which in range(3)),
        check_vma=False,
    )
```

```python
import functools

import jax
import jax.numpy as jnp
from jax import lax
from jax.experimental import pallas as pl
from jax.experimental.pallas import tpu as pltpu
from jax.sharding import Mesh
from jax.sharding import PartitionSpec as P

D = 1536
H = 12
KVH = 2
HD = 128
F = 768
TOP = 4
EXPERTS = 8
LAYERS = 2
STEP = 10
CAP = 160


NORM_EPS = 1e-06
ROPE_BASE = 1000000.0
BETA_ONE = 0.9
BETA_TWO = 0.95
ADAM_EPS = 1e-08
DECAY = 0.1
MASKED = -1e30


def rope_tables(positions):
    half_width = HD // 2
    frequency = ROPE_BASE ** (-(jnp.arange(half_width, dtype=jnp.float32) * 2.0 / HD))
    angles = positions.astype(jnp.float32)[:, None] * frequency[None, :]
    return (jnp.cos(angles)[:, None, :], jnp.sin(angles)[:, None, :])


def rotate(vectors, cosine_table, sine_table):
    half_width = vectors.shape[-1] // 2
    first_half = vectors[..., :half_width]
    second_half = vectors[..., half_width:]
    return jnp.concatenate(
        [
            first_half * cosine_table - second_half * sine_table,
            second_half * cosine_table + first_half * sine_table,
        ],
        axis=-1,
    )


def rotate_back(gradient, cosine_table, sine_table):
    half_width = gradient.shape[-1] // 2
    first_half = gradient[..., :half_width]
    second_half = gradient[..., half_width:]
    return jnp.concatenate(
        [
            first_half * cosine_table + second_half * sine_table,
            second_half * cosine_table - first_half * sine_table,
        ],
        axis=-1,
    )


def normalize(values, gain_row):
    row_scale = lax.rsqrt(jnp.mean(values * values, axis=-1, keepdims=True) + NORM_EPS)
    return (values * row_scale * gain_row, row_scale)


def normalize_back(gradient, values, row_scale, gain_row):
    unit_rows = values * row_scale
    inner_grad = gradient * gain_row
    input_grad = row_scale * (
        inner_grad - unit_rows * jnp.mean(inner_grad * unit_rows, axis=-1, keepdims=True)
    )
    return (input_grad, jnp.sum(gradient * unit_rows, axis=0))


def adamw(parameter, moment, second, gradient, step_rate, decay_rate):
    moment = BETA_ONE * moment + (1.0 - BETA_ONE) * gradient
    second = BETA_TWO * second + (1.0 - BETA_TWO) * gradient * gradient
    direction = (
        moment / (1.0 - BETA_ONE**STEP) / (jnp.sqrt(second / (1.0 - BETA_TWO**STEP)) + ADAM_EPS)
    )
    return (parameter - step_rate * (direction + decay_rate * parameter), moment, second)


def attention_forward(queries, keys_all, values_all, allowed):
    group_size = H // KVH
    score_scale = HD ** (-0.5)
    outputs = []
    totals = []
    for head_group in range(KVH):
        query_part = queries[:, head_group * group_size : (head_group + 1) * group_size, :]
        scores = (
            jnp.einsum(
                "tjd,kd->jtk",
                query_part,
                keys_all[:, head_group, :],
                preferred_element_type=jnp.float32,
            )
            * score_scale
        )
        scores = jnp.where(allowed[None], scores, MASKED)
        row_max = jnp.max(scores, axis=-1, keepdims=True)
        exponent = jnp.exp(scores - row_max)
        row_total = jnp.sum(exponent, axis=-1, keepdims=True)
        probabilities = (exponent / row_total).astype(jnp.bfloat16)
        outputs.append(
            jnp.einsum(
                "jtk,kd->tjd",
                probabilities,
                values_all[:, head_group, :],
                preferred_element_type=jnp.float32,
            )
        )
        totals.append(row_max + jnp.log(row_total))
    return (jnp.concatenate(outputs, axis=1), totals)


def attention_backward(queries, keys_all, values_all, allowed, totals, grad_attended):
    group_size = H // KVH
    score_scale = HD ** (-0.5)
    grad_queries = []
    grad_keys = []
    grad_values = []
    for head_group in range(KVH):
        query_part = queries[:, head_group * group_size : (head_group + 1) * group_size, :]
        grad_part = grad_attended[:, head_group * group_size : (head_group + 1) * group_size, :]
        keys_part = keys_all[:, head_group, :]
        scores = (
            jnp.einsum("tjd,kd->jtk", query_part, keys_part, preferred_element_type=jnp.float32)
            * score_scale
        )
        probabilities = jnp.where(allowed[None], jnp.exp(scores - totals[head_group]), 0.0)
        grad_probs = jnp.einsum(
            "tjd,kd->jtk",
            grad_part,
            values_all[:, head_group, :],
            preferred_element_type=jnp.float32,
        )
        grad_scores = probabilities * (
            grad_probs - jnp.sum(probabilities * grad_probs, axis=-1, keepdims=True)
        )
        grad_scores = grad_scores.astype(jnp.bfloat16)
        grad_queries.append(
            jnp.einsum("jtk,kd->tjd", grad_scores, keys_part, preferred_element_type=jnp.float32)
            * score_scale
        )
        grad_keys.append(
            jnp.einsum("jtk,tjd->kd", grad_scores, query_part, preferred_element_type=jnp.float32)
            * score_scale
        )
        grad_values.append(
            jnp.einsum(
                "jtk,tjd->kd",
                probabilities.astype(jnp.bfloat16),
                grad_part,
                preferred_element_type=jnp.float32,
            )
        )
    return (
        jnp.concatenate(grad_queries, axis=1),
        jnp.stack(grad_keys, axis=1),
        jnp.stack(grad_values, axis=1),
    )


CTX = ("yo", "xi")
SHARD = ("zo", "zi", "core")
ALL = CTX + SHARD
GROUP = ("xi", "zi")
REPLICAS = ("yo", "zo", "core")


def flat_index(axes):
    index = 0
    for axis in axes:
        index = index * lax.axis_size(axis) + lax.axis_index(axis)
    return index


def shift_permutation(axes, offsets, back=False):
    sizes = [lax.axis_size(axis) for axis in axes]
    pairs = []
    for first in range(sizes[0]):
        for second in range(sizes[1]):
            target = ((first + offsets[0]) % sizes[0], (second + offsets[1]) % sizes[1])
            here = first * sizes[1] + second
            there = target[0] * sizes[1] + target[1]
            pairs.append((there, here) if back else (here, there))
    return pairs


def offsets_of(axes):
    sizes = [lax.axis_size(axis) for axis in axes]
    return [(a, b) for a in range(sizes[0]) for b in range(sizes[1])]


def send(value, axes, offsets, back=False):
    if offsets == (0, 0):
        return value
    return lax.ppermute(value, axes, shift_permutation(axes, offsets, back))


def source_index(axes, offsets):
    sizes = [lax.axis_size(axis) for axis in axes]
    return lax.rem(lax.axis_index(axes[0]) - offsets[0] + sizes[0], sizes[0]) * sizes[1] + lax.rem(
        lax.axis_index(axes[1]) - offsets[1] + sizes[1], sizes[1]
    )


def target_index(axes, offsets):
    sizes = [lax.axis_size(axis) for axis in axes]
    return lax.rem(lax.axis_index(axes[0]) + offsets[0], sizes[0]) * sizes[1] + lax.rem(
        lax.axis_index(axes[1]) + offsets[1], sizes[1]
    )


def positions_docs(block_map, lengths_row, ctx_index, block_rows):
    blocks = lax.dynamic_slice_in_dim(block_map, 2 * ctx_index, 2)
    offsets = jnp.arange(block_rows, dtype=jnp.int32)
    positions = (blocks[:, None] * block_rows + offsets[None, :]).reshape(-1)
    bounds = jnp.cumsum(lengths_row)
    documents = jnp.sum((positions[:, None] >= bounds[None, :]).astype(jnp.int32), axis=1)
    return (positions, documents)


def dispatch_tables(routes, gates):
    rows = routes.shape[0]
    hits = (routes[None] == jnp.arange(EXPERTS, dtype=jnp.int32)[:, None, None]).astype(jnp.float32)
    member = jnp.sum(hits, axis=-1)
    gate = jnp.sum(hits * gates[None], axis=-1)
    before = (jnp.arange(rows)[:, None] < jnp.arange(rows)[None, :]).astype(jnp.float32)
    rank = jnp.dot(member, before, preferred_element_type=jnp.float32)
    return jnp.stack([jnp.where(member > 0, rank, -1.0), gate], axis=1)


MESH = pl.DeviceIdType.MESH
QKV = (H + 2 * KVH) * HD


class Place:
    def __init__(self, sizes):
        self.yo_size, self.zo_size = sizes
        self.yo, self.xi, self.zo, self.zi, self.core = [lax.axis_index(axis) for axis in ALL]
        self.y_steps = range(1, self.yo_size)
        self.z_steps = range(1, self.zo_size)
        self.column = [(a, b) for a in range(self.zo_size) for b in range(2)]

    def at(self, y=0, x=0, z=0, w=0, core=0):
        return (
            lax.rem(self.yo + y, self.yo_size),
            1 - self.xi if x else self.xi,
            lax.rem(self.zo + z, self.zo_size),
            1 - self.zi if w else self.zi,
            1 - self.core if core else self.core,
        )

    def chip(self, y=0, x=0, z=0, w=0):
        yo, xi, zo, zi, core = self.at(y, x, z, w)
        return ((yo * 2 + xi) * self.zo_size + zo) * 2 + zi

    def back_y(self, y):
        return (self.yo_size - y) % self.yo_size

    def back_z(self, z):
        return (self.zo_size - z) % self.zo_size


class Wires:
    def __init__(self, send_sems, recv_sems):
        self.send_sems, self.recv_sems = send_sems, recv_sems
        self.started = []

    def send(self, source, target, name, device):
        copy = pltpu.make_async_remote_copy(
            src_ref=source,
            dst_ref=target,
            send_sem=self.send_sems.at[len(self.started)],
            recv_sem=self.recv_sems.at[name],
            device_id=device,
            device_id_type=MESH,
        )
        copy.start()
        self.started.append(copy)

    def arrive(self, target, name, device):
        pltpu.make_async_remote_copy(
            src_ref=target,
            dst_ref=target,
            send_sem=self.send_sems.at[0],
            recv_sem=self.recv_sems.at[name],
            device_id=device,
            device_id_type=MESH,
        ).wait_recv()

    def drain(self):
        for copy in self.started:
            copy.wait_send()


def greet(partners):
    barrier = pltpu.get_barrier_semaphore()
    for partner in partners:
        pl.semaphore_signal(barrier, inc=1, device_id=partner, device_id_type=MESH)
    pl.semaphore_wait(barrier, len(partners))


def mesh_sizes():
    return lax.axis_size("yo"), lax.axis_size("zo")


def add_rows(target, *parts):
    size = 16 if target.shape[0] % 16 == 0 else target.shape[0]

    def step(index, carry):
        rows = pl.ds(pl.multiple_of(index * size, size), size)
        total = target[rows, :].astype(jnp.float32)
        for part in parts:
            total = total + part[rows, :].astype(jnp.float32)
        target[rows, :] = total.astype(target.dtype)
        return carry

    lax.fori_loop(0, target.shape[0] // size, step, 0)


def together(*steps):
    alive = list(steps)
    while alive:
        for one in list(alive):
            try:
                next(one)
            except StopIteration:
                alive.remove(one)


def greet_layer(here):
    greet(
        [here.at(z=z, w=w) for z, w in here.column if (z, w) != (0, 0)]
        + [here.at(x=1), here.at(x=1, w=1), here.at(core=1)]
        + [here.at(y=y) for y in here.y_steps]
    )


def gather_attention_steps(here, wires, shards, wholes):
    count = len(shards)
    far = [offset for offset in here.column if offset != (0, 0)]
    mine = here.chip() * 2 + here.core
    other = here.at(core=1)

    def block(**offsets):
        return here.chip(**offsets) * 2 + here.core

    def name(kind, y, x, z, w, part):
        spot = (((kind * here.yo_size + y) * 2 + x) * here.zo_size + z) * 2 + w
        return spot * count + part

    for z, w in far:
        for part in range(count):
            wires.send(
                shards[part],
                wholes[part].at[mine],
                name(0, 0, 0, here.back_z(z), w, part),
                here.at(z=z, w=w),
            )

    def pass_on(source, y, x, z, w, part, to_x, to_y):
        target = wholes[part].at[block(y=y, x=x, z=z, w=w)]
        if to_x:
            wires.send(source, target, name(0, y, 1 - x, z, w, part), here.at(x=1))
        for step in here.y_steps if to_y else ():
            back = (y + here.back_y(step)) % here.yo_size
            wires.send(source, target, name(0, back, x, z, w, part), here.at(y=step))
        wires.send(source, target, name(1, y, x, z, w, part), other)

    for z, w in here.column:
        for part in range(count):
            if (z, w) == (0, 0):
                pass_on(shards[part], 0, 0, 0, 0, part, True, True)
                wholes[part][mine] = shards[part][...]
            else:
                source = wholes[part].at[block(z=z, w=w)]
                wires.arrive(source, name(0, 0, 0, z, w, part), other)
                pass_on(source, 0, 0, z, w, part, True, True)
        yield
    for z, w in here.column:
        for part in range(count):
            source = wholes[part].at[block(x=1, z=z, w=w)]
            wires.arrive(source, name(0, 0, 1, z, w, part), other)
            pass_on(source, 0, 1, z, w, part, False, part % 2 == 1)
            for y in here.y_steps:
                source = wholes[part].at[block(y=y, z=z, w=w)]
                wires.arrive(source, name(0, y, 0, z, w, part), other)
                pass_on(source, y, 0, z, w, part, part % 2 == 0, False)
        yield
    for z, w in here.column:
        for part in range(count):
            for y in here.y_steps:
                source = wholes[part].at[block(y=y, x=1, z=z, w=w)]
                wires.arrive(source, name(0, y, 1, z, w, part), other)
                pass_on(source, y, 1, z, w, part, False, False)
        yield
    for y in range(here.yo_size):
        for x in range(2):
            for z, w in here.column:
                for part in range(count):
                    index = here.chip(y=y, x=x, z=z, w=w) * 2 + 1 - here.core
                    wires.arrive(wholes[part].at[index], name(1, y, x, z, w, part), other)


def gather_experts_steps(here, wires, shards, wholes):
    count = len(shards)
    group = offsets_of(GROUP)
    other = here.at(core=1)

    def name(kind, y, x, z, w, part):
        spot = (((kind * here.yo_size + y) * 2 + x) * here.zo_size + z) * 2 + w
        return spot * count + part

    def member(x, w):
        yo, xi, zo, zi, core = here.at(x=x, w=w)
        return xi * 2 + zi

    for x, w in group[1:]:
        for part in range(count):
            wires.send(
                shards[part].at[member(x, w)],
                wholes[part].at[0, here.chip()],
                name(0, 0, x, 0, w, part),
                here.at(x=x, w=w),
            )

    def pass_on(source, y, x, z, w, part, to_z, to_y):
        index = here.chip(y=y, x=x, z=z, w=w)
        for step in here.z_steps if to_z else ():
            back = (z + here.back_z(step)) % here.zo_size
            wires.send(
                source, wholes[part].at[0, index], name(0, y, x, back, w, part), here.at(z=step)
            )
        for step in here.y_steps if to_y else ():
            back = (y + here.back_y(step)) % here.yo_size
            wires.send(
                source, wholes[part].at[0, index], name(0, back, x, z, w, part), here.at(y=step)
            )
        wires.send(source, wholes[part].at[1, index], name(1, y, x, z, w, part), other)

    for x, w in group:
        for part in range(count):
            if (x, w) == (0, 0):
                pass_on(shards[part].at[member(0, 0)], 0, 0, 0, 0, part, True, True)
                wholes[part][0, here.chip()] = shards[part][member(0, 0)]
            else:
                source = wholes[part].at[0, here.chip(x=x, w=w)]
                wires.arrive(source, name(0, 0, x, 0, w, part), other)
                pass_on(source, 0, x, 0, w, part, True, True)
        yield
    for x, w in group:
        for part in range(count):
            for z in here.z_steps:
                source = wholes[part].at[0, here.chip(x=x, w=w, z=z)]
                wires.arrive(source, name(0, 0, x, z, w, part), other)
                pass_on(source, 0, x, z, w, part, False, True)
        yield
    for z in range(here.zo_size):
        for x, w in group:
            for part in range(count):
                for y in here.y_steps:
                    source = wholes[part].at[0, here.chip(y=y, x=x, w=w, z=z)]
                    wires.arrive(source, name(0, y, x, z, w, part), other)
                    pass_on(source, y, x, z, w, part, False, False)
            yield
    for y in range(here.yo_size):
        for z in range(here.zo_size):
            for x, w in group:
                for part in range(count):
                    target = wholes[part].at[1, here.chip(y=y, x=x, w=w, z=z)]
                    wires.arrive(target, name(1, y, x, z, w, part), other)


ATTENTION_PARTS = 3
EXPERT_PARTS = 2


def gather_layer_kernel(sizes, *refs):
    count = ATTENTION_PARTS + EXPERT_PARTS
    ins, outs, sems = refs[:count], refs[count : 2 * count], refs[2 * count :]
    here = Place(sizes)
    wires = Wires(*sems[:2]), Wires(*sems[2:])
    cut = ATTENTION_PARTS
    greet_layer(here)
    together(
        gather_attention_steps(here, wires[0], ins[:cut], outs[:cut]),
        gather_experts_steps(here, wires[1], ins[cut:], outs[cut:]),
    )
    for one in wires:
        one.drain()


def gather_layer(attention_shards, expert_parts):
    sizes = mesh_sizes()
    chips = sizes[0] * sizes[1] * 4
    columns = sizes[1] * 2
    first = ATTENTION_PARTS * ((columns - 1) + chips + columns * (2 * sizes[0] + 1) + chips)
    second = EXPERT_PARTS * (3 + 4 * (sizes[0] + sizes[1]) + 4 * sizes[1] * sizes[0] + chips)
    in_vmem = pl.BlockSpec(memory_space=pltpu.VMEM)
    count = ATTENTION_PARTS + EXPERT_PARTS
    return pl.pallas_call(
        functools.partial(gather_layer_kernel, sizes),
        out_shape=[
            jax.ShapeDtypeStruct((2 * chips,) + shard.shape, shard.dtype)
            for shard in attention_shards
        ]
        + [
            jax.ShapeDtypeStruct((2, chips) + part.shape[1:], part.dtype) for part in expert_parts
        ],
        in_specs=[in_vmem] * count,
        out_specs=[in_vmem] * count,
        scratch_shapes=[
            pltpu.SemaphoreType.DMA((first,)),
            pltpu.SemaphoreType.DMA((2 * chips * ATTENTION_PARTS,)),
            pltpu.SemaphoreType.DMA((second,)),
            pltpu.SemaphoreType.DMA((2 * chips * EXPERT_PARTS,)),
        ],
        compiler_params=pltpu.CompilerParams(
            collective_id=0, has_side_effects=True, vmem_limit_bytes=58 * 1024 * 1024
        ),
    )(*attention_shards, *expert_parts)


def sum_experts_steps(here, wires, whole, outs, first, second, third):
    count = len(whole)
    group = offsets_of(GROUP)
    other = here.at(core=1)
    chips = here.yo_size * here.zo_size * 4

    def place(y, z, member):
        return (y * here.zo_size + z) * 4 + member

    def name(kind, index, part):
        return (kind * chips + index) * count + part

    order = [
        (y, z, member)
        for y in list(here.y_steps) + [0]
        for z in list(here.z_steps) + [0]
        for member in (1, 2, 3, 0)
    ]
    for y, z, member in order:
        x, w = group[member]
        index = here.chip(y=y, x=x, z=z, w=w)
        spot = place(y, z, member)
        for part in range(count):
            wires.send(
                whole[part].at[1, index], first[part].at[spot], name(0, spot, part), other
            )
    yield
    for y, z, member in order:
        x, w = group[member]
        index = here.chip(y=y, x=x, z=z, w=w)
        spot = place(y, z, member)
        for part in range(count):
            total = first[part].at[spot]
            wires.arrive(total, name(0, spot, part), other)
            parts = [whole[part].at[0, index]]
            if y:
                add_rows(total, *parts)
                landing = place(here.back_y(y), z, member)
                wires.send(
                    total, second[part].at[landing - 4 * here.zo_size], name(1, landing, part), here.at(y=y)
                )
                continue
            for step in here.y_steps:
                spot_in = place(step, z, member)
                arrived = second[part].at[spot_in - 4 * here.zo_size]
                wires.arrive(arrived, name(1, spot_in, part), other)
                parts.append(arrived)
            if z:
                add_rows(total, *parts)
                landing = here.back_z(z) * 4 + member
                wires.send(
                    total, third[part].at[landing - 4], name(2, landing, part), here.at(z=z)
                )
                continue
            for step in here.z_steps:
                arrived = third[part].at[step * 4 + member - 4]
                wires.arrive(arrived, name(2, step * 4 + member, part), other)
                parts.append(arrived)
            add_rows(total, *parts)
            slot = here.xi * 2 + here.zi
            if member:
                wires.send(total, outs[part].at[slot], name(3, member, part), here.at(x=x, w=w))
            else:
                outs[part][slot] = total[...]
        yield
    for member in range(1, 4):
        x, w = group[member]
        yo, xi, zo, zi, core = here.at(x=x, w=w)
        for part in range(count):
            wires.arrive(outs[part].at[xi * 2 + zi], name(3, member, part), other)


def sum_attention_steps(here, wires, whole, outs, first, second, third, fourth):
    count = len(whole)
    columns = here.column
    other = here.at(core=1)
    width = len(columns)
    chips = here.yo_size * 2 * width

    def place(y, x, column):
        return (y * 2 + x) * width + column

    def name(kind, index, part):
        return (kind * chips + index) * count + part

    rounds = [
        (y, x, (column + 1) % width, part)
        for y in list(here.y_steps) + [0]
        for x in (1, 0)
        for column in range(width)
        for part in range(count)
    ]

    def turn(item):
        y, x, column, part = item
        ahead = x if part % 2 == 0 else y
        return (not (y and x), not ahead, not (y or x))

    rounds.sort(key=turn)
    for y, x, column, part in rounds:
        z, w = columns[column]
        spot = place(y, x, column)
        wires.send(
            whole[part].at[here.chip(y=y, x=x, z=z, w=w), 1 - here.core],
            first[part].at[spot],
            name(0, spot, part),
            other,
        )
    yield
    for y, x, column, part in rounds:
        z, w = columns[column]
        spot = place(y, x, column)
        total = first[part].at[spot]
        wires.arrive(total, name(0, spot, part), other)
        parts = [whole[part].at[here.chip(y=y, x=x, z=z, w=w), here.core]]

        def take_in(buffer, kind, index, offset=0):
            arrived = buffer[part].at[index - offset]
            wires.arrive(arrived, name(kind, index, part), other)
            parts.append(arrived)

        def give(buffer, kind, index, device, offset=0):
            add_rows(total, *parts)
            wires.send(total, buffer[part].at[index - offset], name(kind, index, part), device)

        if part % 2 == 0:
            if x:
                add_rows(total, *parts)
                wires.send(
                    total,
                    second[part].at[y * width + column],
                    name(1, place(y, 0, column), part),
                    here.at(x=1),
                )
                yield
                continue
            arrived = second[part].at[y * width + column]
            wires.arrive(arrived, name(1, place(y, 0, column), part), other)
            parts.append(arrived)
            if y:
                give(third, 2, here.back_y(y) * width + column, here.at(y=y), width)
                yield
                continue
            for step in here.y_steps:
                take_in(third, 2, step * width + column, width)
        else:
            if y:
                give(second, 1, place(here.back_y(y), x, column), here.at(y=y), 2 * width)
                yield
                continue
            for step in here.y_steps:
                take_in(second, 1, place(step, x, column), 2 * width)
            if x:
                give(third, 2, column, here.at(x=1))
                yield
                continue
            take_in(third, 2, column)
        if column:
            landing = columns.index((here.back_z(z), w))
            give(fourth, 3, landing, here.at(z=z, w=w), 1)
            yield
            continue
        for step in range(1, width):
            take_in(fourth, 3, step, 1)
        add_rows(total, *parts)
        outs[part][...] = total[...]
        yield


def sum_layer_kernel(sizes, *refs):
    both = ATTENTION_PARTS + EXPERT_PARTS
    cut = ATTENTION_PARTS
    ins, outs, rest = refs[:both], refs[both : 2 * both], refs[2 * both :]
    buffers, sems = rest[:-4], rest[-4:]
    attention = [buffers[level * cut : (level + 1) * cut] for level in range(4)]
    buffers = buffers[4 * cut :]
    experts = [buffers[level * EXPERT_PARTS : (level + 1) * EXPERT_PARTS] for level in range(3)]
    here = Place(sizes)
    wires = Wires(*sems[:2]), Wires(*sems[2:])
    greet_layer(here)
    together(
        sum_experts_steps(here, wires[1], ins[cut:], outs[cut:], *experts),
        sum_attention_steps(here, wires[0], ins[:cut], outs[:cut], *attention),
    )
    for one in wires:
        one.drain()


def sum_layer(attention_grads, expert_grads):
    sizes = mesh_sizes()
    chips = sizes[0] * sizes[1] * 4
    column = sizes[1] * 2
    attention = [grads.reshape(chips, 2, -1, grads.shape[1]) for grads in attention_grads]
    experts = [grads.reshape(2, chips, -1, D) for grads in expert_grads]
    in_vmem = pl.BlockSpec(memory_space=pltpu.VMEM)
    count = ATTENTION_PARTS + EXPERT_PARTS

    def held(blocks, sizes_of):
        return [
            pltpu.VMEM((sizes_of(part),) + block.shape[2:], jnp.bfloat16)
            for part, block in enumerate(blocks)
        ]

    level_two = (sizes[0] * column, (sizes[0] - 1) * 2 * column)
    level_three = ((sizes[0] - 1) * column, column)
    return pl.pallas_call(
        functools.partial(sum_layer_kernel, sizes),
        out_shape=[jax.ShapeDtypeStruct(block.shape[2:], jnp.bfloat16) for block in attention]
        + [jax.ShapeDtypeStruct((4,) + block.shape[2:], jnp.bfloat16) for block in experts],
        in_specs=[in_vmem] * count,
        out_specs=[in_vmem] * count,
        scratch_shapes=held(attention, lambda part: chips)
        + held(attention, lambda part: level_two[part % 2])
        + held(attention, lambda part: level_three[part % 2])
        + held(attention, lambda part: column - 1)
        + held(experts, lambda part: chips)
        + held(experts, lambda part: (sizes[0] - 1) * sizes[1] * 4)
        + held(experts, lambda part: (sizes[1] - 1) * 4)
        + [
            pltpu.SemaphoreType.DMA((3 * chips * ATTENTION_PARTS,)),
            pltpu.SemaphoreType.DMA((4 * chips * ATTENTION_PARTS,)),
            pltpu.SemaphoreType.DMA((3 * chips * EXPERT_PARTS,)),
            pltpu.SemaphoreType.DMA((4 * chips * EXPERT_PARTS,)),
        ],
        compiler_params=pltpu.CompilerParams(
            collective_id=1, has_side_effects=True, vmem_limit_bytes=62 * 1024 * 1024
        ),
    )(*attention, *experts)


def swap(value, axis):
    return lax.ppermute(value, axis, [(0, 1), (1, 0)])


def pick(value, index, axis=0):
    return lax.dynamic_index_in_dim(value, index, axis, keepdims=False)


def by_core(mine, theirs, axis):
    core = lax.axis_index("core")
    return jnp.where(
        core == 0, jnp.stack([mine, theirs], axis), jnp.stack([theirs, mine], axis)
    )


def gain_columns(gains):
    gains = gains.astype(jnp.bfloat16).T
    return jnp.pad(gains, ((0, 0), (0, 128 - gains.shape[1])))


def layer_weights(w_qkv, w_out, w_gateup, w_down, gains, layer):
    core = lax.axis_index("core")
    parts = []
    for shard in (w_gateup[layer], w_down[layer]):
        shard = shard.astype(jnp.bfloat16)
        shard = shard.reshape((4, 2) + shard.shape[1:])
        theirs = swap(pick(shard, 1 - core, 1), "core")
        parts.append(by_core(pick(shard, core, 1), theirs, 1).reshape(4, -1, D))
    shards = [
        w_qkv[layer].astype(jnp.bfloat16),
        w_out[layer].astype(jnp.bfloat16),
        gain_columns(gains[layer]),
    ]
    qkv, out, gain, up, down = gather_layer(shards, parts)
    gain = gain.reshape(D, 128)[:, :2].T.astype(jnp.float32)
    attention = (qkv.reshape(D, QKV), out.reshape(D, D), gain)
    return attention, (up.reshape(2, D, 2 * F), down.reshape(2, F, D))


def layer_sums(grad_qkv, grad_out, grad_up, grad_down, grad_gains):
    core = lax.axis_index("core")
    attention = [
        grad_qkv.astype(jnp.bfloat16),
        grad_out.astype(jnp.bfloat16),
        gain_columns(grad_gains),
    ]
    qkv, out, gain, up, down = sum_layer(attention, [grad_up, grad_down])
    result = [qkv.astype(jnp.float32), out.astype(jnp.float32)]
    for part in (up, down):
        part = part.reshape(4, 2, -1, D)
        theirs = swap(pick(part, 1 - core, 1), "core")
        pair = by_core(pick(part, core, 1), theirs, 1)
        result.append(pair.reshape(EXPERTS, -1, D).astype(jnp.float32))
    return result + [gain[:, :2].T.astype(jnp.float32)]


SQRT_HALF = 0.7071067811865476
PDF_SCALE = 0.3989422804014327
TILE = 256
TILES = F // TILE


def selections(table, columns):
    rows = table.shape[1]
    slots = lax.broadcasted_iota(jnp.int32, (CAP, rows), 0).astype(jnp.float32)
    take = (table[0:1, :] == slots).astype(jnp.bfloat16)
    slots = lax.broadcasted_iota(jnp.int32, (rows, CAP), 1).astype(jnp.float32)
    spread = (columns[:, 0:1] == slots).astype(jnp.bfloat16)
    return take, spread, columns[:, 1:2]


def dot(left, right, contract=(1, 0)):
    return lax.dot_general(
        left,
        right,
        (((contract[0],), (contract[1],)), ((), ())),
        preferred_element_type=jnp.float32,
    )


def experts_grads_kernel(slot_in, active, slot_grad, grad_gate, grad_up, up_out, down_out):
    up_out[0, :, :F] = dot(slot_in[0], grad_gate[0], (0, 0)).astype(jnp.bfloat16)
    up_out[0, :, F:] = dot(slot_in[0], grad_up[0], (0, 0)).astype(jnp.bfloat16)
    down_out[0] = dot(active[0], slot_grad[0], (0, 0)).astype(jnp.bfloat16)


def whole_block(shape):
    return pl.BlockSpec(shape, lambda e, f: (0,) * len(shape))


def expert_block(shape):
    return pl.BlockSpec((1,) + shape, lambda e, f: (e,) + (0,) * len(shape))


def moe_forward_kernel(
    sizes,
    tokens,
    tables,
    columns,
    up_w,
    down_w,
    merged,
    slot_out,
    gate_out,
    up_out,
    active_out,
    chunks,
    leaving,
    coming,
    slot_in,
    result,
    total,
    send_sems,
    recv_sems,
):
    here = Place(sizes)
    wires = Wires(send_sems, recv_sems)
    partners = [here.at(x=x, w=w) for x, w in offsets_of(GROUP)]
    greet(partners[1:])
    for place in range(1, 4):
        wires.send(tokens, chunks.at[place - 1], place - 1, partners[place])
    for place in range(4):
        chunk = tokens if place == 0 else chunks.at[place - 1]
        if place:
            wires.arrive(chunk, place - 1, partners[place])
        rows = pl.ds(place * CAP, CAP)

        def step(index, carry, place=place, chunk=chunk, rows=rows):
            expert, tile = lax.div(index, TILES), lax.rem(index, TILES)
            at_gate = pl.ds(pl.multiple_of(tile * TILE, TILE), TILE)
            at_up = pl.ds(pl.multiple_of(F + tile * TILE, TILE), TILE)
            take, spread, gates = selections(tables[place, expert], columns[place, expert])

            @pl.when(tile == 0)
            def _():
                slot_in[...] = dot(take, chunk[...]).astype(jnp.bfloat16)
                slot_out[expert, rows, :] = slot_in[...]

            gate = dot(slot_in[...], up_w[expert, :, at_gate])
            up = dot(slot_in[...], up_w[expert, :, at_up])
            active = (0.5 * gate * (1.0 + lax.erf(gate * SQRT_HALF)) * up).astype(jnp.bfloat16)
            gate_out[expert, rows, at_gate] = gate
            up_out[expert, rows, at_gate] = up
            active_out[expert, rows, at_gate] = active
            part = dot(active, down_w[expert, at_gate, :])

            @pl.when(tile == 0)
            def _():
                result[...] = part

            @pl.when(tile > 0)
            def _():
                result[...] += part

            @pl.when(tile == TILES - 1)
            def _():
                share = dot(spread, result[...].astype(jnp.bfloat16)) * gates

                @pl.when(expert == 0)
                def _():
                    total[...] = share

                @pl.when(expert > 0)
                def _():
                    total[...] += share

            return carry

        lax.fori_loop(0, 2 * TILES, step, 0)
        if place == 0:
            merged[...] = total[...]
        else:
            leaving[place - 1] = total[...].astype(jnp.bfloat16)
            wires.send(leaving.at[place - 1], coming.at[place - 1], place + 2, partners[place])
    for place in range(1, 4):
        wires.arrive(coming.at[place - 1], place + 2, partners[place])
        merged[...] += coming[place - 1].astype(jnp.float32)
    wires.drain()


def moe_backward_kernel(
    sizes,
    gradient,
    tables,
    columns,
    up_w,
    down_w,
    gate_in,
    up_in,
    merged,
    slot_out,
    gate_out,
    up_out,
    chunks,
    leaving,
    coming,
    slot_grad,
    slots,
    total,
    send_sems,
    recv_sems,
):
    here = Place(sizes)
    wires = Wires(send_sems, recv_sems)
    partners = [here.at(x=x, w=w) for x, w in offsets_of(GROUP)]
    greet(partners[1:])
    leaving[3] = gradient[...].astype(jnp.bfloat16)
    for place in range(1, 4):
        wires.send(leaving.at[3], chunks.at[place - 1], place - 1, partners[place])
    for place in range(4):
        chunk = gradient if place == 0 else chunks.at[place - 1]
        if place:
            wires.arrive(chunk, place - 1, partners[place])
        rows = pl.ds(place * CAP, CAP)

        def step(index, carry, place=place, chunk=chunk, rows=rows):
            expert, tile = lax.div(index, TILES), lax.rem(index, TILES)
            at_gate = pl.ds(pl.multiple_of(tile * TILE, TILE), TILE)
            at_up = pl.ds(pl.multiple_of(F + tile * TILE, TILE), TILE)
            take, spread, gates = selections(tables[place, expert], columns[place, expert])

            @pl.when(tile == 0)
            def _():
                weighted = (gates * chunk[...].astype(jnp.float32)).astype(jnp.bfloat16)
                slot_grad[...] = dot(take, weighted).astype(jnp.bfloat16)
                slot_out[expert, rows, :] = slot_grad[...]

            grad_act = dot(slot_grad[...], down_w[expert, at_gate, :], (1, 1))
            gate, up = gate_in[expert, rows, at_gate], up_in[expert, rows, at_gate]
            below = 0.5 * (1.0 + lax.erf(gate * SQRT_HALF))
            slope = below + gate * PDF_SCALE * jnp.exp(-0.5 * gate * gate)
            grad_gate = (grad_act * up * slope).astype(jnp.bfloat16)
            grad_up = (grad_act * gate * below).astype(jnp.bfloat16)
            gate_out[expert, rows, at_gate] = grad_gate
            up_out[expert, rows, at_gate] = grad_up
            part = dot(grad_gate, up_w[expert, :, at_gate], (1, 1))
            part = part + dot(grad_up, up_w[expert, :, at_up], (1, 1))

            @pl.when(tile == 0)
            def _():
                slots[...] = part

            @pl.when(tile > 0)
            def _():
                slots[...] += part

            @pl.when(tile == TILES - 1)
            def _():
                share = dot(spread, slots[...].astype(jnp.bfloat16))

                @pl.when(expert == 0)
                def _():
                    total[...] = share

                @pl.when(expert > 0)
                def _():
                    total[...] += share

            return carry

        lax.fori_loop(0, 2 * TILES, step, 0)
        if place == 0:
            merged[...] = total[...]
        else:
            leaving[place - 1] = total[...].astype(jnp.bfloat16)
            wires.send(leaving.at[place - 1], coming.at[place - 1], place + 2, partners[place])
    for place in range(1, 4):
        wires.arrive(coming.at[place - 1], place + 2, partners[place])
        merged[...] += coming[place - 1].astype(jnp.float32)
    wires.drain()


def moe_call(kernel, identity, rows_in, tables, weights, extra, kinds):
    rows = rows_in.shape[0]
    slots = 4 * CAP
    operands = [rows_in, tables, jnp.swapaxes(tables, 2, 3), *weights, *extra]
    in_vmem = pl.BlockSpec(memory_space=pltpu.VMEM)
    return pl.pallas_call(
        functools.partial(kernel, mesh_sizes()),
        in_specs=[in_vmem] * len(operands),
        out_specs=[in_vmem] * (1 + len(kinds)),
        out_shape=[jax.ShapeDtypeStruct((rows, D), jnp.float32)]
        + [jax.ShapeDtypeStruct((2, slots, width), kind) for width, kind in kinds],
        scratch_shapes=[
            pltpu.VMEM((3, rows, D), jnp.bfloat16),
            pltpu.VMEM((4, rows, D), jnp.bfloat16),
            pltpu.VMEM((3, rows, D), jnp.bfloat16),
            pltpu.VMEM((CAP, D), jnp.bfloat16),
            pltpu.VMEM((CAP, D), jnp.float32),
            pltpu.VMEM((rows, D), jnp.float32),
            pltpu.SemaphoreType.DMA((6,)),
            pltpu.SemaphoreType.DMA((6,)),
        ],
        compiler_params=pltpu.CompilerParams(
            collective_id=identity, has_side_effects=True, vmem_limit_bytes=58 * 1024 * 1024
        ),
        cost_estimate=pl.CostEstimate(
            flops=48 * CAP * D * F, bytes_accessed=40_000_000, transcendentals=8 * CAP * F
        ),
    )(*operands)


FORWARD_KEPT = ((D, jnp.bfloat16), (F, jnp.float32), (F, jnp.float32), (F, jnp.bfloat16))
BACKWARD_KEPT = ((D, jnp.bfloat16), (F, jnp.bfloat16), (F, jnp.bfloat16))


def moe_forward(expert_in, tables, weights):
    merged, *kept = moe_call(
        moe_forward_kernel, 2, expert_in, tables, weights, [], FORWARD_KEPT
    )
    return merged, kept


def moe_backward(gradient, tables, weights, kept):
    slot_in, gate, up, active = kept
    total, slot_grad, grad_gate, grad_up = moe_call(
        moe_backward_kernel, 3, gradient, tables, weights, [gate, up], BACKWARD_KEPT
    )
    slots = slot_in.shape[1]

    def columns_of(width):
        return pl.BlockSpec((1, slots, width), lambda e, i: (e, 0, i))

    grads = pl.pallas_call(
        experts_grads_kernel,
        grid=(2, 3),
        in_specs=[
            columns_of(D // 3),
            columns_of(F // 3),
            expert_block((slots, D)),
            expert_block((slots, F)),
            expert_block((slots, F)),
        ],
        out_specs=[
            pl.BlockSpec((1, D // 3, 2 * F), lambda e, i: (e, i, 0)),
            pl.BlockSpec((1, F // 3, D), lambda e, i: (e, i, 0)),
        ],
        out_shape=[
            jax.ShapeDtypeStruct((2, D, 2 * F), jnp.bfloat16),
            jax.ShapeDtypeStruct((2, F, D), jnp.bfloat16),
        ],
        compiler_params=pltpu.CompilerParams(vmem_limit_bytes=48 * 1024 * 1024),
        cost_estimate=pl.CostEstimate(
            flops=12 * slots * D * F, bytes_accessed=30_000_000, transcendentals=0
        ),
    )(slot_in, active, slot_grad, grad_gate, grad_up)
    return total, grads[0], grads[1]


def layer_forward(stream, attn_w, expert_w, tables, allowed, cosine_table, sine_table):
    qkv_w, out_w, gain_full = attn_w
    row_count = stream.shape[0]
    normed, scale_one = normalize(stream, gain_full[0])
    attn_in = normed.astype(jnp.bfloat16)
    projected = jnp.dot(attn_in, qkv_w, preferred_element_type=jnp.float32)
    queries = rotate(
        projected[:, : H * HD].reshape(row_count, H, HD), cosine_table, sine_table
    ).astype(jnp.bfloat16)
    keys_local = rotate(
        projected[:, H * HD : (H + KVH) * HD].reshape(row_count, KVH, HD), cosine_table, sine_table
    ).astype(jnp.bfloat16)
    values_local = projected[:, (H + KVH) * HD :].reshape(row_count, KVH, HD).astype(jnp.bfloat16)
    both = jnp.concatenate([keys_local, values_local], axis=1)
    both_all = jnp.concatenate([send(both, CTX, offsets) for offsets in offsets_of(CTX)], axis=0)
    keys_all, values_all = both_all[:, :KVH], both_all[:, KVH:]
    attended, totals = attention_forward(queries, keys_all, values_all, allowed)
    attended_low = attended.reshape(row_count, H * HD).astype(jnp.bfloat16)
    middle_stream = stream + jnp.dot(attended_low, out_w, preferred_element_type=jnp.float32)
    normed_two, scale_two = normalize(middle_stream, gain_full[1])
    expert_in = normed_two.astype(jnp.bfloat16)
    merged, kept = moe_forward(expert_in, tables, expert_w)
    record = {
        "stream": stream,
        "scale_one": scale_one,
        "attn_in": attn_in,
        "queries": queries,
        "keys_all": keys_all,
        "values_all": values_all,
        "totals": totals,
        "attended": attended_low,
        "middle": middle_stream,
        "scale_two": scale_two,
        "kept": kept,
    }
    return (record, middle_stream + merged)


def layer_backward(gradient, record, attn_w, expert_w, tables, allowed, cosine_table, sine_table):
    qkv_w, out_w, gain_full = attn_w
    row_count = gradient.shape[0]
    grad_normed, grad_up, grad_down = moe_backward(gradient, tables, expert_w, record["kept"])
    grad_normed, grad_up, grad_down = lax.optimization_barrier((grad_normed, grad_up, grad_down))
    grad_in_two, grad_gain_two = normalize_back(
        grad_normed, record["middle"], record["scale_two"], gain_full[1]
    )
    grad_middle = gradient + grad_in_two
    grad_middle_low = grad_middle.astype(jnp.bfloat16)
    grad_out = jnp.dot(record["attended"].T, grad_middle_low, preferred_element_type=jnp.float32)
    grad_attended = jnp.dot(grad_middle_low, out_w.T, preferred_element_type=jnp.float32)
    grad_attended = grad_attended.astype(jnp.bfloat16).reshape(row_count, H, HD)
    grad_queries, grad_keys_all, grad_values_all = attention_backward(
        record["queries"],
        record["keys_all"],
        record["values_all"],
        allowed,
        record["totals"],
        grad_attended,
    )
    both_all = jnp.concatenate([grad_keys_all, grad_values_all], axis=1)
    both = None
    for place, offsets in enumerate(offsets_of(CTX)):
        part = both_all[place * row_count : (place + 1) * row_count]
        if offsets != (0, 0):
            part = send(part.astype(jnp.bfloat16), CTX, offsets, back=True).astype(jnp.float32)
        both = part if both is None else both + part
    grad_keys, grad_values = both[:, :KVH], both[:, KVH:]
    grad_projected = jnp.concatenate(
        [
            rotate_back(grad_queries, cosine_table, sine_table).reshape(row_count, H * HD),
            rotate_back(grad_keys, cosine_table, sine_table).reshape(row_count, KVH * HD),
            grad_values.reshape(row_count, KVH * HD),
        ],
        axis=1,
    ).astype(jnp.bfloat16)
    grad_qkv = jnp.dot(record["attn_in"].T, grad_projected, preferred_element_type=jnp.float32)
    grad_normed_one = jnp.dot(grad_projected, qkv_w.T, preferred_element_type=jnp.float32)
    grad_in_one, grad_gain_one = normalize_back(
        grad_normed_one, record["stream"], record["scale_one"], gain_full[0]
    )
    grad_gains = jnp.stack([grad_gain_one, grad_gain_two])
    return (grad_middle + grad_in_one, (grad_qkv, grad_out, grad_up, grad_down, grad_gains))


def on_device(
    tokens,
    cotangent,
    routes,
    gate_weights,
    lengths,
    block_map,
    w_qkv,
    w_out,
    w_gateup,
    w_down,
    gains,
    m_qkv,
    v_qkv,
    m_out,
    v_out,
    m_gateup,
    v_gateup,
    m_down,
    v_down,
    m_gains,
    v_gains,
):
    row_count = tokens.shape[1]
    block_rows = row_count // 2
    own_pos, own_doc = positions_docs(block_map, lengths[0], flat_index(CTX), block_rows)
    places = [
        positions_docs(block_map, lengths[0], source_index(CTX, offsets), block_rows)
        for offsets in offsets_of(CTX)
    ]
    key_pos = jnp.concatenate([place[0] for place in places])
    key_doc = jnp.concatenate([place[1] for place in places])
    allowed = (own_doc[:, None] == key_doc[None, :]) & (key_pos[None, :] <= own_pos[:, None])
    cosine_table, sine_table = rope_tables(own_pos)
    own_tables = jnp.stack(
        [dispatch_tables(routes[layer, 0], gate_weights[layer, 0]) for layer in range(LAYERS)]
    )
    core = lax.axis_index("core")
    group_tables = []
    for offsets in offsets_of(GROUP):
        theirs = lax.dynamic_slice_in_dim(own_tables, 2 * target_index(GROUP, offsets), 2, axis=1)
        theirs = jnp.where(core == 0, theirs, theirs[:, ::-1])
        group_tables.append(send(theirs, GROUP, offsets))
    group_tables = jnp.stack(group_tables, axis=1)
    stream = tokens[0].astype(jnp.float32)
    records = []
    attn_w, expert_w = zip(
        *[
            layer_weights(w_qkv, w_out, w_gateup, w_down, gains, layer)
            for layer in range(LAYERS)
        ]
    )
    for layer_index in range(LAYERS):
        record, stream = layer_forward(
            stream,
            attn_w[layer_index],
            expert_w[layer_index],
            group_tables[layer_index],
            allowed,
            cosine_table,
            sine_table,
        )
        records.append(record)
    output = stream.astype(jnp.bfloat16)[None]
    gradient = cotangent[0].astype(jnp.float32)
    rates = (D ** (-0.5), 0.5, D ** (-0.5), (F // 8) ** (-0.5), 1.0)
    decays = (DECAY, DECAY, DECAY, DECAY, 0.0)
    params = (w_qkv, w_out, w_gateup, w_down, gains)
    firsts = (m_qkv, m_out, m_gateup, m_down, m_gains)
    seconds = (v_qkv, v_out, v_gateup, v_down, v_gains)
    updated = [[None] * LAYERS for which in range(15)]
    for layer_index in reversed(range(LAYERS)):
        gradient, layer_grads = layer_backward(
            gradient,
            records[layer_index],
            attn_w[layer_index],
            expert_w[layer_index],
            group_tables[layer_index],
            allowed,
            cosine_table,
            sine_table,
        )
        sums = layer_sums(*layer_grads)
        for which in range(5):
            fresh = adamw(
                params[which][layer_index],
                firsts[which][layer_index],
                seconds[which][layer_index],
                sums[which],
                rates[which],
                decays[which],
            )
            updated[3 * which][layer_index] = fresh[0]
            updated[3 * which + 1][layer_index] = fresh[1]
            updated[3 * which + 2][layer_index] = fresh[2]
    stacked = [jnp.stack(pieces) for pieces in updated]
    return (output, gradient[None], *stacked)


def solution(mesh):
    ctx_size, shard_size = mesh.shape["ctx"], mesh.shape["shard"]
    fine = Mesh(mesh.devices.reshape(ctx_size // 2, 2, shard_size // 4, 2, 2), ALL)
    tokens = P(SHARD, CTX, None)
    routed = P(None, SHARD, CTX, None)
    rows_two = P(None, ALL, None)
    rows_three = P(None, None, ALL, None)
    gain = P(None, None, ALL)
    weights = (rows_two, rows_two, rows_three, rows_three, gain)
    states = tuple(spec for spec in weights for which in range(2))
    return jax.shard_map(
        on_device,
        mesh=fine,
        in_specs=(tokens, tokens, routed, routed, P(SHARD, None), P()) + weights + states,
        out_specs=(tokens, tokens) + tuple(spec for spec in weights for which in range(3)),
        check_vma=False,
    )
```

```python
import functools

import jax
import jax.numpy as jnp
from jax import lax
from jax.experimental import pallas as pl
from jax.experimental.pallas import tpu as pltpu
from jax.sharding import Mesh
from jax.sharding import PartitionSpec as P

D = 1536
H = 12
KVH = 2
HD = 128
F = 768
TOP = 4
EXPERTS = 8
LAYERS = 2
STEP = 10
CAP = 160


NORM_EPS = 1e-06
ROPE_BASE = 1000000.0
BETA_ONE = 0.9
BETA_TWO = 0.95
ADAM_EPS = 1e-08
DECAY = 0.1
MASKED = -1e30


def rope_tables(positions):
    half_width = HD // 2
    frequency = ROPE_BASE ** (-(jnp.arange(half_width, dtype=jnp.float32) * 2.0 / HD))
    angles = positions.astype(jnp.float32)[:, None] * frequency[None, :]
    return (jnp.cos(angles)[:, None, :], jnp.sin(angles)[:, None, :])


def rotate(vectors, cosine_table, sine_table):
    half_width = vectors.shape[-1] // 2
    first_half = vectors[..., :half_width]
    second_half = vectors[..., half_width:]
    return jnp.concatenate(
        [
            first_half * cosine_table - second_half * sine_table,
            second_half * cosine_table + first_half * sine_table,
        ],
        axis=-1,
    )


def rotate_back(gradient, cosine_table, sine_table):
    half_width = gradient.shape[-1] // 2
    first_half = gradient[..., :half_width]
    second_half = gradient[..., half_width:]
    return jnp.concatenate(
        [
            first_half * cosine_table + second_half * sine_table,
            second_half * cosine_table - first_half * sine_table,
        ],
        axis=-1,
    )


def normalize(values, gain_row):
    row_scale = lax.rsqrt(jnp.mean(values * values, axis=-1, keepdims=True) + NORM_EPS)
    return (values * row_scale * gain_row, row_scale)


def normalize_back(gradient, values, row_scale, gain_row):
    unit_rows = values * row_scale
    inner_grad = gradient * gain_row
    input_grad = row_scale * (
        inner_grad - unit_rows * jnp.mean(inner_grad * unit_rows, axis=-1, keepdims=True)
    )
    return (input_grad, jnp.sum(gradient * unit_rows, axis=0))


def adamw(parameter, moment, second, gradient, step_rate, decay_rate):
    moment = BETA_ONE * moment + (1.0 - BETA_ONE) * gradient
    second = BETA_TWO * second + (1.0 - BETA_TWO) * gradient * gradient
    direction = (
        moment / (1.0 - BETA_ONE**STEP) / (jnp.sqrt(second / (1.0 - BETA_TWO**STEP)) + ADAM_EPS)
    )
    return (parameter - step_rate * (direction + decay_rate * parameter), moment, second)


def attention_forward(queries, keys_all, values_all, allowed):
    group_size = H // KVH
    score_scale = HD ** (-0.5)
    outputs = []
    totals = []
    for head_group in range(KVH):
        query_part = queries[:, head_group * group_size : (head_group + 1) * group_size, :]
        scores = (
            jnp.einsum(
                "tjd,kd->jtk",
                query_part,
                keys_all[:, head_group, :],
                preferred_element_type=jnp.float32,
            )
            * score_scale
        )
        scores = jnp.where(allowed[None], scores, MASKED)
        row_max = jnp.max(scores, axis=-1, keepdims=True)
        exponent = jnp.exp(scores - row_max)
        row_total = jnp.sum(exponent, axis=-1, keepdims=True)
        probabilities = (exponent / row_total).astype(jnp.bfloat16)
        outputs.append(
            jnp.einsum(
                "jtk,kd->tjd",
                probabilities,
                values_all[:, head_group, :],
                preferred_element_type=jnp.float32,
            )
        )
        totals.append(row_max + jnp.log(row_total))
    return (jnp.concatenate(outputs, axis=1), totals)


def attention_backward(queries, keys_all, values_all, allowed, totals, grad_attended):
    group_size = H // KVH
    score_scale = HD ** (-0.5)
    grad_queries = []
    grad_keys = []
    grad_values = []
    for head_group in range(KVH):
        query_part = queries[:, head_group * group_size : (head_group + 1) * group_size, :]
        grad_part = grad_attended[:, head_group * group_size : (head_group + 1) * group_size, :]
        keys_part = keys_all[:, head_group, :]
        scores = (
            jnp.einsum("tjd,kd->jtk", query_part, keys_part, preferred_element_type=jnp.float32)
            * score_scale
        )
        probabilities = jnp.where(allowed[None], jnp.exp(scores - totals[head_group]), 0.0)
        grad_probs = jnp.einsum(
            "tjd,kd->jtk",
            grad_part,
            values_all[:, head_group, :],
            preferred_element_type=jnp.float32,
        )
        grad_scores = probabilities * (
            grad_probs - jnp.sum(probabilities * grad_probs, axis=-1, keepdims=True)
        )
        grad_scores = grad_scores.astype(jnp.bfloat16)
        grad_queries.append(
            jnp.einsum("jtk,kd->tjd", grad_scores, keys_part, preferred_element_type=jnp.float32)
            * score_scale
        )
        grad_keys.append(
            jnp.einsum("jtk,tjd->kd", grad_scores, query_part, preferred_element_type=jnp.float32)
            * score_scale
        )
        grad_values.append(
            jnp.einsum(
                "jtk,tjd->kd",
                probabilities.astype(jnp.bfloat16),
                grad_part,
                preferred_element_type=jnp.float32,
            )
        )
    return (
        jnp.concatenate(grad_queries, axis=1),
        jnp.stack(grad_keys, axis=1),
        jnp.stack(grad_values, axis=1),
    )


CTX = ("yo", "xi")
SHARD = ("zo", "zi", "core")
ALL = CTX + SHARD
GROUP = ("xi", "zi")
REPLICAS = ("yo", "zo", "core")


def flat_index(axes):
    index = 0
    for axis in axes:
        index = index * lax.axis_size(axis) + lax.axis_index(axis)
    return index


def shift_permutation(axes, offsets, back=False):
    sizes = [lax.axis_size(axis) for axis in axes]
    pairs = []
    for first in range(sizes[0]):
        for second in range(sizes[1]):
            target = ((first + offsets[0]) % sizes[0], (second + offsets[1]) % sizes[1])
            here = first * sizes[1] + second
            there = target[0] * sizes[1] + target[1]
            pairs.append((there, here) if back else (here, there))
    return pairs


def offsets_of(axes):
    sizes = [lax.axis_size(axis) for axis in axes]
    return [(a, b) for a in range(sizes[0]) for b in range(sizes[1])]


def send(value, axes, offsets, back=False):
    if offsets == (0, 0):
        return value
    return lax.ppermute(value, axes, shift_permutation(axes, offsets, back))


def source_index(axes, offsets):
    sizes = [lax.axis_size(axis) for axis in axes]
    return lax.rem(lax.axis_index(axes[0]) - offsets[0] + sizes[0], sizes[0]) * sizes[1] + lax.rem(
        lax.axis_index(axes[1]) - offsets[1] + sizes[1], sizes[1]
    )


def target_index(axes, offsets):
    sizes = [lax.axis_size(axis) for axis in axes]
    return lax.rem(lax.axis_index(axes[0]) + offsets[0], sizes[0]) * sizes[1] + lax.rem(
        lax.axis_index(axes[1]) + offsets[1], sizes[1]
    )


def positions_docs(block_map, lengths_row, ctx_index, block_rows):
    blocks = lax.dynamic_slice_in_dim(block_map, 2 * ctx_index, 2)
    offsets = jnp.arange(block_rows, dtype=jnp.int32)
    positions = (blocks[:, None] * block_rows + offsets[None, :]).reshape(-1)
    bounds = jnp.cumsum(lengths_row)
    documents = jnp.sum((positions[:, None] >= bounds[None, :]).astype(jnp.int32), axis=1)
    return (positions, documents)


def dispatch_tables(routes, gates):
    rows = routes.shape[0]
    hits = (routes[None] == jnp.arange(EXPERTS, dtype=jnp.int32)[:, None, None]).astype(jnp.float32)
    member = jnp.sum(hits, axis=-1)
    gate = jnp.sum(hits * gates[None], axis=-1)
    before = (jnp.arange(rows)[:, None] < jnp.arange(rows)[None, :]).astype(jnp.float32)
    rank = jnp.dot(member, before, preferred_element_type=jnp.float32)
    return jnp.stack([jnp.where(member > 0, rank, -1.0), gate], axis=1)


MESH = pl.DeviceIdType.MESH
QKV = (H + 2 * KVH) * HD


class Place:
    def __init__(self, sizes):
        self.yo_size, self.zo_size = sizes
        self.yo, self.xi, self.zo, self.zi, self.core = [lax.axis_index(axis) for axis in ALL]
        self.y_steps = range(1, self.yo_size)
        self.z_steps = range(1, self.zo_size)
        self.column = [(a, b) for a in range(self.zo_size) for b in range(2)]

    def at(self, y=0, x=0, z=0, w=0, core=0):
        return (
            lax.rem(self.yo + y, self.yo_size),
            1 - self.xi if x else self.xi,
            lax.rem(self.zo + z, self.zo_size),
            1 - self.zi if w else self.zi,
            1 - self.core if core else self.core,
        )

    def chip(self, y=0, x=0, z=0, w=0):
        yo, xi, zo, zi, core = self.at(y, x, z, w)
        return ((yo * 2 + xi) * self.zo_size + zo) * 2 + zi

    def back_y(self, y):
        return (self.yo_size - y) % self.yo_size

    def back_z(self, z):
        return (self.zo_size - z) % self.zo_size


class Wires:
    def __init__(self, send_sems, recv_sems):
        self.send_sems, self.recv_sems = send_sems, recv_sems
        self.started = []

    def send(self, source, target, name, device):
        copy = pltpu.make_async_remote_copy(
            src_ref=source,
            dst_ref=target,
            send_sem=self.send_sems.at[len(self.started)],
            recv_sem=self.recv_sems.at[name],
            device_id=device,
            device_id_type=MESH,
        )
        copy.start()
        self.started.append(copy)

    def arrive(self, target, name, device):
        pltpu.make_async_remote_copy(
            src_ref=target,
            dst_ref=target,
            send_sem=self.send_sems.at[0],
            recv_sem=self.recv_sems.at[name],
            device_id=device,
            device_id_type=MESH,
        ).wait_recv()

    def drain(self):
        for copy in self.started:
            copy.wait_send()


def greet(partners):
    barrier = pltpu.get_barrier_semaphore()
    for partner in partners:
        pl.semaphore_signal(barrier, inc=1, device_id=partner, device_id_type=MESH)
    pl.semaphore_wait(barrier, len(partners))


def mesh_sizes():
    return lax.axis_size("yo"), lax.axis_size("zo")


def add_rows(target, *parts):
    size = 16 if target.shape[0] % 16 == 0 else target.shape[0]

    def step(index, carry):
        rows = pl.ds(pl.multiple_of(index * size, size), size)
        total = target[rows, :].astype(jnp.float32)
        for part in parts:
            total = total + part[rows, :].astype(jnp.float32)
        target[rows, :] = total.astype(target.dtype)
        return carry

    lax.fori_loop(0, target.shape[0] // size, step, 0)


def together(*steps):
    alive = list(steps)
    while alive:
        for one in list(alive):
            try:
                next(one)
            except StopIteration:
                alive.remove(one)


def greet_layer(here):
    greet(
        [here.at(z=z, w=w) for z, w in here.column if (z, w) != (0, 0)]
        + [here.at(x=1), here.at(x=1, w=1), here.at(core=1)]
        + [here.at(y=y) for y in here.y_steps]
    )


def gather_attention_steps(here, wires, shards, wholes):
    count = len(shards)
    far = [offset for offset in here.column if offset != (0, 0)]
    mine = here.chip() * 2 + here.core
    other = here.at(core=1)

    def block(**offsets):
        return here.chip(**offsets) * 2 + here.core

    def name(kind, y, x, z, w, part):
        spot = (((kind * here.yo_size + y) * 2 + x) * here.zo_size + z) * 2 + w
        return spot * count + part

    for z, w in far:
        for part in range(count):
            wires.send(
                shards[part],
                wholes[part].at[mine],
                name(0, 0, 0, here.back_z(z), w, part),
                here.at(z=z, w=w),
            )

    def pass_on(source, y, x, z, w, part, to_x, to_y):
        target = wholes[part].at[block(y=y, x=x, z=z, w=w)]
        if to_x:
            wires.send(source, target, name(0, y, 1 - x, z, w, part), here.at(x=1))
        for step in here.y_steps if to_y else ():
            back = (y + here.back_y(step)) % here.yo_size
            wires.send(source, target, name(0, back, x, z, w, part), here.at(y=step))
        wires.send(source, target, name(1, y, x, z, w, part), other)

    for z, w in here.column:
        for part in range(count):
            if (z, w) == (0, 0):
                pass_on(shards[part], 0, 0, 0, 0, part, True, True)
                wholes[part][mine] = shards[part][...]
            else:
                source = wholes[part].at[block(z=z, w=w)]
                wires.arrive(source, name(0, 0, 0, z, w, part), other)
                pass_on(source, 0, 0, z, w, part, True, True)
        yield
    for z, w in here.column:
        for part in range(count):
            for y in here.y_steps:
                source = wholes[part].at[block(y=y, z=z, w=w)]
                wires.arrive(source, name(0, y, 0, z, w, part), other)
                pass_on(source, y, 0, z, w, part, True, False)
        yield
    for z, w in here.column:
        for part in range(count):
            source = wholes[part].at[block(x=1, z=z, w=w)]
            wires.arrive(source, name(0, 0, 1, z, w, part), other)
            pass_on(source, 0, 1, z, w, part, False, False)
        yield
    for z, w in here.column:
        for part in range(count):
            for y in here.y_steps:
                source = wholes[part].at[block(y=y, x=1, z=z, w=w)]
                wires.arrive(source, name(0, y, 1, z, w, part), other)
                pass_on(source, y, 1, z, w, part, False, False)
        yield
    for y in range(here.yo_size):
        for x in range(2):
            for z, w in here.column:
                for part in range(count):
                    index = here.chip(y=y, x=x, z=z, w=w) * 2 + 1 - here.core
                    wires.arrive(wholes[part].at[index], name(1, y, x, z, w, part), other)


def gather_experts_steps(here, wires, shards, wholes):
    count = len(shards)
    group = offsets_of(GROUP)
    other = here.at(core=1)

    def name(kind, y, x, z, w, part):
        spot = (((kind * here.yo_size + y) * 2 + x) * here.zo_size + z) * 2 + w
        return spot * count + part

    def member(x, w):
        yo, xi, zo, zi, core = here.at(x=x, w=w)
        return xi * 2 + zi

    for x, w in group[1:]:
        for part in range(count):
            wires.send(
                shards[part].at[member(x, w)],
                wholes[part].at[0, here.chip()],
                name(0, 0, x, 0, w, part),
                here.at(x=x, w=w),
            )

    def pass_on(source, y, x, z, w, part, to_z, to_y):
        index = here.chip(y=y, x=x, z=z, w=w)
        for step in here.z_steps if to_z else ():
            back = (z + here.back_z(step)) % here.zo_size
            wires.send(
                source, wholes[part].at[0, index], name(0, y, x, back, w, part), here.at(z=step)
            )
        for step in here.y_steps if to_y else ():
            back = (y + here.back_y(step)) % here.yo_size
            wires.send(
                source, wholes[part].at[0, index], name(0, back, x, z, w, part), here.at(y=step)
            )
        wires.send(source, wholes[part].at[1, index], name(1, y, x, z, w, part), other)

    for x, w in group:
        for part in range(count):
            if (x, w) == (0, 0):
                pass_on(shards[part].at[member(0, 0)], 0, 0, 0, 0, part, True, True)
                wholes[part][0, here.chip()] = shards[part][member(0, 0)]
            else:
                source = wholes[part].at[0, here.chip(x=x, w=w)]
                wires.arrive(source, name(0, 0, x, 0, w, part), other)
                pass_on(source, 0, x, 0, w, part, True, True)
        yield
    for x, w in group:
        for part in range(count):
            for z in here.z_steps:
                source = wholes[part].at[0, here.chip(x=x, w=w, z=z)]
                wires.arrive(source, name(0, 0, x, z, w, part), other)
                pass_on(source, 0, x, z, w, part, False, True)
        yield
    for z in range(here.zo_size):
        for x, w in group:
            for part in range(count):
                for y in here.y_steps:
                    source = wholes[part].at[0, here.chip(y=y, x=x, w=w, z=z)]
                    wires.arrive(source, name(0, y, x, z, w, part), other)
                    pass_on(source, y, x, z, w, part, False, False)
            yield
    for y in range(here.yo_size):
        for z in range(here.zo_size):
            for x, w in group:
                for part in range(count):
                    target = wholes[part].at[1, here.chip(y=y, x=x, w=w, z=z)]
                    wires.arrive(target, name(1, y, x, z, w, part), other)


ATTENTION_PARTS = 3
EXPERT_PARTS = 2


def greet_experts(here):
    greet(
        [here.at(x=x, w=w) for x, w in offsets_of(GROUP)[1:]]
        + [here.at(z=z) for z in here.z_steps]
        + [here.at(y=y) for y in here.y_steps]
        + [here.at(core=1)]
    )


def greet_attention(here):
    greet(
        [here.at(z=z, w=w) for z, w in here.column if (z, w) != (0, 0)]
        + [here.at(x=1), here.at(core=1)]
        + [here.at(y=y) for y in here.y_steps]
    )


def gather_kernel(sizes, count, *refs):
    ins, outs, sems = refs[:count], refs[count : 2 * count], refs[2 * count :]
    here = Place(sizes)
    cut = ATTENTION_PARTS
    wires = [Wires(*sems[:2])]
    steps = [gather_attention_steps(here, wires[0], ins[:cut], outs[:cut])]
    if count > cut:
        greet_layer(here)
        wires.append(Wires(*sems[2:]))
        steps.append(gather_experts_steps(here, wires[1], ins[cut:], outs[cut:]))
    else:
        greet_attention(here)
    together(*steps)
    for one in wires:
        one.drain()


def expert_sems(sizes):
    chips = sizes[0] * sizes[1] * 4
    sends = 3 + 4 * (sizes[0] + sizes[1]) + 4 * sizes[1] * sizes[0] + chips
    return [
        pltpu.SemaphoreType.DMA((EXPERT_PARTS * sends,)),
        pltpu.SemaphoreType.DMA((2 * chips * EXPERT_PARTS,)),
    ]


def gather(identity, attention_shards, expert_parts):
    sizes = mesh_sizes()
    chips = sizes[0] * sizes[1] * 4
    columns = sizes[1] * 2
    sends = ATTENTION_PARTS * ((columns - 1) + chips + columns * (2 * sizes[0] + 1) + chips)
    in_vmem = pl.BlockSpec(memory_space=pltpu.VMEM)
    count = len(attention_shards) + len(expert_parts)
    return pl.pallas_call(
        functools.partial(gather_kernel, sizes, count),
        out_shape=[
            jax.ShapeDtypeStruct((2 * chips,) + shard.shape, shard.dtype)
            for shard in attention_shards
        ]
        + [
            jax.ShapeDtypeStruct((2, chips) + part.shape[1:], part.dtype) for part in expert_parts
        ],
        in_specs=[in_vmem] * count,
        out_specs=[in_vmem] * count,
        scratch_shapes=[
            pltpu.SemaphoreType.DMA((sends,)),
            pltpu.SemaphoreType.DMA((2 * chips * ATTENTION_PARTS,)),
        ]
        + (expert_sems(sizes) if expert_parts else []),
        compiler_params=pltpu.CompilerParams(
            collective_id=identity, has_side_effects=True, vmem_limit_bytes=58 * 1024 * 1024
        ),
    )(*attention_shards, *expert_parts)


def sum_experts_steps(here, wires, whole, outs, first, second, third):
    count = len(whole)
    group = offsets_of(GROUP)
    other = here.at(core=1)
    chips = here.yo_size * here.zo_size * 4

    def place(y, z, member):
        return (y * here.zo_size + z) * 4 + member

    def name(kind, index, part):
        return (kind * chips + index) * count + part

    order = [
        (y, z, member)
        for y in list(here.y_steps) + [0]
        for z in list(here.z_steps) + [0]
        for member in (1, 2, 3, 0)
    ]
    for y, z, member in order:
        x, w = group[member]
        index = here.chip(y=y, x=x, z=z, w=w)
        spot = place(y, z, member)
        for part in range(count):
            wires.send(
                whole[part].at[1, index], first[part].at[spot], name(0, spot, part), other
            )
        if member == 0:
            yield
    for y, z, member in order:
        x, w = group[member]
        index = here.chip(y=y, x=x, z=z, w=w)
        spot = place(y, z, member)
        for part in range(count):
            total = first[part].at[spot]
            wires.arrive(total, name(0, spot, part), other)
            parts = [whole[part].at[0, index]]
            if y:
                add_rows(total, *parts)
                landing = place(here.back_y(y), z, member)
                wires.send(
                    total, second[part].at[landing - 4 * here.zo_size], name(1, landing, part), here.at(y=y)
                )
                continue
            for step in here.y_steps:
                spot_in = place(step, z, member)
                arrived = second[part].at[spot_in - 4 * here.zo_size]
                wires.arrive(arrived, name(1, spot_in, part), other)
                parts.append(arrived)
            if z:
                add_rows(total, *parts)
                landing = here.back_z(z) * 4 + member
                wires.send(
                    total, third[part].at[landing - 4], name(2, landing, part), here.at(z=z)
                )
                continue
            for step in here.z_steps:
                arrived = third[part].at[step * 4 + member - 4]
                wires.arrive(arrived, name(2, step * 4 + member, part), other)
                parts.append(arrived)
            add_rows(total, *parts)
            slot = here.xi * 2 + here.zi
            if member:
                wires.send(total, outs[part].at[slot], name(3, member, part), here.at(x=x, w=w))
            else:
                outs[part][slot] = total[...]
        yield
    for member in range(1, 4):
        x, w = group[member]
        yo, xi, zo, zi, core = here.at(x=x, w=w)
        for part in range(count):
            wires.arrive(outs[part].at[xi * 2 + zi], name(3, member, part), other)


def sum_attention_steps(here, wires, whole, outs, first, second, third, fourth):
    count = len(whole)
    columns = here.column
    other = here.at(core=1)
    width = len(columns)
    chips = here.yo_size * 2 * width

    def place(y, x, column):
        return (y * 2 + x) * width + column

    def name(kind, index, part):
        return (kind * chips + index) * count + part

    rounds = [
        (y, x, (column + 1) % width, part)
        for y, x in [(y, 1) for y in here.y_steps] + [(0, 1)] + [(y, 0) for y in here.y_steps] + [(0, 0)]
        for column in range(width)
        for part in range(count)
    ]
    for y, x, column, part in rounds:
        z, w = columns[column]
        spot = place(y, x, column)
        wires.send(
            whole[part].at[here.chip(y=y, x=x, z=z, w=w), 1 - here.core],
            first[part].at[spot],
            name(0, spot, part),
            other,
        )
        if (column, part) == (0, count - 1):
            yield
    for y, x, column, part in rounds:
        z, w = columns[column]
        spot = place(y, x, column)
        total = first[part].at[spot]
        wires.arrive(total, name(0, spot, part), other)
        parts = [whole[part].at[here.chip(y=y, x=x, z=z, w=w), here.core]]

        def take_in(buffer, kind, index, offset=0):
            arrived = buffer[part].at[index - offset]
            wires.arrive(arrived, name(kind, index, part), other)
            parts.append(arrived)

        def give(buffer, kind, index, device, offset=0):
            add_rows(total, *parts)
            wires.send(total, buffer[part].at[index - offset], name(kind, index, part), device)

        if x:
            give(second, 1, y * width + column, here.at(x=1))
            if part == count - 1:
                yield
            continue
        take_in(second, 1, y * width + column)
        if y:
            give(third, 2, here.back_y(y) * width + column, here.at(y=y), width)
            if part == count - 1:
                yield
            continue
        for step in here.y_steps:
            take_in(third, 2, step * width + column, width)
        if column:
            landing = columns.index((here.back_z(z), w))
            give(fourth, 3, landing, here.at(z=z, w=w), 1)
            if part == count - 1:
                yield
            continue
        for step in range(1, width):
            take_in(fourth, 3, step, 1)
        add_rows(total, *parts)
        outs[part][...] = total[...]


def sum_layer_kernel(sizes, *refs):
    both = ATTENTION_PARTS + EXPERT_PARTS
    cut = ATTENTION_PARTS
    ins, outs, rest = refs[:both], refs[both : 2 * both], refs[2 * both :]
    buffers, sems = rest[:-4], rest[-4:]
    attention = [buffers[level * cut : (level + 1) * cut] for level in range(4)]
    buffers = buffers[4 * cut :]
    experts = [buffers[level * EXPERT_PARTS : (level + 1) * EXPERT_PARTS] for level in range(3)]
    here = Place(sizes)
    wires = Wires(*sems[:2]), Wires(*sems[2:])
    greet_layer(here)
    together(
        sum_experts_steps(here, wires[1], ins[cut:], outs[cut:], *experts),
        sum_attention_steps(here, wires[0], ins[:cut], outs[:cut], *attention),
    )
    for one in wires:
        one.drain()


def sum_layer(attention_grads, expert_grads):
    sizes = mesh_sizes()
    chips = sizes[0] * sizes[1] * 4
    column = sizes[1] * 2
    attention = [grads.reshape(chips, 2, -1, grads.shape[1]) for grads in attention_grads]
    experts = [grads.reshape(2, chips, -1, D) for grads in expert_grads]
    in_vmem = pl.BlockSpec(memory_space=pltpu.VMEM)
    count = ATTENTION_PARTS + EXPERT_PARTS

    def held(blocks, sizes_of):
        return [
            pltpu.VMEM((sizes_of(part),) + block.shape[2:], jnp.bfloat16)
            for part, block in enumerate(blocks)
        ]

    return pl.pallas_call(
        functools.partial(sum_layer_kernel, sizes),
        out_shape=[jax.ShapeDtypeStruct(block.shape[2:], jnp.bfloat16) for block in attention]
        + [jax.ShapeDtypeStruct((4,) + block.shape[2:], jnp.bfloat16) for block in experts],
        in_specs=[in_vmem] * count,
        out_specs=[in_vmem] * count,
        scratch_shapes=held(attention, lambda part: chips)
        + held(attention, lambda part: sizes[0] * column)
        + held(attention, lambda part: (sizes[0] - 1) * column)
        + held(attention, lambda part: column - 1)
        + held(experts, lambda part: chips)
        + held(experts, lambda part: (sizes[0] - 1) * sizes[1] * 4)
        + held(experts, lambda part: (sizes[1] - 1) * 4)
        + [
            pltpu.SemaphoreType.DMA((3 * chips * ATTENTION_PARTS,)),
            pltpu.SemaphoreType.DMA((4 * chips * ATTENTION_PARTS,)),
            pltpu.SemaphoreType.DMA((3 * chips * EXPERT_PARTS,)),
            pltpu.SemaphoreType.DMA((4 * chips * EXPERT_PARTS,)),
        ],
        compiler_params=pltpu.CompilerParams(
            collective_id=5, has_side_effects=True, vmem_limit_bytes=62 * 1024 * 1024
        ),
    )(*attention, *experts)


def swap(value, axis):
    return lax.ppermute(value, axis, [(0, 1), (1, 0)])


def pick(value, index, axis=0):
    return lax.dynamic_index_in_dim(value, index, axis, keepdims=False)


def by_core(mine, theirs, axis):
    core = lax.axis_index("core")
    return jnp.where(
        core == 0, jnp.stack([mine, theirs], axis), jnp.stack([theirs, mine], axis)
    )


def gain_columns(gains):
    gains = gains.astype(jnp.bfloat16).T
    return jnp.pad(gains, ((0, 0), (0, 128 - gains.shape[1])))


def attention_shards(w_qkv, w_out, gains, layer):
    return [
        w_qkv[layer].astype(jnp.bfloat16),
        w_out[layer].astype(jnp.bfloat16),
        gain_columns(gains[layer]),
    ]


def expert_parts(w_gateup, w_down, layer):
    core = lax.axis_index("core")
    parts = []
    for shard in (w_gateup[layer], w_down[layer]):
        shard = shard.astype(jnp.bfloat16)
        shard = shard.reshape((4, 2) + shard.shape[1:])
        theirs = swap(pick(shard, 1 - core, 1), "core")
        parts.append(by_core(pick(shard, core, 1), theirs, 1).reshape(4, -1, D))
    return parts


def attention_matrices(qkv, out, gain):
    gain = gain.reshape(D, 128)[:, :2].T.astype(jnp.float32)
    return qkv.reshape(D, QKV), out.reshape(D, D), gain


def expert_matrices(up, down):
    return up.reshape(2, D, 2 * F), down.reshape(2, F, D)


def layer_sums(grad_qkv, grad_out, grad_up, grad_down, grad_gains):
    core = lax.axis_index("core")
    attention = [
        grad_qkv.astype(jnp.bfloat16),
        grad_out.astype(jnp.bfloat16),
        gain_columns(grad_gains),
    ]
    qkv, out, gain, up, down = sum_layer(attention, [grad_up, grad_down])
    result = [qkv, out]
    for part in (up, down):
        part = part.reshape(4, 2, -1, D)
        theirs = swap(pick(part, 1 - core, 1), "core")
        pair = by_core(pick(part, core, 1), theirs, 1)
        result.append(pair.reshape(EXPERTS, -1, D))
    return result + [gain[:, :2].T]


SQRT_HALF = 0.7071067811865476
PDF_SCALE = 0.3989422804014327
TILE = 256
TILES = F // TILE


def selections(table, columns):
    rows = table.shape[1]
    slots = lax.broadcasted_iota(jnp.int32, (CAP, rows), 0).astype(jnp.float32)
    take = (table[0:1, :] == slots).astype(jnp.bfloat16)
    slots = lax.broadcasted_iota(jnp.int32, (rows, CAP), 1).astype(jnp.float32)
    spread = (columns[:, 0:1] == slots).astype(jnp.bfloat16)
    return take, spread, columns[:, 1:2]


def dot(left, right, contract=(1, 0)):
    return lax.dot_general(
        left,
        right,
        (((contract[0],), (contract[1],)), ((), ())),
        preferred_element_type=jnp.float32,
    )


def experts_grads_kernel(slot_in, active, slot_grad, grad_gate, grad_up, up_out, down_out):
    up_out[0, :, :F] = dot(slot_in[0], grad_gate[0], (0, 0)).astype(jnp.bfloat16)
    up_out[0, :, F:] = dot(slot_in[0], grad_up[0], (0, 0)).astype(jnp.bfloat16)
    down_out[0] = dot(active[0], slot_grad[0], (0, 0)).astype(jnp.bfloat16)


def whole_block(shape):
    return pl.BlockSpec(shape, lambda e, f: (0,) * len(shape))


def expert_block(shape):
    return pl.BlockSpec((1,) + shape, lambda e, f: (e,) + (0,) * len(shape))


WAVES = ((0,), (3,), (1, 2))
TURNS = ((0, 2), (1, 1), (2, 2))


def moe_forward_kernel(sizes, background, *refs):
    tokens, tables, columns, up_w, down_w = refs[:5]
    extra = EXPERT_PARTS if background else 0
    shards, refs = refs[5 : 5 + extra], refs[5 + extra :]
    merged, slot_out, gate_out, up_out, active_out = refs[:5]
    wholes, refs = refs[5 : 5 + extra], refs[5 + extra :]
    chunks, leaving, coming, slot_in, result, total = refs[:6]
    sems = refs[6:]
    here = Place(sizes)
    wires = Wires(*sems[:2])
    partners = [here.at(x=x, w=w) for x, w in offsets_of(GROUP)]
    if background:
        greet_experts(here)
        other_wires = Wires(*sems[2:])
        steps = gather_experts_steps(here, other_wires, shards, wholes)
    else:
        greet(partners[1:])
        steps = iter(())
    for place in (3, 1, 2):
        wires.send(tokens, chunks.at[place - 1], place - 1, partners[place])
    next(steps, None)
    for wave, turns in zip(WAVES, TURNS):
        sources = []
        for place in wave:
            source = tokens if place == 0 else chunks.at[place - 1]
            if place:
                wires.arrive(source, place - 1, partners[place])
            sources.append(source)
        count = CAP * len(wave)
        rows = pl.ds(wave[0] * CAP, count)
        for expert in range(2):
            picks = [selections(tables[place, expert], columns[place, expert]) for place in wave]
            for index, source in enumerate(sources):
                chosen = dot(picks[index][0], source[...]).astype(jnp.bfloat16)
                slot_in[index * CAP : (index + 1) * CAP] = chosen
            slot_out[expert, rows, :] = slot_in[:count]

            def step(tile, carry, expert=expert, count=count, rows=rows):
                at_gate = pl.ds(pl.multiple_of(tile * TILE, TILE), TILE)
                at_up = pl.ds(pl.multiple_of(F + tile * TILE, TILE), TILE)
                gate = dot(slot_in[:count], up_w[expert, :, at_gate])
                up = dot(slot_in[:count], up_w[expert, :, at_up])
                active = (0.5 * gate * (1.0 + lax.erf(gate * SQRT_HALF)) * up).astype(jnp.bfloat16)
                gate_out[expert, rows, at_gate] = gate.astype(jnp.bfloat16)
                up_out[expert, rows, at_gate] = up.astype(jnp.bfloat16)
                active_out[expert, rows, at_gate] = active
                return carry

            lax.fori_loop(0, TILES, step, 0)

            def finish(tile, carry, expert=expert, count=count, rows=rows):
                lanes = pl.ds(pl.multiple_of(tile * 2 * TILE, TILE), 2 * TILE)
                result[:count, lanes] = dot(
                    active_out[expert, rows, :], down_w[expert, :, lanes]
                ).astype(jnp.bfloat16)
                return carry

            lax.fori_loop(0, D // (2 * TILE), finish, 0)
            for index in range(len(wave)):
                take, spread, gates = picks[index]
                share = dot(spread, result[index * CAP : (index + 1) * CAP]) * gates
                if expert == 0:
                    total[index] = share
                else:
                    total[index] += share
            for turn in range(turns[expert]):
                next(steps, None)
        for index, place in enumerate(wave):
            if place == 0:
                merged[...] = total[index]
            else:
                leaving[place - 1] = total[index].astype(jnp.bfloat16)
                wires.send(
                    leaving.at[place - 1], coming.at[place - 1], place + 2, partners[place]
                )
    for one in steps:
        pass
    for place in range(1, 4):
        wires.arrive(coming.at[place - 1], place + 2, partners[place])
        merged[...] += coming[place - 1].astype(jnp.float32)
    wires.drain()
    if background:
        other_wires.drain()


def moe_backward_kernel(sizes, background, *refs):
    gradient, tables, columns, up_w, down_w, gate_in, up_in = refs[:7]
    merged, slot_out, gate_out, up_out = refs[7:11]
    chunks, leaving, coming, slot_grad, slots, total = refs[11:17]
    here = Place(sizes)
    wires = Wires(*refs[17:])
    partners = [here.at(x=x, w=w) for x, w in offsets_of(GROUP)]
    greet(partners[1:])
    leaving[3] = gradient[...].astype(jnp.bfloat16)
    for place in (3, 1, 2):
        wires.send(leaving.at[3], chunks.at[place - 1], place - 1, partners[place])
    for wave in WAVES:
        sources = []
        for place in wave:
            source = gradient if place == 0 else chunks.at[place - 1]
            if place:
                wires.arrive(source, place - 1, partners[place])
            sources.append(source)
        count = CAP * len(wave)
        rows = pl.ds(wave[0] * CAP, count)
        for expert in range(2):
            picks = [selections(tables[place, expert], columns[place, expert]) for place in wave]
            for index, source in enumerate(sources):
                take, spread, gates = picks[index]
                weighted = (gates * source[...].astype(jnp.float32)).astype(jnp.bfloat16)
                slot_grad[index * CAP : (index + 1) * CAP] = dot(take, weighted).astype(jnp.bfloat16)
            slot_out[expert, rows, :] = slot_grad[:count]

            def step(tile, carry, expert=expert, count=count, rows=rows):
                at_gate = pl.ds(pl.multiple_of(tile * TILE, TILE), TILE)
                grad_act = dot(slot_grad[:count], down_w[expert, at_gate, :], (1, 1))
                gate = gate_in[expert, rows, at_gate].astype(jnp.float32)
                up = up_in[expert, rows, at_gate].astype(jnp.float32)
                below = 0.5 * (1.0 + lax.erf(gate * SQRT_HALF))
                slope = below + gate * PDF_SCALE * jnp.exp(-0.5 * gate * gate)
                gate_out[expert, rows, at_gate] = (grad_act * up * slope).astype(jnp.bfloat16)
                up_out[expert, rows, at_gate] = (grad_act * gate * below).astype(jnp.bfloat16)
                return carry

            lax.fori_loop(0, TILES, step, 0)

            def finish(tile, carry, expert=expert, count=count, rows=rows):
                lanes = pl.ds(pl.multiple_of(tile * 2 * TILE, TILE), 2 * TILE)
                part = dot(gate_out[expert, rows, :], up_w[expert, lanes, :F], (1, 1))
                part = part + dot(up_out[expert, rows, :], up_w[expert, lanes, F:], (1, 1))
                slots[:count, lanes] = part.astype(jnp.bfloat16)
                return carry

            lax.fori_loop(0, D // (2 * TILE), finish, 0)
            for index in range(len(wave)):
                share = dot(picks[index][1], slots[index * CAP : (index + 1) * CAP])
                if expert == 0:
                    total[index] = share
                else:
                    total[index] += share
        for index, place in enumerate(wave):
            if place == 0:
                merged[...] = total[index]
            else:
                leaving[place - 1] = total[index].astype(jnp.bfloat16)
                wires.send(
                    leaving.at[place - 1], coming.at[place - 1], place + 2, partners[place]
                )
    for place in range(1, 4):
        wires.arrive(coming.at[place - 1], place + 2, partners[place])
        merged[...] += coming[place - 1].astype(jnp.float32)
    wires.drain()


def moe_call(kernel, identity, rows_in, tables, weights, extra, kinds, background=()):
    rows = rows_in.shape[0]
    slots = 4 * CAP
    sizes = mesh_sizes()
    chips = sizes[0] * sizes[1] * 4
    operands = [rows_in, tables, jnp.swapaxes(tables, 2, 3), *weights, *extra, *background]
    in_vmem = pl.BlockSpec(memory_space=pltpu.VMEM)
    more_sems = expert_sems(sizes) if background else []
    return pl.pallas_call(
        functools.partial(kernel, sizes, bool(background)),
        in_specs=[in_vmem] * len(operands),
        out_specs=[in_vmem] * (1 + len(kinds) + len(background)),
        out_shape=[jax.ShapeDtypeStruct((rows, D), jnp.float32)]
        + [jax.ShapeDtypeStruct((2, slots, width), jnp.bfloat16) for width in kinds]
        + [jax.ShapeDtypeStruct((2, chips) + part.shape[1:], part.dtype) for part in background],
        scratch_shapes=[
            pltpu.VMEM((3, rows, D), jnp.bfloat16),
            pltpu.VMEM((4, rows, D), jnp.bfloat16),
            pltpu.VMEM((3, rows, D), jnp.bfloat16),
            pltpu.VMEM((2 * CAP, D), jnp.bfloat16),
            pltpu.VMEM((2 * CAP, D), jnp.bfloat16),
            pltpu.VMEM((2, rows, D), jnp.float32),
            pltpu.SemaphoreType.DMA((6,)),
            pltpu.SemaphoreType.DMA((6,)),
        ]
        + more_sems,
        compiler_params=pltpu.CompilerParams(
            collective_id=identity, has_side_effects=True, vmem_limit_bytes=62 * 1024 * 1024
        ),
        cost_estimate=pl.CostEstimate(
            flops=48 * CAP * D * F, bytes_accessed=40_000_000, transcendentals=8 * CAP * F
        ),
    )(*operands)


def moe_forward(expert_in, tables, weights, background):
    merged, *kept = moe_call(
        moe_forward_kernel,
        2 if background else 3,
        expert_in,
        tables,
        weights,
        [],
        (D, F, F, F),
        background,
    )
    return merged, kept[:4], expert_matrices(*kept[4:]) if background else None


def moe_backward(gradient, tables, weights, kept):
    slot_in, gate, up, active = kept
    total, slot_grad, grad_gate, grad_up = moe_call(
        moe_backward_kernel, 4, gradient, tables, weights, [gate, up], (D, F, F)
    )
    slots = slot_in.shape[1]

    def columns_of(width):
        return pl.BlockSpec((1, slots, width), lambda e, i: (e, 0, i))

    grads = pl.pallas_call(
        experts_grads_kernel,
        grid=(2, 3),
        in_specs=[
            columns_of(D // 3),
            columns_of(F // 3),
            expert_block((slots, D)),
            expert_block((slots, F)),
            expert_block((slots, F)),
        ],
        out_specs=[
            pl.BlockSpec((1, D // 3, 2 * F), lambda e, i: (e, i, 0)),
            pl.BlockSpec((1, F // 3, D), lambda e, i: (e, i, 0)),
        ],
        out_shape=[
            jax.ShapeDtypeStruct((2, D, 2 * F), jnp.bfloat16),
            jax.ShapeDtypeStruct((2, F, D), jnp.bfloat16),
        ],
        compiler_params=pltpu.CompilerParams(vmem_limit_bytes=48 * 1024 * 1024),
        cost_estimate=pl.CostEstimate(
            flops=12 * slots * D * F, bytes_accessed=30_000_000, transcendentals=0
        ),
    )(slot_in, active, slot_grad, grad_gate, grad_up)
    return total, grads[0], grads[1]


def layer_forward(stream, attn_w, expert_w, ahead, tables, allowed, cosine_table, sine_table):
    qkv_w, out_w, gain_full = attn_w
    row_count = stream.shape[0]
    normed, scale_one = normalize(stream, gain_full[0])
    attn_in = normed.astype(jnp.bfloat16)
    projected = jnp.dot(attn_in, qkv_w, preferred_element_type=jnp.float32)
    queries = rotate(
        projected[:, : H * HD].reshape(row_count, H, HD), cosine_table, sine_table
    ).astype(jnp.bfloat16)
    keys_local = rotate(
        projected[:, H * HD : (H + KVH) * HD].reshape(row_count, KVH, HD), cosine_table, sine_table
    ).astype(jnp.bfloat16)
    values_local = projected[:, (H + KVH) * HD :].reshape(row_count, KVH, HD).astype(jnp.bfloat16)
    both = jnp.concatenate([keys_local, values_local], axis=1)
    both_all = jnp.concatenate([send(both, CTX, offsets) for offsets in offsets_of(CTX)], axis=0)
    keys_all, values_all = both_all[:, :KVH], both_all[:, KVH:]
    attended, totals = attention_forward(queries, keys_all, values_all, allowed)
    attended_low = attended.reshape(row_count, H * HD).astype(jnp.bfloat16)
    middle_stream = stream + jnp.dot(attended_low, out_w, preferred_element_type=jnp.float32)
    normed_two, scale_two = normalize(middle_stream, gain_full[1])
    expert_in = normed_two.astype(jnp.bfloat16)
    merged, kept, gathered = moe_forward(expert_in, tables, expert_w, ahead)
    record = {
        "stream": stream,
        "scale_one": scale_one,
        "attn_in": attn_in,
        "queries": queries,
        "keys_all": keys_all,
        "values_all": values_all,
        "totals": totals,
        "attended": attended_low,
        "middle": middle_stream,
        "scale_two": scale_two,
        "kept": kept,
    }
    return (record, middle_stream + merged, gathered)


def layer_backward(gradient, record, attn_w, expert_w, tables, allowed, cosine_table, sine_table):
    qkv_w, out_w, gain_full = attn_w
    row_count = gradient.shape[0]
    grad_normed, grad_up, grad_down = moe_backward(gradient, tables, expert_w, record["kept"])
    grad_normed, grad_up, grad_down = lax.optimization_barrier((grad_normed, grad_up, grad_down))
    grad_in_two, grad_gain_two = normalize_back(
        grad_normed, record["middle"], record["scale_two"], gain_full[1]
    )
    grad_middle = gradient + grad_in_two
    grad_middle_low = grad_middle.astype(jnp.bfloat16)
    grad_out = jnp.dot(record["attended"].T, grad_middle_low, preferred_element_type=jnp.float32)
    grad_attended = jnp.dot(grad_middle_low, out_w.T, preferred_element_type=jnp.float32)
    grad_attended = grad_attended.astype(jnp.bfloat16).reshape(row_count, H, HD)
    grad_queries, grad_keys_all, grad_values_all = attention_backward(
        record["queries"],
        record["keys_all"],
        record["values_all"],
        allowed,
        record["totals"],
        grad_attended,
    )
    both_all = jnp.concatenate([grad_keys_all, grad_values_all], axis=1)
    both = None
    for place, offsets in enumerate(offsets_of(CTX)):
        part = both_all[place * row_count : (place + 1) * row_count]
        if offsets != (0, 0):
            part = send(part.astype(jnp.bfloat16), CTX, offsets, back=True).astype(jnp.float32)
        both = part if both is None else both + part
    grad_keys, grad_values = both[:, :KVH], both[:, KVH:]
    grad_projected = jnp.concatenate(
        [
            rotate_back(grad_queries, cosine_table, sine_table).reshape(row_count, H * HD),
            rotate_back(grad_keys, cosine_table, sine_table).reshape(row_count, KVH * HD),
            grad_values.reshape(row_count, KVH * HD),
        ],
        axis=1,
    ).astype(jnp.bfloat16)
    grad_qkv = jnp.dot(record["attn_in"].T, grad_projected, preferred_element_type=jnp.float32)
    grad_normed_one = jnp.dot(grad_projected, qkv_w.T, preferred_element_type=jnp.float32)
    grad_in_one, grad_gain_one = normalize_back(
        grad_normed_one, record["stream"], record["scale_one"], gain_full[0]
    )
    grad_gains = jnp.stack([grad_gain_one, grad_gain_two])
    return (grad_middle + grad_in_one, (grad_qkv, grad_out, grad_up, grad_down, grad_gains))


def on_device(
    tokens,
    cotangent,
    routes,
    gate_weights,
    lengths,
    block_map,
    w_qkv,
    w_out,
    w_gateup,
    w_down,
    gains,
    m_qkv,
    v_qkv,
    m_out,
    v_out,
    m_gateup,
    v_gateup,
    m_down,
    v_down,
    m_gains,
    v_gains,
):
    row_count = tokens.shape[1]
    block_rows = row_count // 2
    own_pos, own_doc = positions_docs(block_map, lengths[0], flat_index(CTX), block_rows)
    places = [
        positions_docs(block_map, lengths[0], source_index(CTX, offsets), block_rows)
        for offsets in offsets_of(CTX)
    ]
    key_pos = jnp.concatenate([place[0] for place in places])
    key_doc = jnp.concatenate([place[1] for place in places])
    allowed = (own_doc[:, None] == key_doc[None, :]) & (key_pos[None, :] <= own_pos[:, None])
    cosine_table, sine_table = rope_tables(own_pos)
    own_tables = jnp.stack(
        [dispatch_tables(routes[layer, 0], gate_weights[layer, 0]) for layer in range(LAYERS)]
    )
    core = lax.axis_index("core")
    group_tables = []
    for offsets in offsets_of(GROUP):
        theirs = lax.dynamic_slice_in_dim(own_tables, 2 * target_index(GROUP, offsets), 2, axis=1)
        theirs = jnp.where(core == 0, theirs, theirs[:, ::-1])
        group_tables.append(send(theirs, GROUP, offsets))
    group_tables = jnp.stack(group_tables, axis=1)
    stream = tokens[0].astype(jnp.float32)
    records = []
    shards = [attention_shards(w_qkv, w_out, gains, layer) for layer in range(LAYERS)]
    parts = [expert_parts(w_gateup, w_down, layer) for layer in range(LAYERS)]
    first = gather(0, shards[0], [])
    parts[0], first = lax.optimization_barrier((parts[0], first))
    second = gather(1, shards[1], parts[0])
    cut = ATTENTION_PARTS
    attn_w = [attention_matrices(*first), attention_matrices(*second[:cut])]
    expert_w = [expert_matrices(*second[cut:]), None]
    for layer_index in range(LAYERS):
        ahead = [] if layer_index else parts[1]
        record, stream, gathered = layer_forward(
            stream,
            attn_w[layer_index],
            expert_w[layer_index],
            ahead,
            group_tables[layer_index],
            allowed,
            cosine_table,
            sine_table,
        )
        records.append(record)
        if ahead:
            expert_w[1] = gathered
    output = stream.astype(jnp.bfloat16)[None]
    gradient = cotangent[0].astype(jnp.float32)
    rates = (D ** (-0.5), 0.5, D ** (-0.5), (F // 8) ** (-0.5), 1.0)
    decays = (DECAY, DECAY, DECAY, DECAY, 0.0)
    params = (w_qkv, w_out, w_gateup, w_down, gains)
    firsts = (m_qkv, m_out, m_gateup, m_down, m_gains)
    seconds = (v_qkv, v_out, v_gateup, v_down, v_gains)
    sums = [None] * LAYERS
    for layer_index in reversed(range(LAYERS)):
        gradient, layer_grads = layer_backward(
            gradient,
            records[layer_index],
            attn_w[layer_index],
            expert_w[layer_index],
            group_tables[layer_index],
            allowed,
            cosine_table,
            sine_table,
        )
        sums[layer_index] = layer_sums(*layer_grads)
    updated = []
    for which in range(5):
        total = jnp.stack([sums[layer][which] for layer in range(LAYERS)]).astype(jnp.float32)
        updated.extend(
            adamw(
                params[which], firsts[which], seconds[which], total, rates[which], decays[which]
            )
        )
    return (output, gradient[None], *updated)


def solution(mesh):
    ctx_size, shard_size = mesh.shape["ctx"], mesh.shape["shard"]
    fine = Mesh(mesh.devices.reshape(ctx_size // 2, 2, shard_size // 4, 2, 2), ALL)
    tokens = P(SHARD, CTX, None)
    routed = P(None, SHARD, CTX, None)
    rows_two = P(None, ALL, None)
    rows_three = P(None, None, ALL, None)
    gain = P(None, None, ALL)
    weights = (rows_two, rows_two, rows_three, rows_three, gain)
    states = tuple(spec for spec in weights for which in range(2))
    return jax.shard_map(
        on_device,
        mesh=fine,
        in_specs=(tokens, tokens, routed, routed, P(SHARD, None), P()) + weights + states,
        out_specs=(tokens, tokens) + tuple(spec for spec in weights for which in range(3)),
        check_vma=False,
    )
```

```python
import functools

import jax
import jax.numpy as jnp
from jax import lax
from jax.experimental import pallas as pl
from jax.experimental.pallas import tpu as pltpu
from jax.sharding import Mesh
from jax.sharding import PartitionSpec as P

D = 1536
H = 12
KVH = 2
HD = 128
F = 768
TOP = 4
EXPERTS = 8
LAYERS = 2
STEP = 10
CAP = 160


NORM_EPS = 1e-06
ROPE_BASE = 1000000.0
BETA_ONE = 0.9
BETA_TWO = 0.95
ADAM_EPS = 1e-08
DECAY = 0.1
MASKED = -1e30


def rope_tables(positions):
    half_width = HD // 2
    frequency = ROPE_BASE ** (-(jnp.arange(half_width, dtype=jnp.float32) * 2.0 / HD))
    angles = positions.astype(jnp.float32)[:, None] * frequency[None, :]
    cosine, sine = jnp.cos(angles), jnp.sin(angles)
    return jnp.concatenate([cosine, cosine], axis=1), jnp.concatenate([-sine, sine], axis=1)


def normalize(values, gain_row):
    row_scale = lax.rsqrt(jnp.mean(values * values, axis=-1, keepdims=True) + NORM_EPS)
    return (values * row_scale * gain_row, row_scale)


def normalize_back(gradient, values, row_scale, gain_row):
    unit_rows = values * row_scale
    inner_grad = gradient * gain_row
    input_grad = row_scale * (
        inner_grad - unit_rows * jnp.mean(inner_grad * unit_rows, axis=-1, keepdims=True)
    )
    return (input_grad, jnp.sum(gradient * unit_rows, axis=0))


def adamw(parameter, moment, second, gradient, step_rate, decay_rate):
    moment = BETA_ONE * moment + (1.0 - BETA_ONE) * gradient
    second = BETA_TWO * second + (1.0 - BETA_TWO) * gradient * gradient
    direction = (
        moment / (1.0 - BETA_ONE**STEP) / (jnp.sqrt(second / (1.0 - BETA_TWO**STEP)) + ADAM_EPS)
    )
    return (parameter - step_rate * (direction + decay_rate * parameter), moment, second)


CTX = ("yo", "xi")
SHARD = ("zo", "zi", "core")
ALL = CTX + SHARD
GROUP = ("xi", "zi")
REPLICAS = ("yo", "zo", "core")


def flat_index(axes):
    index = 0
    for axis in axes:
        index = index * lax.axis_size(axis) + lax.axis_index(axis)
    return index


def shift_permutation(axes, offsets, back=False):
    sizes = [lax.axis_size(axis) for axis in axes]
    pairs = []
    for first in range(sizes[0]):
        for second in range(sizes[1]):
            target = ((first + offsets[0]) % sizes[0], (second + offsets[1]) % sizes[1])
            here = first * sizes[1] + second
            there = target[0] * sizes[1] + target[1]
            pairs.append((there, here) if back else (here, there))
    return pairs


def offsets_of(axes):
    sizes = [lax.axis_size(axis) for axis in axes]
    return [(a, b) for a in range(sizes[0]) for b in range(sizes[1])]


def send(value, axes, offsets, back=False):
    if offsets == (0, 0):
        return value
    return lax.ppermute(value, axes, shift_permutation(axes, offsets, back))


def source_index(axes, offsets):
    sizes = [lax.axis_size(axis) for axis in axes]
    return lax.rem(lax.axis_index(axes[0]) - offsets[0] + sizes[0], sizes[0]) * sizes[1] + lax.rem(
        lax.axis_index(axes[1]) - offsets[1] + sizes[1], sizes[1]
    )


def target_index(axes, offsets):
    sizes = [lax.axis_size(axis) for axis in axes]
    return lax.rem(lax.axis_index(axes[0]) + offsets[0], sizes[0]) * sizes[1] + lax.rem(
        lax.axis_index(axes[1]) + offsets[1], sizes[1]
    )


def positions_docs(block_map, lengths_row, ctx_index, block_rows):
    blocks = lax.dynamic_slice_in_dim(block_map, 2 * ctx_index, 2)
    offsets = jnp.arange(block_rows, dtype=jnp.int32)
    positions = (blocks[:, None] * block_rows + offsets[None, :]).reshape(-1)
    bounds = jnp.cumsum(lengths_row)
    documents = jnp.sum((positions[:, None] >= bounds[None, :]).astype(jnp.int32), axis=1)
    return (positions, documents)


def dispatch_tables(routes, gates):
    rows = routes.shape[0]
    hits = (routes[None] == jnp.arange(EXPERTS, dtype=jnp.int32)[:, None, None]).astype(jnp.float32)
    member = jnp.sum(hits, axis=-1)
    gate = jnp.sum(hits * gates[None], axis=-1)
    before = (jnp.arange(rows)[:, None] < jnp.arange(rows)[None, :]).astype(jnp.float32)
    rank = jnp.dot(member, before, preferred_element_type=jnp.float32)
    return jnp.stack([jnp.where(member > 0, rank, -1.0), gate], axis=1)


MESH = pl.DeviceIdType.MESH
QKV = (H + 2 * KVH) * HD


class Place:
    def __init__(self, sizes):
        self.yo_size, self.zo_size = sizes
        self.yo, self.xi, self.zo, self.zi, self.core = [lax.axis_index(axis) for axis in ALL]
        self.y_steps = range(1, self.yo_size)
        self.z_steps = range(1, self.zo_size)
        self.column = [(a, b) for a in range(self.zo_size) for b in range(2)]

    def at(self, y=0, x=0, z=0, w=0, core=0):
        return (
            lax.rem(self.yo + y, self.yo_size),
            1 - self.xi if x else self.xi,
            lax.rem(self.zo + z, self.zo_size),
            1 - self.zi if w else self.zi,
            1 - self.core if core else self.core,
        )

    def chip(self, y=0, x=0, z=0, w=0):
        yo, xi, zo, zi, core = self.at(y, x, z, w)
        return ((yo * 2 + xi) * self.zo_size + zo) * 2 + zi

    def back_y(self, y):
        return (self.yo_size - y) % self.yo_size

    def back_z(self, z):
        return (self.zo_size - z) % self.zo_size


class Wires:
    def __init__(self, send_sems, recv_sems):
        self.send_sems, self.recv_sems = send_sems, recv_sems
        self.started = []

    def send(self, source, target, name, device):
        copy = pltpu.make_async_remote_copy(
            src_ref=source,
            dst_ref=target,
            send_sem=self.send_sems.at[len(self.started)],
            recv_sem=self.recv_sems.at[name],
            device_id=device,
            device_id_type=MESH,
        )
        copy.start()
        self.started.append(copy)

    def arrive(self, target, name, device):
        pltpu.make_async_remote_copy(
            src_ref=target,
            dst_ref=target,
            send_sem=self.send_sems.at[0],
            recv_sem=self.recv_sems.at[name],
            device_id=device,
            device_id_type=MESH,
        ).wait_recv()

    def drain(self):
        for copy in self.started:
            copy.wait_send()


def greet(partners):
    barrier = pltpu.get_barrier_semaphore()
    for partner in partners:
        pl.semaphore_signal(barrier, inc=1, device_id=partner, device_id_type=MESH)
    pl.semaphore_wait(barrier, len(partners))


def mesh_sizes():
    return lax.axis_size("yo"), lax.axis_size("zo")


def add_rows(target, *parts):
    size = 16 if target.shape[0] % 16 == 0 else target.shape[0]

    def step(index, carry):
        rows = pl.ds(pl.multiple_of(index * size, size), size)
        total = target[rows, :].astype(jnp.float32)
        for part in parts:
            total = total + part[rows, :].astype(jnp.float32)
        target[rows, :] = total.astype(target.dtype)
        return carry

    lax.fori_loop(0, target.shape[0] // size, step, 0)


def together(*steps):
    alive = list(steps)
    while alive:
        for one in list(alive):
            try:
                next(one)
            except StopIteration:
                alive.remove(one)


def greet_layer(here):
    greet(
        [here.at(z=z, w=w) for z, w in here.column if (z, w) != (0, 0)]
        + [here.at(x=1), here.at(x=1, w=1), here.at(core=1)]
        + [here.at(y=y) for y in here.y_steps]
    )


def gather_attention_steps(here, wires, shards, wholes, even):
    count = len(shards)
    far = [offset for offset in here.column if offset != (0, 0)]
    mine = here.chip() * 2 + here.core
    other = here.at(core=1)

    def block(**offsets):
        return here.chip(**offsets) * 2 + here.core

    def name(kind, y, x, z, w, part):
        spot = (((kind * here.yo_size + y) * 2 + x) * here.zo_size + z) * 2 + w
        return spot * count + part

    for z, w in far:
        for part in range(count):
            wires.send(
                shards[part],
                wholes[part].at[mine],
                name(0, 0, 0, here.back_z(z), w, part),
                here.at(z=z, w=w),
            )

    def pass_on(source, y, x, z, w, part, to_x, to_y):
        target = wholes[part].at[block(y=y, x=x, z=z, w=w)]
        if to_x:
            wires.send(source, target, name(0, y, 1 - x, z, w, part), here.at(x=1))
        for step in here.y_steps if to_y else ():
            back = (y + here.back_y(step)) % here.yo_size
            wires.send(source, target, name(0, back, x, z, w, part), here.at(y=step))
        wires.send(source, target, name(1, y, x, z, w, part), other)

    for z, w in here.column:
        for part in range(count):
            if (z, w) == (0, 0):
                pass_on(shards[part], 0, 0, 0, 0, part, True, True)
                wholes[part][mine] = shards[part][...]
            else:
                source = wholes[part].at[block(z=z, w=w)]
                wires.arrive(source, name(0, 0, 0, z, w, part), other)
                pass_on(source, 0, 0, z, w, part, True, True)
        yield
    for z, w in here.column:
        for part in range(count):
            for y in here.y_steps:
                source = wholes[part].at[block(y=y, z=z, w=w)]
                wires.arrive(source, name(0, y, 0, z, w, part), other)
                pass_on(source, y, 0, z, w, part, not even or part % 2 == 0, False)
        yield
    for z, w in here.column:
        for part in range(count):
            source = wholes[part].at[block(x=1, z=z, w=w)]
            wires.arrive(source, name(0, 0, 1, z, w, part), other)
            pass_on(source, 0, 1, z, w, part, False, even and part % 2 == 1)
        yield
    for z, w in here.column:
        for part in range(count):
            for y in here.y_steps:
                source = wholes[part].at[block(y=y, x=1, z=z, w=w)]
                wires.arrive(source, name(0, y, 1, z, w, part), other)
                pass_on(source, y, 1, z, w, part, False, False)
        yield
    for y in range(here.yo_size):
        for x in range(2):
            for z, w in here.column:
                for part in range(count):
                    index = here.chip(y=y, x=x, z=z, w=w) * 2 + 1 - here.core
                    wires.arrive(wholes[part].at[index], name(1, y, x, z, w, part), other)


def gather_experts_steps(here, wires, shards, wholes):
    count = len(shards)
    group = offsets_of(GROUP)
    other = here.at(core=1)

    def name(kind, y, x, z, w, part):
        spot = (((kind * here.yo_size + y) * 2 + x) * here.zo_size + z) * 2 + w
        return spot * count + part

    def member(x, w):
        yo, xi, zo, zi, core = here.at(x=x, w=w)
        return xi * 2 + zi

    for x, w in group[1:]:
        for part in range(count):
            wires.send(
                shards[part].at[member(x, w)],
                wholes[part].at[0, here.chip()],
                name(0, 0, x, 0, w, part),
                here.at(x=x, w=w),
            )

    def pass_on(source, y, x, z, w, part, to_z, to_y):
        index = here.chip(y=y, x=x, z=z, w=w)
        for step in here.z_steps if to_z else ():
            back = (z + here.back_z(step)) % here.zo_size
            wires.send(
                source, wholes[part].at[0, index], name(0, y, x, back, w, part), here.at(z=step)
            )
        for step in here.y_steps if to_y else ():
            back = (y + here.back_y(step)) % here.yo_size
            wires.send(
                source, wholes[part].at[0, index], name(0, back, x, z, w, part), here.at(y=step)
            )
        wires.send(source, wholes[part].at[1, index], name(1, y, x, z, w, part), other)

    for x, w in group:
        for part in range(count):
            if (x, w) == (0, 0):
                pass_on(shards[part].at[member(0, 0)], 0, 0, 0, 0, part, True, True)
                wholes[part][0, here.chip()] = shards[part][member(0, 0)]
            else:
                source = wholes[part].at[0, here.chip(x=x, w=w)]
                wires.arrive(source, name(0, 0, x, 0, w, part), other)
                pass_on(source, 0, x, 0, w, part, True, True)
        yield
    for x, w in group:
        for part in range(count):
            for z in here.z_steps:
                source = wholes[part].at[0, here.chip(x=x, w=w, z=z)]
                wires.arrive(source, name(0, 0, x, z, w, part), other)
                pass_on(source, 0, x, z, w, part, False, True)
        yield
    for z in range(here.zo_size):
        for x, w in group:
            for part in range(count):
                for y in here.y_steps:
                    source = wholes[part].at[0, here.chip(y=y, x=x, w=w, z=z)]
                    wires.arrive(source, name(0, y, x, z, w, part), other)
                    pass_on(source, y, x, z, w, part, False, False)
            yield
    for y in range(here.yo_size):
        for z in range(here.zo_size):
            for x, w in group:
                for part in range(count):
                    target = wholes[part].at[1, here.chip(y=y, x=x, w=w, z=z)]
                    wires.arrive(target, name(1, y, x, z, w, part), other)


ATTENTION_PARTS = 3
EXPERT_PARTS = 2


def greet_experts(here):
    greet(
        [here.at(x=x, w=w) for x, w in offsets_of(GROUP)[1:]]
        + [here.at(z=z) for z in here.z_steps]
        + [here.at(y=y) for y in here.y_steps]
        + [here.at(core=1)]
    )


def greet_attention(here):
    greet(
        [here.at(z=z, w=w) for z, w in here.column if (z, w) != (0, 0)]
        + [here.at(x=1), here.at(core=1)]
        + [here.at(y=y) for y in here.y_steps]
    )


def gather_kernel(sizes, count, *refs):
    ins, outs, sems = refs[:count], refs[count : 2 * count], refs[2 * count :]
    here = Place(sizes)
    cut = ATTENTION_PARTS
    wires = [Wires(*sems[:2])]
    steps = [gather_attention_steps(here, wires[0], ins[:cut], outs[:cut], count == cut)]
    if count > cut:
        greet_layer(here)
        wires.append(Wires(*sems[2:]))
        steps.append(gather_experts_steps(here, wires[1], ins[cut:], outs[cut:]))
    else:
        greet_attention(here)
    together(*steps)
    for one in wires:
        one.drain()


def expert_sems(sizes):
    chips = sizes[0] * sizes[1] * 4
    sends = 3 + 4 * (sizes[0] + sizes[1]) + 4 * sizes[1] * sizes[0] + chips
    return [
        pltpu.SemaphoreType.DMA((EXPERT_PARTS * sends,)),
        pltpu.SemaphoreType.DMA((2 * chips * EXPERT_PARTS,)),
    ]


def gather(identity, attention_shards, expert_parts):
    sizes = mesh_sizes()
    chips = sizes[0] * sizes[1] * 4
    columns = sizes[1] * 2
    sends = ATTENTION_PARTS * ((columns - 1) + chips + columns * (2 * sizes[0] + 1) + chips)
    in_vmem = pl.BlockSpec(memory_space=pltpu.VMEM)
    count = len(attention_shards) + len(expert_parts)
    return pl.pallas_call(
        functools.partial(gather_kernel, sizes, count),
        out_shape=[
            jax.ShapeDtypeStruct((2 * chips,) + shard.shape, shard.dtype)
            for shard in attention_shards
        ]
        + [
            jax.ShapeDtypeStruct((2, chips) + part.shape[1:], part.dtype) for part in expert_parts
        ],
        in_specs=[in_vmem] * count,
        out_specs=[in_vmem] * count,
        scratch_shapes=[
            pltpu.SemaphoreType.DMA((sends,)),
            pltpu.SemaphoreType.DMA((2 * chips * ATTENTION_PARTS,)),
        ]
        + (expert_sems(sizes) if expert_parts else []),
        compiler_params=pltpu.CompilerParams(
            collective_id=identity, has_side_effects=True, vmem_limit_bytes=58 * 1024 * 1024
        ),
    )(*attention_shards, *expert_parts)


def sum_experts_steps(here, wires, whole, outs, first, second, third):
    count = len(whole)
    group = offsets_of(GROUP)
    other = here.at(core=1)
    chips = here.yo_size * here.zo_size * 4

    def place(y, z, member):
        return (y * here.zo_size + z) * 4 + member

    def name(kind, index, part):
        return (kind * chips + index) * count + part

    order = [
        (y, z, member)
        for y in list(here.y_steps) + [0]
        for z in list(here.z_steps) + [0]
        for member in (1, 2, 3, 0)
    ]
    for y, z, member in order:
        x, w = group[member]
        index = here.chip(y=y, x=x, z=z, w=w)
        spot = place(y, z, member)
        for part in range(count):
            wires.send(
                whole[part].at[1, index], first[part].at[spot], name(0, spot, part), other
            )
        if member == 0:
            yield
    for y, z, member in order:
        x, w = group[member]
        index = here.chip(y=y, x=x, z=z, w=w)
        spot = place(y, z, member)
        for part in range(count):
            total = first[part].at[spot]
            wires.arrive(total, name(0, spot, part), other)
            parts = [whole[part].at[0, index]]
            if y:
                add_rows(total, *parts)
                landing = place(here.back_y(y), z, member)
                wires.send(
                    total, second[part].at[landing - 4 * here.zo_size], name(1, landing, part), here.at(y=y)
                )
                continue
            for step in here.y_steps:
                spot_in = place(step, z, member)
                arrived = second[part].at[spot_in - 4 * here.zo_size]
                wires.arrive(arrived, name(1, spot_in, part), other)
                parts.append(arrived)
            if z:
                add_rows(total, *parts)
                landing = here.back_z(z) * 4 + member
                wires.send(
                    total, third[part].at[landing - 4], name(2, landing, part), here.at(z=z)
                )
                continue
            for step in here.z_steps:
                arrived = third[part].at[step * 4 + member - 4]
                wires.arrive(arrived, name(2, step * 4 + member, part), other)
                parts.append(arrived)
            add_rows(total, *parts)
            slot = here.xi * 2 + here.zi
            if member:
                wires.send(total, outs[part].at[slot], name(3, member, part), here.at(x=x, w=w))
            else:
                outs[part][slot] = total[...]
        yield
    for member in range(1, 4):
        x, w = group[member]
        yo, xi, zo, zi, core = here.at(x=x, w=w)
        for part in range(count):
            wires.arrive(outs[part].at[xi * 2 + zi], name(3, member, part), other)


def sum_attention_steps(here, wires, whole, outs, first, second, third, fourth):
    count = len(whole)
    columns = here.column
    other = here.at(core=1)
    width = len(columns)
    chips = here.yo_size * 2 * width

    def place(y, x, column):
        return (y * 2 + x) * width + column

    def name(kind, index, part):
        return (kind * chips + index) * count + part

    rounds = [
        (y, x, (column + 1) % width, part)
        for y, x in [(y, 1) for y in here.y_steps] + [(0, 1)] + [(y, 0) for y in here.y_steps] + [(0, 0)]
        for column in range(width)
        for part in range(count)
    ]
    for y, x, column, part in rounds:
        z, w = columns[column]
        spot = place(y, x, column)
        wires.send(
            whole[part].at[here.chip(y=y, x=x, z=z, w=w), 1 - here.core],
            first[part].at[spot],
            name(0, spot, part),
            other,
        )
        if (column, part) == (0, count - 1):
            yield
    for y, x, column, part in rounds:
        z, w = columns[column]
        spot = place(y, x, column)
        total = first[part].at[spot]
        wires.arrive(total, name(0, spot, part), other)
        parts = [whole[part].at[here.chip(y=y, x=x, z=z, w=w), here.core]]

        def take_in(buffer, kind, index, offset=0):
            arrived = buffer[part].at[index - offset]
            wires.arrive(arrived, name(kind, index, part), other)
            parts.append(arrived)

        def give(buffer, kind, index, device, offset=0):
            add_rows(total, *parts)
            wires.send(total, buffer[part].at[index - offset], name(kind, index, part), device)

        if x:
            give(second, 1, y * width + column, here.at(x=1))
            if part == count - 1:
                yield
            continue
        take_in(second, 1, y * width + column)
        if y:
            give(third, 2, here.back_y(y) * width + column, here.at(y=y), width)
            if part == count - 1:
                yield
            continue
        for step in here.y_steps:
            take_in(third, 2, step * width + column, width)
        if column:
            landing = columns.index((here.back_z(z), w))
            give(fourth, 3, landing, here.at(z=z, w=w), 1)
            if part == count - 1:
                yield
            continue
        for step in range(1, width):
            take_in(fourth, 3, step, 1)
        add_rows(total, *parts)
        outs[part][...] = total[...]


def sum_layer_kernel(sizes, *refs):
    both = ATTENTION_PARTS + EXPERT_PARTS
    cut = ATTENTION_PARTS
    ins, outs, rest = refs[:both], refs[both : 2 * both], refs[2 * both :]
    buffers, sems = rest[:-4], rest[-4:]
    attention = [buffers[level * cut : (level + 1) * cut] for level in range(4)]
    buffers = buffers[4 * cut :]
    experts = [buffers[level * EXPERT_PARTS : (level + 1) * EXPERT_PARTS] for level in range(3)]
    here = Place(sizes)
    wires = Wires(*sems[:2]), Wires(*sems[2:])
    greet_layer(here)
    together(
        sum_experts_steps(here, wires[1], ins[cut:], outs[cut:], *experts),
        sum_attention_steps(here, wires[0], ins[:cut], outs[:cut], *attention),
    )
    for one in wires:
        one.drain()


def sum_layer(attention_grads, expert_grads):
    sizes = mesh_sizes()
    chips = sizes[0] * sizes[1] * 4
    column = sizes[1] * 2
    attention = [grads.reshape(chips, 2, -1, grads.shape[1]) for grads in attention_grads]
    experts = [grads.reshape(2, chips, -1, D) for grads in expert_grads]
    in_vmem = pl.BlockSpec(memory_space=pltpu.VMEM)
    count = ATTENTION_PARTS + EXPERT_PARTS

    def held(blocks, sizes_of):
        return [
            pltpu.VMEM((sizes_of(part),) + block.shape[2:], jnp.bfloat16)
            for part, block in enumerate(blocks)
        ]

    return pl.pallas_call(
        functools.partial(sum_layer_kernel, sizes),
        out_shape=[jax.ShapeDtypeStruct(block.shape[2:], jnp.bfloat16) for block in attention]
        + [jax.ShapeDtypeStruct((4,) + block.shape[2:], jnp.bfloat16) for block in experts],
        in_specs=[in_vmem] * count,
        out_specs=[in_vmem] * count,
        scratch_shapes=held(attention, lambda part: chips)
        + held(attention, lambda part: sizes[0] * column)
        + held(attention, lambda part: (sizes[0] - 1) * column)
        + held(attention, lambda part: column - 1)
        + held(experts, lambda part: chips)
        + held(experts, lambda part: (sizes[0] - 1) * sizes[1] * 4)
        + held(experts, lambda part: (sizes[1] - 1) * 4)
        + [
            pltpu.SemaphoreType.DMA((3 * chips * ATTENTION_PARTS,)),
            pltpu.SemaphoreType.DMA((4 * chips * ATTENTION_PARTS,)),
            pltpu.SemaphoreType.DMA((3 * chips * EXPERT_PARTS,)),
            pltpu.SemaphoreType.DMA((4 * chips * EXPERT_PARTS,)),
        ],
        compiler_params=pltpu.CompilerParams(
            collective_id=5, has_side_effects=True, vmem_limit_bytes=62 * 1024 * 1024
        ),
    )(*attention, *experts)


def swap(value, axis):
    return lax.ppermute(value, axis, [(0, 1), (1, 0)])


def pick(value, index, axis=0):
    return lax.dynamic_index_in_dim(value, index, axis, keepdims=False)


def by_core(mine, theirs, axis):
    core = lax.axis_index("core")
    return jnp.where(
        core == 0, jnp.stack([mine, theirs], axis), jnp.stack([theirs, mine], axis)
    )


def gain_columns(gains):
    gains = gains.astype(jnp.bfloat16).T
    return jnp.pad(gains, ((0, 0), (0, 128 - gains.shape[1])))


def attention_shards(w_qkv, w_out, gains, layer):
    return [
        w_qkv[layer].astype(jnp.bfloat16),
        w_out[layer].astype(jnp.bfloat16),
        gain_columns(gains[layer]),
    ]


def expert_parts(w_gateup, w_down, layer):
    core = lax.axis_index("core")
    parts = []
    for shard in (w_gateup[layer], w_down[layer]):
        shard = shard.reshape((4, 2) + shard.shape[1:])
        theirs = swap(pick(shard, 1 - core, 1).astype(jnp.bfloat16), "core").astype(jnp.float32)
        pair = by_core(pick(shard, core, 1), theirs, 1).reshape(4, -1, D)
        parts.append(pair.astype(jnp.bfloat16))
    return parts


def attention_matrices(qkv, out, gain):
    gain = gain.reshape(D, 128)[:, :2].T.astype(jnp.float32)
    return qkv.reshape(D, QKV), out.reshape(D, D), gain


def expert_matrices(up, down):
    return up.reshape(2, D, 2 * F), down.reshape(2, F, D)


def layer_sums(grad_qkv, grad_out, grad_up, grad_down, grad_gains):
    core = lax.axis_index("core")
    attention = [
        grad_qkv.astype(jnp.bfloat16),
        grad_out.astype(jnp.bfloat16),
        gain_columns(grad_gains),
    ]
    qkv, out, gain, up, down = sum_layer(attention, [grad_up, grad_down])
    result = [qkv, out]
    for part in (up, down):
        part = part.astype(jnp.float32).reshape(4, 2, -1, D)
        theirs = swap(pick(part, 1 - core, 1).astype(jnp.bfloat16), "core").astype(jnp.float32)
        pair = by_core(pick(part, core, 1), theirs, 1)
        result.append(pair.reshape(EXPERTS, -1, D))
    return result + [gain[:, :2].T]


SQRT_HALF = 0.7071067811865476
PDF_SCALE = 0.3989422804014327
TILE = 256
TILES = F // TILE


def selections(table, columns):
    rows = table.shape[1]
    slots = lax.broadcasted_iota(jnp.int32, (CAP, rows), 0).astype(jnp.float32)
    take = (table[0:1, :] == slots).astype(jnp.bfloat16)
    slots = lax.broadcasted_iota(jnp.int32, (rows, CAP), 1).astype(jnp.float32)
    spread = (columns[:, 0:1] == slots).astype(jnp.bfloat16)
    return take, spread, columns[:, 1:2]


def dot(left, right, contract=(1, 0)):
    return lax.dot_general(
        left,
        right,
        (((contract[0],), (contract[1],)), ((), ())),
        preferred_element_type=jnp.float32,
    )


def experts_grads_kernel(slot_in, active, slot_grad, grad_gate, grad_up, up_out, down_out):
    up_out[0, :, :F] = dot(slot_in[0], grad_gate[0], (0, 0)).astype(jnp.bfloat16)
    up_out[0, :, F:] = dot(slot_in[0], grad_up[0], (0, 0)).astype(jnp.bfloat16)
    down_out[0] = dot(active[0], slot_grad[0], (0, 0)).astype(jnp.bfloat16)


def whole_block(shape):
    return pl.BlockSpec(shape, lambda e, f: (0,) * len(shape))


def expert_block(shape):
    return pl.BlockSpec((1,) + shape, lambda e, f: (e,) + (0,) * len(shape))


WAVES = ((0,), (3,), (1, 2))
TURNS = ((0, 2), (1, 1), (2, 2))


def moe_forward_kernel(sizes, background, *refs):
    tokens, tables, columns, up_w, down_w = refs[:5]
    extra = EXPERT_PARTS if background else 0
    shards, refs = refs[5 : 5 + extra], refs[5 + extra :]
    merged, slot_out, gate_out, up_out, active_out = refs[:5]
    wholes, refs = refs[5 : 5 + extra], refs[5 + extra :]
    chunks, leaving, coming, slot_in, result, total = refs[:6]
    sems = refs[6:]
    here = Place(sizes)
    wires = Wires(*sems[:2])
    partners = [here.at(x=x, w=w) for x, w in offsets_of(GROUP)]
    if background:
        greet_experts(here)
        other_wires = Wires(*sems[2:])
        steps = gather_experts_steps(here, other_wires, shards, wholes)
    else:
        greet(partners[1:])
        steps = iter(())
    for place in (3, 1, 2):
        wires.send(tokens, chunks.at[place - 1], place - 1, partners[place])
    next(steps, None)
    for wave, turns in zip(WAVES, TURNS):
        sources = []
        for place in wave:
            source = tokens if place == 0 else chunks.at[place - 1]
            if place:
                wires.arrive(source, place - 1, partners[place])
            sources.append(source)
        count = CAP * len(wave)
        rows = pl.ds(wave[0] * CAP, count)
        for expert in range(2):
            picks = [selections(tables[place, expert], columns[place, expert]) for place in wave]
            for index, source in enumerate(sources):
                chosen = dot(picks[index][0], source[...]).astype(jnp.bfloat16)
                slot_in[index * CAP : (index + 1) * CAP] = chosen
            slot_out[expert, rows, :] = slot_in[:count]

            def step(tile, carry, expert=expert, count=count, rows=rows):
                at_gate = pl.ds(pl.multiple_of(tile * TILE, TILE), TILE)
                at_up = pl.ds(pl.multiple_of(F + tile * TILE, TILE), TILE)
                gate = dot(slot_in[:count], up_w[expert, :, at_gate])
                up = dot(slot_in[:count], up_w[expert, :, at_up])
                active = (0.5 * gate * (1.0 + lax.erf(gate * SQRT_HALF)) * up).astype(jnp.bfloat16)
                gate_out[expert, rows, at_gate] = gate.astype(jnp.bfloat16)
                up_out[expert, rows, at_gate] = up.astype(jnp.bfloat16)
                active_out[expert, rows, at_gate] = active
                return carry

            lax.fori_loop(0, TILES, step, 0)

            def finish(tile, carry, expert=expert, count=count, rows=rows):
                lanes = pl.ds(pl.multiple_of(tile * 2 * TILE, TILE), 2 * TILE)
                result[:count, lanes] = dot(
                    active_out[expert, rows, :], down_w[expert, :, lanes]
                ).astype(jnp.bfloat16)
                return carry

            lax.fori_loop(0, D // (2 * TILE), finish, 0)
            for index in range(len(wave)):
                take, spread, gates = picks[index]
                share = dot(spread, result[index * CAP : (index + 1) * CAP]) * gates
                if expert == 0:
                    total[index] = share
                else:
                    total[index] += share
            for turn in range(turns[expert]):
                next(steps, None)
        for index, place in enumerate(wave):
            if place == 0:
                merged[...] = total[index]
            else:
                leaving[place - 1] = total[index].astype(jnp.bfloat16)
                wires.send(
                    leaving.at[place - 1], coming.at[place - 1], place + 2, partners[place]
                )
    for one in steps:
        pass
    for place in range(1, 4):
        wires.arrive(coming.at[place - 1], place + 2, partners[place])
        merged[...] += coming[place - 1].astype(jnp.float32)
    wires.drain()
    if background:
        other_wires.drain()


def moe_backward_kernel(sizes, background, *refs):
    gradient, tables, columns, up_w, down_w, gate_in, up_in = refs[:7]
    merged, slot_out, gate_out, up_out = refs[7:11]
    chunks, leaving, coming, slot_grad, slots, total = refs[11:17]
    here = Place(sizes)
    wires = Wires(*refs[17:])
    partners = [here.at(x=x, w=w) for x, w in offsets_of(GROUP)]
    greet(partners[1:])
    leaving[3] = gradient[...].astype(jnp.bfloat16)
    for place in (3, 1, 2):
        wires.send(leaving.at[3], chunks.at[place - 1], place - 1, partners[place])
    for wave in WAVES:
        sources = []
        for place in wave:
            source = gradient if place == 0 else chunks.at[place - 1]
            if place:
                wires.arrive(source, place - 1, partners[place])
            sources.append(source)
        count = CAP * len(wave)
        rows = pl.ds(wave[0] * CAP, count)
        for expert in range(2):
            picks = [selections(tables[place, expert], columns[place, expert]) for place in wave]
            for index, source in enumerate(sources):
                take, spread, gates = picks[index]
                weighted = (gates * source[...].astype(jnp.float32)).astype(jnp.bfloat16)
                slot_grad[index * CAP : (index + 1) * CAP] = dot(take, weighted).astype(jnp.bfloat16)
            slot_out[expert, rows, :] = slot_grad[:count]

            def step(tile, carry, expert=expert, count=count, rows=rows):
                at_gate = pl.ds(pl.multiple_of(tile * TILE, TILE), TILE)
                grad_act = dot(slot_grad[:count], down_w[expert, at_gate, :], (1, 1))
                gate = gate_in[expert, rows, at_gate].astype(jnp.float32)
                up = up_in[expert, rows, at_gate].astype(jnp.float32)
                below = 0.5 * (1.0 + lax.erf(gate * SQRT_HALF))
                slope = below + gate * PDF_SCALE * jnp.exp(-0.5 * gate * gate)
                gate_out[expert, rows, at_gate] = (grad_act * up * slope).astype(jnp.bfloat16)
                up_out[expert, rows, at_gate] = (grad_act * gate * below).astype(jnp.bfloat16)
                return carry

            lax.fori_loop(0, TILES, step, 0)

            def finish(tile, carry, expert=expert, count=count, rows=rows):
                lanes = pl.ds(pl.multiple_of(tile * 2 * TILE, TILE), 2 * TILE)
                part = dot(gate_out[expert, rows, :], up_w[expert, lanes, :F], (1, 1))
                part = part + dot(up_out[expert, rows, :], up_w[expert, lanes, F:], (1, 1))
                slots[:count, lanes] = part.astype(jnp.bfloat16)
                return carry

            lax.fori_loop(0, D // (2 * TILE), finish, 0)
            for index in range(len(wave)):
                share = dot(picks[index][1], slots[index * CAP : (index + 1) * CAP])
                if expert == 0:
                    total[index] = share
                else:
                    total[index] += share
        for index, place in enumerate(wave):
            if place == 0:
                merged[...] = total[index]
            else:
                leaving[place - 1] = total[index].astype(jnp.bfloat16)
                wires.send(
                    leaving.at[place - 1], coming.at[place - 1], place + 2, partners[place]
                )
    for place in range(1, 4):
        wires.arrive(coming.at[place - 1], place + 2, partners[place])
        merged[...] += coming[place - 1].astype(jnp.float32)
    wires.drain()


def moe_call(kernel, identity, rows_in, tables, weights, extra, kinds, background=()):
    rows = rows_in.shape[0]
    slots = 4 * CAP
    sizes = mesh_sizes()
    chips = sizes[0] * sizes[1] * 4
    operands = [rows_in, tables, jnp.swapaxes(tables, 2, 3), *weights, *extra, *background]
    in_vmem = pl.BlockSpec(memory_space=pltpu.VMEM)
    more_sems = expert_sems(sizes) if background else []
    return pl.pallas_call(
        functools.partial(kernel, sizes, bool(background)),
        in_specs=[in_vmem] * len(operands),
        out_specs=[in_vmem] * (1 + len(kinds) + len(background)),
        out_shape=[jax.ShapeDtypeStruct((rows, D), jnp.float32)]
        + [jax.ShapeDtypeStruct((2, slots, width), jnp.bfloat16) for width in kinds]
        + [jax.ShapeDtypeStruct((2, chips) + part.shape[1:], part.dtype) for part in background],
        scratch_shapes=[
            pltpu.VMEM((3, rows, D), jnp.bfloat16),
            pltpu.VMEM((4, rows, D), jnp.bfloat16),
            pltpu.VMEM((3, rows, D), jnp.bfloat16),
            pltpu.VMEM((2 * CAP, D), jnp.bfloat16),
            pltpu.VMEM((2 * CAP, D), jnp.bfloat16),
            pltpu.VMEM((2, rows, D), jnp.float32),
            pltpu.SemaphoreType.DMA((6,)),
            pltpu.SemaphoreType.DMA((6,)),
        ]
        + more_sems,
        compiler_params=pltpu.CompilerParams(
            collective_id=identity, has_side_effects=True, vmem_limit_bytes=62 * 1024 * 1024
        ),
        cost_estimate=pl.CostEstimate(
            flops=48 * CAP * D * F, bytes_accessed=40_000_000, transcendentals=8 * CAP * F
        ),
    )(*operands)


def moe_forward(expert_in, tables, weights, background):
    merged, *kept = moe_call(
        moe_forward_kernel,
        2 if background else 3,
        expert_in,
        tables,
        weights,
        [],
        (D, F, F, F),
        background,
    )
    return merged, kept[:4], expert_matrices(*kept[4:]) if background else None


def moe_backward(gradient, tables, weights, kept):
    slot_in, gate, up, active = kept
    total, slot_grad, grad_gate, grad_up = moe_call(
        moe_backward_kernel, 4, gradient, tables, weights, [gate, up], (D, F, F)
    )
    slots = slot_in.shape[1]

    def columns_of(width):
        return pl.BlockSpec((1, slots, width), lambda e, i: (e, 0, i))

    grads = pl.pallas_call(
        experts_grads_kernel,
        grid=(2, 3),
        in_specs=[
            columns_of(D // 3),
            columns_of(F // 3),
            expert_block((slots, D)),
            expert_block((slots, F)),
            expert_block((slots, F)),
        ],
        out_specs=[
            pl.BlockSpec((1, D // 3, 2 * F), lambda e, i: (e, i, 0)),
            pl.BlockSpec((1, F // 3, D), lambda e, i: (e, i, 0)),
        ],
        out_shape=[
            jax.ShapeDtypeStruct((2, D, 2 * F), jnp.bfloat16),
            jax.ShapeDtypeStruct((2, F, D), jnp.bfloat16),
        ],
        compiler_params=pltpu.CompilerParams(vmem_limit_bytes=48 * 1024 * 1024),
        cost_estimate=pl.CostEstimate(
            flops=12 * slots * D * F, bytes_accessed=30_000_000, transcendentals=0
        ),
    )(slot_in, active, slot_grad, grad_gate, grad_up)
    return total, grads[0], grads[1]


def turned(vectors, cosine, sine):
    return vectors * cosine + pltpu.roll(vectors, HD // 2, 1) * sine


def project_kernel(stream, gain, weight, cosine, sine, normed, heads):
    tile = pl.program_id(0)

    @pl.when(tile == 0)
    def _():
        values = stream[...]
        scale = lax.rsqrt(jnp.mean(values * values, axis=-1, keepdims=True) + NORM_EPS)
        normed[...] = (values * scale * gain[...]).astype(jnp.bfloat16)

    result = dot(normed[...], weight[...])
    rotated = (H + KVH) // 2

    @pl.when(tile < rotated)
    def _():
        for head in range(2):
            lanes = slice(head * HD, (head + 1) * HD)
            heads[:, lanes] = turned(result[:, lanes], cosine[...], sine[...]).astype(jnp.bfloat16)

    @pl.when(tile >= rotated)
    def _():
        heads[...] = result.astype(jnp.bfloat16)


def project(stream, gain, weight, cosine, sine):
    rows, width = stream.shape[0], 2 * HD

    def same(shape):
        return pl.BlockSpec(shape, lambda tile: (0, 0))

    return pl.pallas_call(
        project_kernel,
        grid=(QKV // width,),
        in_specs=[
            same((rows, D)),
            same((1, D)),
            pl.BlockSpec((D, width), lambda tile: (0, tile)),
            same((rows, HD)),
            same((rows, HD)),
        ],
        out_specs=[
            same((rows, D)),
            pl.BlockSpec((rows, width), lambda tile: (0, tile)),
        ],
        out_shape=[
            jax.ShapeDtypeStruct((rows, D), jnp.bfloat16),
            jax.ShapeDtypeStruct((rows, QKV), jnp.bfloat16),
        ],
        compiler_params=pltpu.CompilerParams(vmem_limit_bytes=60 * 1024 * 1024),
        cost_estimate=pl.CostEstimate(
            flops=2 * rows * D * QKV, bytes_accessed=12_000_000, transcendentals=rows
        ),
    )(stream, gain[None], weight, cosine, sine)


def head_columns(rows, offset):
    return pl.BlockSpec((rows, HD), lambda head: (0, offset + head // (H // KVH)))


def attention_kernel(*refs):
    query, allowed = refs[:2]
    attended, total = refs[-3:-1]
    scores = refs[-1]
    count = (len(refs) - 5) // 2
    keys, values = refs[2 : 2 + count], refs[2 + count : 2 + 2 * count]
    rows = query.shape[0]
    for index, key in enumerate(keys):
        lanes = slice(index * rows, (index + 1) * rows)
        part = dot(query[...], key[...], (1, 1)) * HD ** (-0.5)
        scores[:, lanes] = jnp.where(allowed[:, lanes] > 0, part, MASKED)
    row_max = jnp.max(scores[...], axis=-1, keepdims=True)
    exponent = jnp.exp(scores[...] - row_max)
    row_total = jnp.sum(exponent, axis=-1, keepdims=True)
    probabilities = (exponent / row_total).astype(jnp.bfloat16)
    result = None
    for index, value in enumerate(values):
        part = dot(probabilities[:, index * rows : (index + 1) * rows], value[...])
        result = part if result is None else result + part
    attended[...] = result.astype(jnp.bfloat16)
    total[0] = jnp.broadcast_to(row_max + jnp.log(row_total), total.shape[1:])


def attention_forward(heads, blocks, allowed):
    rows, count = heads.shape[0], len(blocks)
    one = pl.BlockSpec((rows, HD), lambda head: (0, head))
    return pl.pallas_call(
        attention_kernel,
        grid=(H,),
        in_specs=[one, pl.BlockSpec(allowed.shape, lambda head: (0, 0))]
        + [head_columns(rows, 0)] * count
        + [head_columns(rows, KVH)] * count,
        out_specs=[one, pl.BlockSpec((1, rows, HD), lambda head: (head, 0, 0))],
        out_shape=[
            jax.ShapeDtypeStruct((rows, H * HD), jnp.bfloat16),
            jax.ShapeDtypeStruct((H, rows, HD), jnp.float32),
        ],
        scratch_shapes=[pltpu.VMEM((rows, rows * count), jnp.float32)],
        compiler_params=pltpu.CompilerParams(vmem_limit_bytes=60 * 1024 * 1024),
        cost_estimate=pl.CostEstimate(
            flops=4 * H * HD * rows * rows * count,
            bytes_accessed=8_000_000,
            transcendentals=H * rows * rows * count,
        ),
    )(heads, allowed, *blocks, *blocks)


def attention_backward_kernel(*refs):
    query, allowed, gradient, total, cosine, sine = refs[:6]
    turned_back, blocks_out, probabilities, grads, key_sum, value_sum = refs[-6:]
    count = (len(refs) - 12) // 2
    keys, values = refs[6 : 6 + count], refs[6 + count : 6 + 2 * count]
    rows = query.shape[0]
    head, group = pl.program_id(0), H // KVH
    scale = HD ** (-0.5)
    inner = jnp.zeros((rows, 1), jnp.float32)
    for index in range(count):
        lanes = slice(index * rows, (index + 1) * rows)
        part = dot(query[...], keys[index][...], (1, 1)) * scale
        part = jnp.where(allowed[:, lanes] > 0, jnp.exp(part - total[0, :, :1]), 0.0)
        slope = dot(gradient[...], values[index][...], (1, 1))
        probabilities[:, lanes] = part
        grads[:, lanes] = slope
        inner = inner + jnp.sum(part * slope, axis=-1, keepdims=True)
    back = None
    for index in range(count):
        lanes = slice(index * rows, (index + 1) * rows)
        part = probabilities[:, lanes]
        grad_scores = (part * (grads[:, lanes] - inner)).astype(jnp.bfloat16)
        share = dot(grad_scores, keys[index][...])
        back = share if back is None else back + share
        key_part = dot(grad_scores, query[...], (0, 0)) * scale
        value_part = dot(part.astype(jnp.bfloat16), gradient[...], (0, 0))

        @pl.when(lax.rem(head, group) == 0)
        def _(index=index, key_part=key_part, value_part=value_part):
            key_sum[index] = key_part
            value_sum[index] = value_part

        @pl.when(lax.rem(head, group) > 0)
        def _(index=index, key_part=key_part, value_part=value_part):
            key_sum[index] += key_part
            value_sum[index] += value_part

    turned_back[...] = turned(back * scale, cosine[...], -sine[...]).astype(jnp.bfloat16)
    for place in range(KVH):

        @pl.when(head == (place + 1) * group - 1)
        def _(place=place):
            for index in range(count):
                blocks_out[index, :, place * HD : (place + 1) * HD] = key_sum[index].astype(
                    jnp.bfloat16
                )
                blocks_out[index, :, (KVH + place) * HD : (KVH + place + 1) * HD] = value_sum[
                    index
                ].astype(jnp.bfloat16)


def attention_backward(heads, blocks, allowed, totals, gradient, cosine, sine):
    rows, count = heads.shape[0], len(blocks)
    one = pl.BlockSpec((rows, HD), lambda head: (0, head))
    table = pl.BlockSpec((rows, HD), lambda head: (0, 0))
    width = 2 * KVH * HD
    return pl.pallas_call(
        attention_backward_kernel,
        grid=(H,),
        in_specs=[
            one,
            pl.BlockSpec(allowed.shape, lambda head: (0, 0)),
            one,
            pl.BlockSpec((1, rows, HD), lambda head: (head, 0, 0)),
            table,
            table,
        ]
        + [head_columns(rows, 0)] * count
        + [head_columns(rows, KVH)] * count,
        out_specs=[one, pl.BlockSpec((count, rows, width), lambda head: (0, 0, 0))],
        out_shape=[
            jax.ShapeDtypeStruct((rows, QKV), jnp.bfloat16),
            jax.ShapeDtypeStruct((count, rows, width), jnp.bfloat16),
        ],
        scratch_shapes=[
            pltpu.VMEM((rows, rows * count), jnp.float32),
            pltpu.VMEM((rows, rows * count), jnp.float32),
            pltpu.VMEM((count, rows, HD), jnp.float32),
            pltpu.VMEM((count, rows, HD), jnp.float32),
        ],
        compiler_params=pltpu.CompilerParams(vmem_limit_bytes=60 * 1024 * 1024),
        cost_estimate=pl.CostEstimate(
            flops=10 * H * HD * rows * rows * count,
            bytes_accessed=10_000_000,
            transcendentals=H * rows * rows * count,
        ),
    )(heads, allowed, gradient, totals, cosine, sine, *blocks, *blocks)


def finish_keys_kernel(*refs):
    parts, (cosine, sine, unused, out) = refs[:-4], refs[-4:]
    for place in range(2 * KVH):
        lanes = slice(place * HD, (place + 1) * HD)
        total = parts[0][:, lanes].astype(jnp.float32)
        for part in parts[1:]:
            total = total + part[:, lanes].astype(jnp.float32)
        if place < KVH:
            total = turned(total, cosine[...], -sine[...])
        out[:, lanes] = total.astype(jnp.bfloat16)


def finish_keys(parts, cosine, sine, projected):
    rows, width = parts[0].shape
    return pl.pallas_call(
        finish_keys_kernel,
        grid=(1,),
        in_specs=[pl.BlockSpec((rows, width), lambda step: (0, 0))] * len(parts)
        + [pl.BlockSpec((rows, HD), lambda step: (0, 0))] * 2
        + [pl.BlockSpec(memory_space=pl.ANY)],
        out_specs=pl.BlockSpec((rows, width), lambda step: (0, QKV // width - 1)),
        out_shape=jax.ShapeDtypeStruct(projected.shape, projected.dtype),
        input_output_aliases={len(parts) + 2: 0},
        compiler_params=pltpu.CompilerParams(vmem_limit_bytes=60 * 1024 * 1024),
        cost_estimate=pl.CostEstimate(flops=0, bytes_accessed=2_000_000, transcendentals=0),
    )(*parts, cosine, sine, projected)


def weight_grad_kernel(rows_in, grads, out):
    out[...] = dot(rows_in[...], grads[...], (0, 0)).astype(jnp.bfloat16)


def weight_grad(rows_in, grads):
    rows, width = grads.shape
    tile = D // 3
    return pl.pallas_call(
        weight_grad_kernel,
        grid=(3,),
        in_specs=[
            pl.BlockSpec((rows, tile), lambda step: (0, step)),
            pl.BlockSpec((rows, width), lambda step: (0, 0)),
        ],
        out_specs=pl.BlockSpec((tile, width), lambda step: (step, 0)),
        out_shape=jax.ShapeDtypeStruct((D, width), jnp.bfloat16),
        compiler_params=pltpu.CompilerParams(vmem_limit_bytes=60 * 1024 * 1024),
        cost_estimate=pl.CostEstimate(
            flops=2 * rows * D * width, bytes_accessed=2 * D * width, transcendentals=0
        ),
    )(rows_in, grads)


def rotate_back(gradient, cosine_table, sine_table):
    half_width = gradient.shape[-1] // 2
    first_half = gradient[..., :half_width]
    second_half = gradient[..., half_width:]
    return jnp.concatenate(
        [
            first_half * cosine_table + second_half * sine_table,
            second_half * cosine_table - first_half * sine_table,
        ],
        axis=-1,
    )


def plain_backward(queries, keys_all, values_all, allowed, totals, grad_attended):
    group_size = H // KVH
    score_scale = HD ** (-0.5)
    grad_queries = []
    grad_keys = []
    grad_values = []
    for head_group in range(KVH):
        query_part = queries[:, head_group * group_size : (head_group + 1) * group_size, :]
        grad_part = grad_attended[:, head_group * group_size : (head_group + 1) * group_size, :]
        keys_part = keys_all[:, head_group, :]
        scores = (
            jnp.einsum("tjd,kd->jtk", query_part, keys_part, preferred_element_type=jnp.float32)
            * score_scale
        )
        probabilities = jnp.where(allowed[None], jnp.exp(scores - totals[head_group]), 0.0)
        grad_probs = jnp.einsum(
            "tjd,kd->jtk",
            grad_part,
            values_all[:, head_group, :],
            preferred_element_type=jnp.float32,
        )
        grad_scores = probabilities * (
            grad_probs - jnp.sum(probabilities * grad_probs, axis=-1, keepdims=True)
        )
        grad_scores = grad_scores.astype(jnp.bfloat16)
        grad_queries.append(
            jnp.einsum("jtk,kd->tjd", grad_scores, keys_part, preferred_element_type=jnp.float32)
            * score_scale
        )
        grad_keys.append(
            jnp.einsum("jtk,tjd->kd", grad_scores, query_part, preferred_element_type=jnp.float32)
            * score_scale
        )
        grad_values.append(
            jnp.einsum(
                "jtk,tjd->kd",
                probabilities.astype(jnp.bfloat16),
                grad_part,
                preferred_element_type=jnp.float32,
            )
        )
    return (
        jnp.concatenate(grad_queries, axis=1),
        jnp.stack(grad_keys, axis=1),
        jnp.stack(grad_values, axis=1),
    )


def layer_forward(stream, attn_w, expert_w, ahead, tables, allowed, cosine_table, sine_table):
    qkv_w, out_w, gain_full = attn_w
    attn_in, heads = project(stream, gain_full[0], qkv_w, cosine_table, sine_table)
    own = heads[:, H * HD :]
    blocks = [send(own, CTX, offsets) for offsets in offsets_of(CTX)]
    attended, totals = attention_forward(heads, blocks, allowed)
    middle_stream = stream + jnp.dot(attended, out_w, preferred_element_type=jnp.float32)
    normed_two, scale_two = normalize(middle_stream, gain_full[1])
    expert_in = normed_two.astype(jnp.bfloat16)
    merged, kept, gathered = moe_forward(expert_in, tables, expert_w, ahead)
    record = {
        "stream": stream,
        "attn_in": attn_in,
        "heads": heads,
        "blocks": blocks,
        "totals": totals,
        "attended": attended,
        "middle": middle_stream,
        "scale_two": scale_two,
        "kept": kept,
    }
    return (record, middle_stream + merged, gathered)


def layer_backward(gradient, record, attn_w, expert_w, tables, allowed, cosine_table, sine_table):
    qkv_w, out_w, gain_full = attn_w
    grad_normed, grad_up, grad_down = moe_backward(gradient, tables, expert_w, record["kept"])
    grad_in_two, grad_gain_two = normalize_back(
        grad_normed, record["middle"], record["scale_two"], gain_full[1]
    )
    grad_middle = gradient + grad_in_two
    grad_middle_low = grad_middle.astype(jnp.bfloat16)
    grad_out = weight_grad(record["attended"], grad_middle_low)
    grad_attended = jnp.dot(grad_middle_low, out_w.T, preferred_element_type=jnp.float32)
    keys_all = jnp.concatenate(record["blocks"], axis=0).reshape(-1, 2 * KVH, HD)
    totals = record["totals"][:, :, :1].reshape(KVH, H // KVH, -1, 1)
    row_count = gradient.shape[0]
    grad_queries, grad_keys_all, grad_values_all = plain_backward(
        record["heads"][:, : H * HD].reshape(-1, H, HD),
        keys_all[:, :KVH],
        keys_all[:, KVH:],
        allowed > 0,
        [totals[0], totals[1]],
        grad_attended.astype(jnp.bfloat16).reshape(-1, H, HD),
    )
    both_all = jnp.concatenate([grad_keys_all, grad_values_all], axis=1)
    both = None
    for place, offsets in enumerate(offsets_of(CTX)):
        part = both_all[place * row_count : (place + 1) * row_count]
        if offsets != (0, 0):
            part = send(part.astype(jnp.bfloat16), CTX, offsets, back=True).astype(jnp.float32)
        both = part if both is None else both + part
    grad_keys, grad_values = both[:, :KVH], both[:, KVH:]
    ct, st = cosine_table[:, None, : HD // 2], sine_table[:, None, HD // 2 :]
    grad_projected = jnp.concatenate(
        [
            rotate_back(grad_queries, ct, st).reshape(row_count, H * HD),
            rotate_back(grad_keys, ct, st).reshape(row_count, KVH * HD),
            grad_values.reshape(row_count, KVH * HD),
        ],
        axis=1,
    ).astype(jnp.bfloat16)
    grad_qkv = weight_grad(record["attn_in"], grad_projected)
    grad_normed_one = jnp.dot(grad_projected, qkv_w.T, preferred_element_type=jnp.float32)
    unused, scale_one = normalize(record["stream"], gain_full[0])
    grad_in_one, grad_gain_one = normalize_back(
        grad_normed_one, record["stream"], scale_one, gain_full[0]
    )
    grad_gains = jnp.stack([grad_gain_one, grad_gain_two])
    return (grad_middle + grad_in_one, (grad_qkv, grad_out, grad_up, grad_down, grad_gains))


def on_device(
    tokens,
    cotangent,
    routes,
    gate_weights,
    lengths,
    block_map,
    w_qkv,
    w_out,
    w_gateup,
    w_down,
    gains,
    m_qkv,
    v_qkv,
    m_out,
    v_out,
    m_gateup,
    v_gateup,
    m_down,
    v_down,
    m_gains,
    v_gains,
):
    row_count = tokens.shape[1]
    block_rows = row_count // 2
    own_pos, own_doc = positions_docs(block_map, lengths[0], flat_index(CTX), block_rows)
    places = [
        positions_docs(block_map, lengths[0], source_index(CTX, offsets), block_rows)
        for offsets in offsets_of(CTX)
    ]
    key_pos = jnp.concatenate([place[0] for place in places])
    key_doc = jnp.concatenate([place[1] for place in places])
    allowed = (own_doc[:, None] == key_doc[None, :]) & (key_pos[None, :] <= own_pos[:, None])
    allowed = allowed.astype(jnp.float32)
    cosine_table, sine_table = rope_tables(own_pos)
    own_tables = jnp.stack(
        [dispatch_tables(routes[layer, 0], gate_weights[layer, 0]) for layer in range(LAYERS)]
    )
    core = lax.axis_index("core")
    group_tables = []
    for offsets in offsets_of(GROUP):
        theirs = lax.dynamic_slice_in_dim(own_tables, 2 * target_index(GROUP, offsets), 2, axis=1)
        theirs = jnp.where(core == 0, theirs, theirs[:, ::-1])
        group_tables.append(send(theirs, GROUP, offsets))
    group_tables = jnp.stack(group_tables, axis=1)
    stream = tokens[0].astype(jnp.float32)
    records = []
    shards = [attention_shards(w_qkv, w_out, gains, layer) for layer in range(LAYERS)]
    parts = [expert_parts(w_gateup, w_down, layer) for layer in range(LAYERS)]
    first = gather(0, shards[0], [])
    parts[0], first = lax.optimization_barrier((parts[0], first))
    second = gather(1, shards[1], parts[0])
    cut = ATTENTION_PARTS
    attn_w = [attention_matrices(*first), attention_matrices(*second[:cut])]
    expert_w = [expert_matrices(*second[cut:]), None]
    for layer_index in range(LAYERS):
        ahead = [] if layer_index else parts[1]
        record, stream, gathered = layer_forward(
            stream,
            attn_w[layer_index],
            expert_w[layer_index],
            ahead,
            group_tables[layer_index],
            allowed,
            cosine_table,
            sine_table,
        )
        records.append(record)
        if ahead:
            expert_w[1] = gathered
    output = stream.astype(jnp.bfloat16)[None]
    gradient = cotangent[0].astype(jnp.float32)
    rates = (D ** (-0.5), 0.5, D ** (-0.5), (F // 8) ** (-0.5), 1.0)
    decays = (DECAY, DECAY, DECAY, DECAY, 0.0)
    params = (w_qkv, w_out, w_gateup, w_down, gains)
    firsts = (m_qkv, m_out, m_gateup, m_down, m_gains)
    seconds = (v_qkv, v_out, v_gateup, v_down, v_gains)
    sums = [None] * LAYERS
    for layer_index in reversed(range(LAYERS)):
        gradient, layer_grads = layer_backward(
            gradient,
            records[layer_index],
            attn_w[layer_index],
            expert_w[layer_index],
            group_tables[layer_index],
            allowed,
            cosine_table,
            sine_table,
        )
        sums[layer_index] = layer_sums(*layer_grads)
    updated = []
    for which in range(5):
        total = jnp.stack([sums[layer][which] for layer in range(LAYERS)]).astype(jnp.float32)
        updated.extend(
            adamw(
                params[which], firsts[which], seconds[which], total, rates[which], decays[which]
            )
        )
    return (output, gradient[None], *updated)


def solution(mesh):
    ctx_size, shard_size = mesh.shape["ctx"], mesh.shape["shard"]
    fine = Mesh(mesh.devices.reshape(ctx_size // 2, 2, shard_size // 4, 2, 2), ALL)
    tokens = P(SHARD, CTX, None)
    routed = P(None, SHARD, CTX, None)
    rows_two = P(None, ALL, None)
    rows_three = P(None, None, ALL, None)
    gain = P(None, None, ALL)
    weights = (rows_two, rows_two, rows_three, rows_three, gain)
    states = tuple(spec for spec in weights for which in range(2))
    return jax.shard_map(
        on_device,
        mesh=fine,
        in_specs=(tokens, tokens, routed, routed, P(SHARD, None), P()) + weights + states,
        out_specs=(tokens, tokens) + tuple(spec for spec in weights for which in range(3)),
        check_vma=False,
    )
```

```python
import functools

import jax
import jax.numpy as jnp
from jax import lax
from jax.experimental import pallas as pl
from jax.experimental.pallas import tpu as pltpu
from jax.sharding import Mesh
from jax.sharding import PartitionSpec as P

D = 1536
H = 12
KVH = 2
HD = 128
F = 768
TOP = 4
EXPERTS = 8
LAYERS = 2
STEP = 10
CAP = 160


NORM_EPS = 1e-06
ROPE_BASE = 1000000.0
BETA_ONE = 0.9
BETA_TWO = 0.95
ADAM_EPS = 1e-08
DECAY = 0.1
MASKED = -1e30


def rope_tables(positions):
    half_width = HD // 2
    frequency = ROPE_BASE ** (-(jnp.arange(half_width, dtype=jnp.float32) * 2.0 / HD))
    angles = positions.astype(jnp.float32)[:, None] * frequency[None, :]
    cosine, sine = jnp.cos(angles), jnp.sin(angles)
    return jnp.concatenate([cosine, cosine], axis=1), jnp.concatenate([-sine, sine], axis=1)


def normalize(values, gain_row):
    row_scale = lax.rsqrt(jnp.mean(values * values, axis=-1, keepdims=True) + NORM_EPS)
    return (values * row_scale * gain_row, row_scale)


def normalize_back(gradient, values, row_scale, gain_row):
    unit_rows = values * row_scale
    inner_grad = gradient * gain_row
    input_grad = row_scale * (
        inner_grad - unit_rows * jnp.mean(inner_grad * unit_rows, axis=-1, keepdims=True)
    )
    return (input_grad, jnp.sum(gradient * unit_rows, axis=0))


def adamw(parameter, moment, second, gradient, step_rate, decay_rate):
    moment = BETA_ONE * moment + (1.0 - BETA_ONE) * gradient
    second = BETA_TWO * second + (1.0 - BETA_TWO) * gradient * gradient
    direction = (
        moment / (1.0 - BETA_ONE**STEP) / (jnp.sqrt(second / (1.0 - BETA_TWO**STEP)) + ADAM_EPS)
    )
    return (parameter - step_rate * (direction + decay_rate * parameter), moment, second)


CTX = ("yo", "xi")
SHARD = ("zo", "zi", "core")
ALL = CTX + SHARD
GROUP = ("xi", "zi")
REPLICAS = ("yo", "zo", "core")


def flat_index(axes):
    index = 0
    for axis in axes:
        index = index * lax.axis_size(axis) + lax.axis_index(axis)
    return index


def shift_permutation(axes, offsets, back=False):
    sizes = [lax.axis_size(axis) for axis in axes]
    pairs = []
    for first in range(sizes[0]):
        for second in range(sizes[1]):
            target = ((first + offsets[0]) % sizes[0], (second + offsets[1]) % sizes[1])
            here = first * sizes[1] + second
            there = target[0] * sizes[1] + target[1]
            pairs.append((there, here) if back else (here, there))
    return pairs


def offsets_of(axes):
    sizes = [lax.axis_size(axis) for axis in axes]
    return [(a, b) for a in range(sizes[0]) for b in range(sizes[1])]


def send(value, axes, offsets, back=False):
    if offsets == (0, 0):
        return value
    return lax.ppermute(value, axes, shift_permutation(axes, offsets, back))


def source_index(axes, offsets):
    sizes = [lax.axis_size(axis) for axis in axes]
    return lax.rem(lax.axis_index(axes[0]) - offsets[0] + sizes[0], sizes[0]) * sizes[1] + lax.rem(
        lax.axis_index(axes[1]) - offsets[1] + sizes[1], sizes[1]
    )


def target_index(axes, offsets):
    sizes = [lax.axis_size(axis) for axis in axes]
    return lax.rem(lax.axis_index(axes[0]) + offsets[0], sizes[0]) * sizes[1] + lax.rem(
        lax.axis_index(axes[1]) + offsets[1], sizes[1]
    )


def positions_docs(block_map, lengths_row, ctx_index, block_rows):
    blocks = lax.dynamic_slice_in_dim(block_map, 2 * ctx_index, 2)
    offsets = jnp.arange(block_rows, dtype=jnp.int32)
    positions = (blocks[:, None] * block_rows + offsets[None, :]).reshape(-1)
    bounds = jnp.cumsum(lengths_row)
    documents = jnp.sum((positions[:, None] >= bounds[None, :]).astype(jnp.int32), axis=1)
    return (positions, documents)


def dispatch_tables(routes, gates):
    rows = routes.shape[0]
    hits = (routes[None] == jnp.arange(EXPERTS, dtype=jnp.int32)[:, None, None]).astype(jnp.float32)
    member = jnp.sum(hits, axis=-1)
    gate = jnp.sum(hits * gates[None], axis=-1)
    before = (jnp.arange(rows)[:, None] < jnp.arange(rows)[None, :]).astype(jnp.float32)
    rank = jnp.dot(member, before, preferred_element_type=jnp.float32)
    return jnp.stack([jnp.where(member > 0, rank, -1.0), gate], axis=1)


MESH = pl.DeviceIdType.MESH
QKV = (H + 2 * KVH) * HD


class Place:
    def __init__(self, sizes):
        self.yo_size, self.zo_size = sizes
        self.yo, self.xi, self.zo, self.zi, self.core = [lax.axis_index(axis) for axis in ALL]
        self.y_steps = range(1, self.yo_size)
        self.z_steps = range(1, self.zo_size)
        self.column = [(a, b) for a in range(self.zo_size) for b in range(2)]

    def at(self, y=0, x=0, z=0, w=0, core=0):
        return (
            lax.rem(self.yo + y, self.yo_size),
            1 - self.xi if x else self.xi,
            lax.rem(self.zo + z, self.zo_size),
            1 - self.zi if w else self.zi,
            1 - self.core if core else self.core,
        )

    def chip(self, y=0, x=0, z=0, w=0):
        yo, xi, zo, zi, core = self.at(y, x, z, w)
        return ((yo * 2 + xi) * self.zo_size + zo) * 2 + zi

    def back_y(self, y):
        return (self.yo_size - y) % self.yo_size

    def back_z(self, z):
        return (self.zo_size - z) % self.zo_size


class Wires:
    def __init__(self, send_sems, recv_sems):
        self.send_sems, self.recv_sems = send_sems, recv_sems
        self.started = []

    def send(self, source, target, name, device):
        copy = pltpu.make_async_remote_copy(
            src_ref=source,
            dst_ref=target,
            send_sem=self.send_sems.at[len(self.started)],
            recv_sem=self.recv_sems.at[name],
            device_id=device,
            device_id_type=MESH,
        )
        copy.start()
        self.started.append(copy)

    def arrive(self, target, name, device):
        pltpu.make_async_remote_copy(
            src_ref=target,
            dst_ref=target,
            send_sem=self.send_sems.at[0],
            recv_sem=self.recv_sems.at[name],
            device_id=device,
            device_id_type=MESH,
        ).wait_recv()

    def drain(self):
        for copy in self.started:
            copy.wait_send()


def greet(partners):
    barrier = pltpu.get_barrier_semaphore()
    for partner in partners:
        pl.semaphore_signal(barrier, inc=1, device_id=partner, device_id_type=MESH)
    pl.semaphore_wait(barrier, len(partners))


def mesh_sizes():
    return lax.axis_size("yo"), lax.axis_size("zo")


def add_rows(target, *parts):
    size = 16 if target.shape[0] % 16 == 0 else target.shape[0]

    def step(index, carry):
        rows = pl.ds(pl.multiple_of(index * size, size), size)
        total = target[rows, :].astype(jnp.float32)
        for part in parts:
            total = total + part[rows, :].astype(jnp.float32)
        target[rows, :] = total.astype(target.dtype)
        return carry

    lax.fori_loop(0, target.shape[0] // size, step, 0)


def together(*steps):
    alive = list(steps)
    while alive:
        for one in list(alive):
            try:
                next(one)
            except StopIteration:
                alive.remove(one)


def greet_layer(here):
    greet(
        [here.at(z=z, w=w) for z, w in here.column if (z, w) != (0, 0)]
        + [here.at(x=1), here.at(x=1, w=1), here.at(core=1)]
        + [here.at(y=y) for y in here.y_steps]
    )


def gather_attention_steps(here, wires, shards, wholes, even):
    count = len(shards)
    far = [offset for offset in here.column if offset != (0, 0)]
    mine = here.chip() * 2 + here.core
    other = here.at(core=1)

    def block(**offsets):
        return here.chip(**offsets) * 2 + here.core

    def name(kind, y, x, z, w, part):
        spot = (((kind * here.yo_size + y) * 2 + x) * here.zo_size + z) * 2 + w
        return spot * count + part

    for z, w in far:
        for part in range(count):
            wires.send(
                shards[part],
                wholes[part].at[mine],
                name(0, 0, 0, here.back_z(z), w, part),
                here.at(z=z, w=w),
            )

    def pass_on(source, y, x, z, w, part, to_x, to_y):
        target = wholes[part].at[block(y=y, x=x, z=z, w=w)]
        if to_x:
            wires.send(source, target, name(0, y, 1 - x, z, w, part), here.at(x=1))
        for step in here.y_steps if to_y else ():
            back = (y + here.back_y(step)) % here.yo_size
            wires.send(source, target, name(0, back, x, z, w, part), here.at(y=step))
        wires.send(source, target, name(1, y, x, z, w, part), other)

    for z, w in here.column:
        for part in range(count):
            if (z, w) == (0, 0):
                pass_on(shards[part], 0, 0, 0, 0, part, True, True)
                wholes[part][mine] = shards[part][...]
            else:
                source = wholes[part].at[block(z=z, w=w)]
                wires.arrive(source, name(0, 0, 0, z, w, part), other)
                pass_on(source, 0, 0, z, w, part, True, True)
        yield
    for z, w in here.column:
        for part in range(count):
            for y in here.y_steps:
                source = wholes[part].at[block(y=y, z=z, w=w)]
                wires.arrive(source, name(0, y, 0, z, w, part), other)
                pass_on(source, y, 0, z, w, part, not even or part % 2 == 0, False)
        yield
    for z, w in here.column:
        for part in range(count):
            source = wholes[part].at[block(x=1, z=z, w=w)]
            wires.arrive(source, name(0, 0, 1, z, w, part), other)
            pass_on(source, 0, 1, z, w, part, False, even and part % 2 == 1)
        yield
    for z, w in here.column:
        for part in range(count):
            for y in here.y_steps:
                source = wholes[part].at[block(y=y, x=1, z=z, w=w)]
                wires.arrive(source, name(0, y, 1, z, w, part), other)
                pass_on(source, y, 1, z, w, part, False, False)
        yield
    for y in range(here.yo_size):
        for x in range(2):
            for z, w in here.column:
                for part in range(count):
                    index = here.chip(y=y, x=x, z=z, w=w) * 2 + 1 - here.core
                    wires.arrive(wholes[part].at[index], name(1, y, x, z, w, part), other)


def gather_experts_steps(here, wires, shards, wholes):
    count = len(shards)
    group = offsets_of(GROUP)
    other = here.at(core=1)

    def name(kind, y, x, z, w, part):
        spot = (((kind * here.yo_size + y) * 2 + x) * here.zo_size + z) * 2 + w
        return spot * count + part

    def member(x, w):
        yo, xi, zo, zi, core = here.at(x=x, w=w)
        return xi * 2 + zi

    for x, w in group[1:]:
        for part in range(count):
            wires.send(
                shards[part].at[member(x, w)],
                wholes[part].at[0, here.chip()],
                name(0, 0, x, 0, w, part),
                here.at(x=x, w=w),
            )

    def pass_on(source, y, x, z, w, part, to_z, to_y):
        index = here.chip(y=y, x=x, z=z, w=w)
        for step in here.z_steps if to_z else ():
            back = (z + here.back_z(step)) % here.zo_size
            wires.send(
                source, wholes[part].at[0, index], name(0, y, x, back, w, part), here.at(z=step)
            )
        for step in here.y_steps if to_y else ():
            back = (y + here.back_y(step)) % here.yo_size
            wires.send(
                source, wholes[part].at[0, index], name(0, back, x, z, w, part), here.at(y=step)
            )
        wires.send(source, wholes[part].at[1, index], name(1, y, x, z, w, part), other)

    for x, w in group:
        for part in range(count):
            if (x, w) == (0, 0):
                pass_on(shards[part].at[member(0, 0)], 0, 0, 0, 0, part, True, True)
                wholes[part][0, here.chip()] = shards[part][member(0, 0)]
            else:
                source = wholes[part].at[0, here.chip(x=x, w=w)]
                wires.arrive(source, name(0, 0, x, 0, w, part), other)
                pass_on(source, 0, x, 0, w, part, True, True)
        yield
    for x, w in group:
        for part in range(count):
            for z in here.z_steps:
                source = wholes[part].at[0, here.chip(x=x, w=w, z=z)]
                wires.arrive(source, name(0, 0, x, z, w, part), other)
                pass_on(source, 0, x, z, w, part, False, True)
        yield
    for z in range(here.zo_size):
        for x, w in group:
            for part in range(count):
                for y in here.y_steps:
                    source = wholes[part].at[0, here.chip(y=y, x=x, w=w, z=z)]
                    wires.arrive(source, name(0, y, x, z, w, part), other)
                    pass_on(source, y, x, z, w, part, False, False)
            yield
    for y in range(here.yo_size):
        for z in range(here.zo_size):
            for x, w in group:
                for part in range(count):
                    target = wholes[part].at[1, here.chip(y=y, x=x, w=w, z=z)]
                    wires.arrive(target, name(1, y, x, z, w, part), other)


ATTENTION_PARTS = 3
EXPERT_PARTS = 2


def greet_experts(here):
    greet(
        [here.at(x=x, w=w) for x, w in offsets_of(GROUP)[1:]]
        + [here.at(z=z) for z in here.z_steps]
        + [here.at(y=y) for y in here.y_steps]
        + [here.at(core=1)]
    )


def greet_attention(here):
    greet(
        [here.at(z=z, w=w) for z, w in here.column if (z, w) != (0, 0)]
        + [here.at(x=1), here.at(core=1)]
        + [here.at(y=y) for y in here.y_steps]
    )


def gather_kernel(sizes, count, *refs):
    ins, outs, sems = refs[:count], refs[count : 2 * count], refs[2 * count :]
    here = Place(sizes)
    cut = ATTENTION_PARTS
    wires = [Wires(*sems[:2])]
    steps = [gather_attention_steps(here, wires[0], ins[:cut], outs[:cut], count == cut)]
    if count > cut:
        greet_layer(here)
        wires.append(Wires(*sems[2:]))
        steps.append(gather_experts_steps(here, wires[1], ins[cut:], outs[cut:]))
    else:
        greet_attention(here)
    together(*steps)
    for one in wires:
        one.drain()


def expert_sems(sizes):
    chips = sizes[0] * sizes[1] * 4
    sends = 3 + 4 * (sizes[0] + sizes[1]) + 4 * sizes[1] * sizes[0] + chips
    return [
        pltpu.SemaphoreType.DMA((EXPERT_PARTS * sends,)),
        pltpu.SemaphoreType.DMA((2 * chips * EXPERT_PARTS,)),
    ]


def gather(identity, attention_shards, expert_parts):
    sizes = mesh_sizes()
    chips = sizes[0] * sizes[1] * 4
    columns = sizes[1] * 2
    sends = ATTENTION_PARTS * ((columns - 1) + chips + columns * (2 * sizes[0] + 1) + chips)
    in_vmem = pl.BlockSpec(memory_space=pltpu.VMEM)
    count = len(attention_shards) + len(expert_parts)
    return pl.pallas_call(
        functools.partial(gather_kernel, sizes, count),
        out_shape=[
            jax.ShapeDtypeStruct((2 * chips,) + shard.shape, shard.dtype)
            for shard in attention_shards
        ]
        + [
            jax.ShapeDtypeStruct((2, chips) + part.shape[1:], part.dtype) for part in expert_parts
        ],
        in_specs=[in_vmem] * count,
        out_specs=[in_vmem] * count,
        scratch_shapes=[
            pltpu.SemaphoreType.DMA((sends,)),
            pltpu.SemaphoreType.DMA((2 * chips * ATTENTION_PARTS,)),
        ]
        + (expert_sems(sizes) if expert_parts else []),
        compiler_params=pltpu.CompilerParams(
            collective_id=identity, has_side_effects=True, vmem_limit_bytes=58 * 1024 * 1024
        ),
    )(*attention_shards, *expert_parts)


def sum_experts_steps(here, wires, whole, outs, first, second, third):
    count = len(whole)
    group = offsets_of(GROUP)
    other = here.at(core=1)
    chips = here.yo_size * here.zo_size * 4

    def place(y, z, member):
        return (y * here.zo_size + z) * 4 + member

    def name(kind, index, part):
        return (kind * chips + index) * count + part

    order = [
        (y, z, member)
        for y in list(here.y_steps) + [0]
        for z in list(here.z_steps) + [0]
        for member in (1, 2, 3, 0)
    ]
    for y, z, member in order:
        x, w = group[member]
        index = here.chip(y=y, x=x, z=z, w=w)
        spot = place(y, z, member)
        for part in range(count):
            wires.send(
                whole[part].at[1, index], first[part].at[spot], name(0, spot, part), other
            )
        if member == 0:
            yield
    for y, z, member in order:
        x, w = group[member]
        index = here.chip(y=y, x=x, z=z, w=w)
        spot = place(y, z, member)
        for part in range(count):
            total = first[part].at[spot]
            wires.arrive(total, name(0, spot, part), other)
            parts = [whole[part].at[0, index]]
            if y:
                add_rows(total, *parts)
                landing = place(here.back_y(y), z, member)
                wires.send(
                    total, second[part].at[landing - 4 * here.zo_size], name(1, landing, part), here.at(y=y)
                )
                continue
            for step in here.y_steps:
                spot_in = place(step, z, member)
                arrived = second[part].at[spot_in - 4 * here.zo_size]
                wires.arrive(arrived, name(1, spot_in, part), other)
                parts.append(arrived)
            if z:
                add_rows(total, *parts)
                landing = here.back_z(z) * 4 + member
                wires.send(
                    total, third[part].at[landing - 4], name(2, landing, part), here.at(z=z)
                )
                continue
            for step in here.z_steps:
                arrived = third[part].at[step * 4 + member - 4]
                wires.arrive(arrived, name(2, step * 4 + member, part), other)
                parts.append(arrived)
            add_rows(total, *parts)
            slot = here.xi * 2 + here.zi
            if member:
                wires.send(total, outs[part].at[slot], name(3, member, part), here.at(x=x, w=w))
            else:
                outs[part][slot] = total[...]
        yield
    for member in range(1, 4):
        x, w = group[member]
        yo, xi, zo, zi, core = here.at(x=x, w=w)
        for part in range(count):
            wires.arrive(outs[part].at[xi * 2 + zi], name(3, member, part), other)


def sum_attention_steps(here, wires, whole, outs, first, second, third, fourth):
    count = len(whole)
    columns = here.column
    other = here.at(core=1)
    width = len(columns)
    chips = here.yo_size * 2 * width

    def place(y, x, column):
        return (y * 2 + x) * width + column

    def name(kind, index, part):
        return (kind * chips + index) * count + part

    rounds = [
        (y, x, (column + 1) % width, part)
        for y, x in [(y, 1) for y in here.y_steps] + [(0, 1)] + [(y, 0) for y in here.y_steps] + [(0, 0)]
        for column in range(width)
        for part in range(count)
    ]
    for y, x, column, part in rounds:
        z, w = columns[column]
        spot = place(y, x, column)
        wires.send(
            whole[part].at[here.chip(y=y, x=x, z=z, w=w), 1 - here.core],
            first[part].at[spot],
            name(0, spot, part),
            other,
        )
        if (column, part) == (0, count - 1):
            yield
    for y, x, column, part in rounds:
        z, w = columns[column]
        spot = place(y, x, column)
        total = first[part].at[spot]
        wires.arrive(total, name(0, spot, part), other)
        parts = [whole[part].at[here.chip(y=y, x=x, z=z, w=w), here.core]]

        def take_in(buffer, kind, index, offset=0):
            arrived = buffer[part].at[index - offset]
            wires.arrive(arrived, name(kind, index, part), other)
            parts.append(arrived)

        def give(buffer, kind, index, device, offset=0):
            add_rows(total, *parts)
            wires.send(total, buffer[part].at[index - offset], name(kind, index, part), device)

        if x:
            give(second, 1, y * width + column, here.at(x=1))
            if part == count - 1:
                yield
            continue
        take_in(second, 1, y * width + column)
        if y:
            give(third, 2, here.back_y(y) * width + column, here.at(y=y), width)
            if part == count - 1:
                yield
            continue
        for step in here.y_steps:
            take_in(third, 2, step * width + column, width)
        if column:
            landing = columns.index((here.back_z(z), w))
            give(fourth, 3, landing, here.at(z=z, w=w), 1)
            if part == count - 1:
                yield
            continue
        for step in range(1, width):
            take_in(fourth, 3, step, 1)
        add_rows(total, *parts)
        outs[part][...] = total[...]


def sum_layer_kernel(sizes, *refs):
    both = ATTENTION_PARTS + EXPERT_PARTS
    cut = ATTENTION_PARTS
    ins, outs, rest = refs[:both], refs[both : 2 * both], refs[2 * both :]
    buffers, sems = rest[:-4], rest[-4:]
    attention = [buffers[level * cut : (level + 1) * cut] for level in range(4)]
    buffers = buffers[4 * cut :]
    experts = [buffers[level * EXPERT_PARTS : (level + 1) * EXPERT_PARTS] for level in range(3)]
    here = Place(sizes)
    wires = Wires(*sems[:2]), Wires(*sems[2:])
    greet_layer(here)
    together(
        sum_experts_steps(here, wires[1], ins[cut:], outs[cut:], *experts),
        sum_attention_steps(here, wires[0], ins[:cut], outs[:cut], *attention),
    )
    for one in wires:
        one.drain()


def sum_layer(attention_grads, expert_grads):
    sizes = mesh_sizes()
    chips = sizes[0] * sizes[1] * 4
    column = sizes[1] * 2
    attention = [grads.reshape(chips, 2, -1, grads.shape[1]) for grads in attention_grads]
    experts = [grads.reshape(2, chips, -1, D) for grads in expert_grads]
    in_vmem = pl.BlockSpec(memory_space=pltpu.VMEM)
    count = ATTENTION_PARTS + EXPERT_PARTS

    def held(blocks, sizes_of):
        return [
            pltpu.VMEM((sizes_of(part),) + block.shape[2:], jnp.bfloat16)
            for part, block in enumerate(blocks)
        ]

    return pl.pallas_call(
        functools.partial(sum_layer_kernel, sizes),
        out_shape=[jax.ShapeDtypeStruct(block.shape[2:], jnp.bfloat16) for block in attention]
        + [jax.ShapeDtypeStruct((4,) + block.shape[2:], jnp.bfloat16) for block in experts],
        in_specs=[in_vmem] * count,
        out_specs=[in_vmem] * count,
        scratch_shapes=held(attention, lambda part: chips)
        + held(attention, lambda part: sizes[0] * column)
        + held(attention, lambda part: (sizes[0] - 1) * column)
        + held(attention, lambda part: column - 1)
        + held(experts, lambda part: chips)
        + held(experts, lambda part: (sizes[0] - 1) * sizes[1] * 4)
        + held(experts, lambda part: (sizes[1] - 1) * 4)
        + [
            pltpu.SemaphoreType.DMA((3 * chips * ATTENTION_PARTS,)),
            pltpu.SemaphoreType.DMA((4 * chips * ATTENTION_PARTS,)),
            pltpu.SemaphoreType.DMA((3 * chips * EXPERT_PARTS,)),
            pltpu.SemaphoreType.DMA((4 * chips * EXPERT_PARTS,)),
        ],
        compiler_params=pltpu.CompilerParams(
            collective_id=5, has_side_effects=True, vmem_limit_bytes=62 * 1024 * 1024
        ),
    )(*attention, *experts)


def swap(value, axis):
    return lax.ppermute(value, axis, [(0, 1), (1, 0)])


def pick(value, index, axis=0):
    return lax.dynamic_index_in_dim(value, index, axis, keepdims=False)


def by_core(mine, theirs, axis):
    core = lax.axis_index("core")
    return jnp.where(
        core == 0, jnp.stack([mine, theirs], axis), jnp.stack([theirs, mine], axis)
    )


def gain_columns(gains):
    gains = gains.astype(jnp.bfloat16).T
    return jnp.pad(gains, ((0, 0), (0, 128 - gains.shape[1])))


def attention_shards(w_qkv, w_out, gains, layer):
    return [
        w_qkv[layer].astype(jnp.bfloat16),
        w_out[layer].astype(jnp.bfloat16),
        gain_columns(gains[layer]),
    ]


def expert_parts(w_gateup, w_down, layer):
    core = lax.axis_index("core")
    parts = []
    for shard in (w_gateup[layer], w_down[layer]):
        shard = shard.reshape((4, 2) + shard.shape[1:])
        theirs = swap(pick(shard, 1 - core, 1).astype(jnp.bfloat16), "core").astype(jnp.float32)
        pair = by_core(pick(shard, core, 1), theirs, 1).reshape(4, -1, D)
        parts.append(pair.astype(jnp.bfloat16))
    return parts


def attention_matrices(qkv, out, gain):
    gain = gain.reshape(D, 128)[:, :2].T.astype(jnp.float32)
    return qkv.reshape(D, QKV), out.reshape(D, D), gain


def expert_matrices(up, down):
    return up.reshape(2, D, 2 * F), down.reshape(2, F, D)


def layer_sums(grad_qkv, grad_out, grad_up, grad_down, grad_gains):
    core = lax.axis_index("core")
    attention = [
        grad_qkv.astype(jnp.bfloat16),
        grad_out.astype(jnp.bfloat16),
        gain_columns(grad_gains),
    ]
    qkv, out, gain, up, down = sum_layer(attention, [grad_up, grad_down])
    result = [qkv, out]
    for part in (up, down):
        part = part.astype(jnp.float32).reshape(4, 2, -1, D)
        theirs = swap(pick(part, 1 - core, 1).astype(jnp.bfloat16), "core").astype(jnp.float32)
        pair = by_core(pick(part, core, 1), theirs, 1)
        result.append(pair.reshape(EXPERTS, -1, D))
    return result + [gain[:, :2].T]


SQRT_HALF = 0.7071067811865476
PDF_SCALE = 0.3989422804014327
TILE = 384
TILES = F // TILE


def selections(table, columns):
    rows = table.shape[1]
    slots = lax.broadcasted_iota(jnp.int32, (CAP, rows), 0).astype(jnp.float32)
    take = (table[0:1, :] == slots).astype(jnp.bfloat16)
    slots = lax.broadcasted_iota(jnp.int32, (rows, CAP), 1).astype(jnp.float32)
    spread = (columns[:, 0:1] == slots).astype(jnp.bfloat16)
    return take, spread, columns[:, 1:2]


def dot(left, right, contract=(1, 0)):
    return lax.dot_general(
        left,
        right,
        (((contract[0],), (contract[1],)), ((), ())),
        preferred_element_type=jnp.float32,
    )


WAVES = ((0,), (3,), (1, 2))
TURNS = ((0, 2), (1, 1), (2, 2))


def moe_forward_kernel(sizes, background, *refs):
    tokens, tables, columns, up_w, down_w = refs[:5]
    extra = EXPERT_PARTS if background else 0
    shards, refs = refs[5 : 5 + extra], refs[5 + extra :]
    merged, slot_out, gate_out, up_out, active_out = refs[:5]
    wholes, refs = refs[5 : 5 + extra], refs[5 + extra :]
    chunks, leaving, coming, slot_in, result, total = refs[:6]
    sems = refs[6:]
    here = Place(sizes)
    wires = Wires(*sems[:2])
    partners = [here.at(x=x, w=w) for x, w in offsets_of(GROUP)]
    if background:
        greet_experts(here)
        other_wires = Wires(*sems[2:])
        steps = gather_experts_steps(here, other_wires, shards, wholes)
    else:
        greet(partners[1:])
        steps = iter(())
    for place in (3, 1, 2):
        wires.send(tokens, chunks.at[place - 1], place - 1, partners[place])
    next(steps, None)
    for wave, turns in zip(WAVES, TURNS):
        sources = []
        for place in wave:
            source = tokens if place == 0 else chunks.at[place - 1]
            if place:
                wires.arrive(source, place - 1, partners[place])
            sources.append(source)
        count = CAP * len(wave)
        rows = pl.ds(wave[0] * CAP, count)
        for expert in range(2):
            picks = [selections(tables[place, expert], columns[place, expert]) for place in wave]
            for index, source in enumerate(sources):
                chosen = dot(picks[index][0], source[...]).astype(jnp.bfloat16)
                slot_in[index * CAP : (index + 1) * CAP] = chosen
            slot_out[expert, rows, :] = slot_in[:count]

            def step(tile, carry, expert=expert, count=count, rows=rows):
                at_gate = pl.ds(pl.multiple_of(tile * TILE, TILE), TILE)
                at_up = pl.ds(pl.multiple_of(F + tile * TILE, TILE), TILE)
                gate = dot(slot_in[:count], up_w[expert, :, at_gate])
                up = dot(slot_in[:count], up_w[expert, :, at_up])
                active = (0.5 * gate * (1.0 + lax.erf(gate * SQRT_HALF)) * up).astype(jnp.bfloat16)
                gate_out[expert, rows, at_gate] = gate.astype(jnp.bfloat16)
                up_out[expert, rows, at_gate] = up.astype(jnp.bfloat16)
                active_out[expert, rows, at_gate] = active
                return carry

            lax.fori_loop(0, TILES, step, 0)

            def finish(tile, carry, expert=expert, count=count, rows=rows):
                lanes = pl.ds(pl.multiple_of(tile * 2 * TILE, TILE), 2 * TILE)
                result[:count, lanes] = dot(
                    active_out[expert, rows, :], down_w[expert, :, lanes]
                ).astype(jnp.bfloat16)
                return carry

            lax.fori_loop(0, D // (2 * TILE), finish, 0)
            for index in range(len(wave)):
                take, spread, gates = picks[index]
                share = dot(spread, result[index * CAP : (index + 1) * CAP]) * gates
                if expert == 0:
                    total[index] = share
                else:
                    total[index] += share
            for turn in range(turns[expert]):
                next(steps, None)
        for index, place in enumerate(wave):
            if place == 0:
                merged[...] = total[index]
            else:
                leaving[place - 1] = total[index].astype(jnp.bfloat16)
                wires.send(
                    leaving.at[place - 1], coming.at[place - 1], place + 2, partners[place]
                )
    for one in steps:
        pass
    for place in range(1, 4):
        wires.arrive(coming.at[place - 1], place + 2, partners[place])
        merged[...] += coming[place - 1].astype(jnp.float32)
    wires.drain()
    if background:
        other_wires.drain()


STAGES = 6


def moe_backward_kernel(sizes, *refs):
    gradient, tables, columns, up_w, down_w, slot_in, gate_in, up_in, active = refs[:9]
    merged, up_grads, down_grads = refs[9:12]
    chunks, leaving, coming, slot_grad, slots, total = refs[12:18]
    slot_out, gate_out, up_out, up_stage, down_stage = refs[18:23]
    here = Place(sizes)
    wires = Wires(*refs[23:25])
    stage_sems = refs[25]
    partners = [here.at(x=x, w=w) for x, w in offsets_of(GROUP)]
    greet(partners[1:])
    leaving[3] = gradient[...].astype(jnp.bfloat16)
    for place in (3, 1, 2):
        wires.send(leaving.at[3], chunks.at[place - 1], place - 1, partners[place])
    for wave in WAVES:
        sources = []
        for place in wave:
            source = gradient if place == 0 else chunks.at[place - 1]
            if place:
                wires.arrive(source, place - 1, partners[place])
            sources.append(source)
        count = CAP * len(wave)
        rows = pl.ds(wave[0] * CAP, count)
        for expert in range(2):
            picks = [selections(tables[place, expert], columns[place, expert]) for place in wave]
            for index, source in enumerate(sources):
                take, spread, gates = picks[index]
                weighted = (gates * source[...].astype(jnp.float32)).astype(jnp.bfloat16)
                slot_grad[index * CAP : (index + 1) * CAP] = dot(take, weighted).astype(jnp.bfloat16)
            slot_out[expert, rows, :] = slot_grad[:count]

            def step(tile, carry, expert=expert, count=count, rows=rows):
                at_gate = pl.ds(pl.multiple_of(tile * TILE, TILE), TILE)
                grad_act = dot(slot_grad[:count], down_w[expert, at_gate, :], (1, 1))
                gate = gate_in[expert, rows, at_gate].astype(jnp.float32)
                up = up_in[expert, rows, at_gate].astype(jnp.float32)
                below = 0.5 * (1.0 + lax.erf(gate * SQRT_HALF))
                slope = below + gate * PDF_SCALE * jnp.exp(-0.5 * gate * gate)
                gate_out[expert, rows, at_gate] = (grad_act * up * slope).astype(jnp.bfloat16)
                up_out[expert, rows, at_gate] = (grad_act * gate * below).astype(jnp.bfloat16)
                return carry

            lax.fori_loop(0, TILES, step, 0)

            def finish(tile, carry, expert=expert, count=count, rows=rows):
                lanes = pl.ds(pl.multiple_of(tile * 2 * TILE, TILE), 2 * TILE)
                part = dot(gate_out[expert, rows, :], up_w[expert, lanes, :F], (1, 1))
                part = part + dot(up_out[expert, rows, :], up_w[expert, lanes, F:], (1, 1))
                slots[:count, lanes] = part.astype(jnp.bfloat16)
                return carry

            lax.fori_loop(0, D // (2 * TILE), finish, 0)
            for index in range(len(wave)):
                share = dot(picks[index][1], slots[index * CAP : (index + 1) * CAP])
                if expert == 0:
                    total[index] = share
                else:
                    total[index] += share
        for index, place in enumerate(wave):
            if place == 0:
                merged[...] = total[index]
            else:
                leaving[place - 1] = total[index].astype(jnp.bfloat16)
                wires.send(
                    leaving.at[place - 1], coming.at[place - 1], place + 2, partners[place]
                )

    def copies(index):
        expert, tile, slot = lax.div(index, STAGES), lax.rem(index, STAGES), lax.rem(index, 2)
        up_rows = pl.ds(pl.multiple_of(tile * (D // STAGES), D // STAGES), D // STAGES)
        down_rows = pl.ds(pl.multiple_of(tile * (F // STAGES), F // STAGES), F // STAGES)
        pair = (
            pltpu.make_async_copy(
                up_stage.at[slot], up_grads.at[expert, up_rows], stage_sems.at[slot, 0]
            ),
            pltpu.make_async_copy(
                down_stage.at[slot], down_grads.at[expert, down_rows], stage_sems.at[slot, 1]
            ),
        )
        return expert, slot, up_rows, down_rows, pair

    def weight_step(index, carry):
        expert, slot, up_rows, down_rows, pair = copies(index)

        @pl.when(index >= 2)
        def _():
            for copy in copies(index - 2)[-1]:
                copy.wait()

        taken = slot_in[expert, :, up_rows]
        up_stage[slot, :, :F] = dot(taken, gate_out[expert], (0, 0)).astype(jnp.bfloat16)
        up_stage[slot, :, F:] = dot(taken, up_out[expert], (0, 0)).astype(jnp.bfloat16)
        down_stage[slot] = dot(active[expert, :, down_rows], slot_out[expert], (0, 0)).astype(
            jnp.bfloat16
        )
        for copy in pair:
            copy.start()
        return carry

    lax.fori_loop(0, 2 * STAGES, weight_step, 0)
    for index in range(2 * STAGES - 2, 2 * STAGES):
        for copy in copies(index)[-1]:
            copy.wait()
    for place in range(1, 4):
        wires.arrive(coming.at[place - 1], place + 2, partners[place])
        merged[...] += coming[place - 1].astype(jnp.float32)
    wires.drain()


def moe_call(kernel, identity, rows_in, tables, weights, extra, kinds, background=()):
    rows = rows_in.shape[0]
    slots = 4 * CAP
    sizes = mesh_sizes()
    chips = sizes[0] * sizes[1] * 4
    operands = [rows_in, tables, jnp.swapaxes(tables, 2, 3), *weights, *extra, *background]
    in_vmem = pl.BlockSpec(memory_space=pltpu.VMEM)
    more_sems = expert_sems(sizes) if background else []
    return pl.pallas_call(
        functools.partial(kernel, sizes, bool(background)),
        in_specs=[in_vmem] * len(operands),
        out_specs=[in_vmem] * (1 + len(kinds) + len(background)),
        out_shape=[jax.ShapeDtypeStruct((rows, D), jnp.float32)]
        + [jax.ShapeDtypeStruct((2, slots, width), jnp.bfloat16) for width in kinds]
        + [jax.ShapeDtypeStruct((2, chips) + part.shape[1:], part.dtype) for part in background],
        scratch_shapes=[
            pltpu.VMEM((3, rows, D), jnp.bfloat16),
            pltpu.VMEM((4, rows, D), jnp.bfloat16),
            pltpu.VMEM((3, rows, D), jnp.bfloat16),
            pltpu.VMEM((2 * CAP, D), jnp.bfloat16),
            pltpu.VMEM((2 * CAP, D), jnp.bfloat16),
            pltpu.VMEM((2, rows, D), jnp.float32),
            pltpu.SemaphoreType.DMA((6,)),
            pltpu.SemaphoreType.DMA((6,)),
        ]
        + more_sems,
        compiler_params=pltpu.CompilerParams(
            collective_id=identity, has_side_effects=True, vmem_limit_bytes=62 * 1024 * 1024
        ),
        cost_estimate=pl.CostEstimate(
            flops=48 * CAP * D * F, bytes_accessed=40_000_000, transcendentals=8 * CAP * F
        ),
    )(*operands)


def moe_forward(expert_in, tables, weights, background):
    merged, *kept = moe_call(
        moe_forward_kernel,
        2 if background else 3,
        expert_in,
        tables,
        weights,
        [],
        (D, F, F, F),
        background,
    )
    return merged, kept[:4], expert_matrices(*kept[4:]) if background else None


def moe_backward(gradient, tables, weights, kept):
    rows = gradient.shape[0]
    slots = 4 * CAP
    operands = [gradient, tables, jnp.swapaxes(tables, 2, 3), *weights, *kept]
    in_vmem, anywhere = pl.BlockSpec(memory_space=pltpu.VMEM), pl.BlockSpec(memory_space=pl.ANY)
    low = jnp.bfloat16
    return pl.pallas_call(
        functools.partial(moe_backward_kernel, mesh_sizes()),
        in_specs=[in_vmem] * len(operands),
        out_specs=[in_vmem, anywhere, anywhere],
        out_shape=[
            jax.ShapeDtypeStruct((rows, D), jnp.float32),
            jax.ShapeDtypeStruct((2, D, 2 * F), low),
            jax.ShapeDtypeStruct((2, F, D), low),
        ],
        scratch_shapes=[
            pltpu.VMEM((3, rows, D), low),
            pltpu.VMEM((4, rows, D), low),
            pltpu.VMEM((3, rows, D), low),
            pltpu.VMEM((2 * CAP, D), low),
            pltpu.VMEM((2 * CAP, D), low),
            pltpu.VMEM((2, rows, D), jnp.float32),
            pltpu.VMEM((2, slots, D), low),
            pltpu.VMEM((2, slots, F), low),
            pltpu.VMEM((2, slots, F), low),
            pltpu.VMEM((2, D // STAGES, 2 * F), low),
            pltpu.VMEM((2, F // STAGES, D), low),
            pltpu.SemaphoreType.DMA((6,)),
            pltpu.SemaphoreType.DMA((6,)),
            pltpu.SemaphoreType.DMA((2, 2)),
        ],
        compiler_params=pltpu.CompilerParams(
            collective_id=4, has_side_effects=True, vmem_limit_bytes=62 * 1024 * 1024
        ),
        cost_estimate=pl.CostEstimate(
            flops=96 * CAP * D * F, bytes_accessed=40_000_000, transcendentals=8 * CAP * F
        ),
    )(*operands)


def turned(vectors, cosine, sine):
    return vectors * cosine + pltpu.roll(vectors, HD // 2, 1) * sine


def project_kernel(stream, gain, weight, cosine, sine, normed, heads):
    tile = pl.program_id(0)

    @pl.when(tile == 0)
    def _():
        values = stream[...]
        scale = lax.rsqrt(jnp.mean(values * values, axis=-1, keepdims=True) + NORM_EPS)
        normed[...] = (values * scale * gain[...]).astype(jnp.bfloat16)

    result = dot(normed[...], weight[...])
    rotated = (H + KVH) // 2

    @pl.when(tile < rotated)
    def _():
        for head in range(2):
            lanes = slice(head * HD, (head + 1) * HD)
            heads[:, lanes] = turned(result[:, lanes], cosine[...], sine[...]).astype(jnp.bfloat16)

    @pl.when(tile >= rotated)
    def _():
        heads[...] = result.astype(jnp.bfloat16)


def project(stream, gain, weight, cosine, sine):
    rows, width = stream.shape[0], 2 * HD

    def same(shape):
        return pl.BlockSpec(shape, lambda tile: (0, 0))

    return pl.pallas_call(
        project_kernel,
        grid=(QKV // width,),
        in_specs=[
            same((rows, D)),
            same((1, D)),
            pl.BlockSpec((D, width), lambda tile: (0, tile)),
            same((rows, HD)),
            same((rows, HD)),
        ],
        out_specs=[
            same((rows, D)),
            pl.BlockSpec((rows, width), lambda tile: (0, tile)),
        ],
        out_shape=[
            jax.ShapeDtypeStruct((rows, D), jnp.bfloat16),
            jax.ShapeDtypeStruct((rows, QKV), jnp.bfloat16),
        ],
        compiler_params=pltpu.CompilerParams(vmem_limit_bytes=60 * 1024 * 1024),
        cost_estimate=pl.CostEstimate(
            flops=2 * rows * D * QKV, bytes_accessed=12_000_000, transcendentals=rows
        ),
    )(stream, gain[None], weight, cosine, sine)


def head_columns(rows, offset):
    return pl.BlockSpec((rows, HD), lambda head: (0, offset + head // (H // KVH)))


def attention_kernel(*refs):
    query, allowed = refs[:2]
    attended, total = refs[-3:-1]
    scores = refs[-1]
    count = (len(refs) - 5) // 2
    keys, values = refs[2 : 2 + count], refs[2 + count : 2 + 2 * count]
    rows = query.shape[0]
    for index, key in enumerate(keys):
        lanes = slice(index * rows, (index + 1) * rows)
        part = dot(query[...], key[...], (1, 1)) * HD ** (-0.5)
        scores[:, lanes] = jnp.where(allowed[:, lanes] > 0, part, MASKED)
    row_max = jnp.max(scores[...], axis=-1, keepdims=True)
    exponent = jnp.exp(scores[...] - row_max)
    row_total = jnp.sum(exponent, axis=-1, keepdims=True)
    probabilities = (exponent / row_total).astype(jnp.bfloat16)
    result = None
    for index, value in enumerate(values):
        part = dot(probabilities[:, index * rows : (index + 1) * rows], value[...])
        result = part if result is None else result + part
    attended[...] = result.astype(jnp.bfloat16)
    total[0] = jnp.broadcast_to(row_max + jnp.log(row_total), total.shape[1:])


def attention_forward(heads, blocks, allowed):
    rows, count = heads.shape[0], len(blocks)
    one = pl.BlockSpec((rows, HD), lambda head: (0, head))
    return pl.pallas_call(
        attention_kernel,
        grid=(H,),
        in_specs=[one, pl.BlockSpec(allowed.shape, lambda head: (0, 0))]
        + [head_columns(rows, 0)] * count
        + [head_columns(rows, KVH)] * count,
        out_specs=[one, pl.BlockSpec((1, rows, HD), lambda head: (head, 0, 0))],
        out_shape=[
            jax.ShapeDtypeStruct((rows, H * HD), jnp.bfloat16),
            jax.ShapeDtypeStruct((H, rows, HD), jnp.float32),
        ],
        scratch_shapes=[pltpu.VMEM((rows, rows * count), jnp.float32)],
        compiler_params=pltpu.CompilerParams(vmem_limit_bytes=60 * 1024 * 1024),
        cost_estimate=pl.CostEstimate(
            flops=4 * H * HD * rows * rows * count,
            bytes_accessed=8_000_000,
            transcendentals=H * rows * rows * count,
        ),
    )(heads, allowed, *blocks, *blocks)


def attention_backward_kernel(*refs):
    query, allowed, gradient, total, cosine, sine = refs[:6]
    turned_back, blocks_out, probabilities, grads, key_sum, value_sum = refs[-6:]
    count = (len(refs) - 12) // 2
    keys, values = refs[6 : 6 + count], refs[6 + count : 6 + 2 * count]
    rows = query.shape[0]
    head, group = pl.program_id(0), H // KVH
    scale = HD ** (-0.5)
    inner = jnp.zeros((rows, 1), jnp.float32)
    for index in range(count):
        lanes = slice(index * rows, (index + 1) * rows)
        part = dot(query[...], keys[index][...], (1, 1)) * scale
        part = jnp.where(allowed[:, lanes] > 0, jnp.exp(part - total[0, :, :1]), 0.0)
        slope = dot(gradient[...], values[index][...], (1, 1))
        probabilities[:, lanes] = part
        grads[:, lanes] = slope
        inner = inner + jnp.sum(part * slope, axis=-1, keepdims=True)
    back = None
    for index in range(count):
        lanes = slice(index * rows, (index + 1) * rows)
        part = probabilities[:, lanes]
        grad_scores = (part * (grads[:, lanes] - inner)).astype(jnp.bfloat16)
        share = dot(grad_scores, keys[index][...])
        back = share if back is None else back + share
        key_part = dot(grad_scores, query[...], (0, 0)) * scale
        value_part = dot(part.astype(jnp.bfloat16), gradient[...], (0, 0))

        @pl.when(lax.rem(head, group) == 0)
        def _(index=index, key_part=key_part, value_part=value_part):
            key_sum[index] = key_part
            value_sum[index] = value_part

        @pl.when(lax.rem(head, group) > 0)
        def _(index=index, key_part=key_part, value_part=value_part):
            key_sum[index] += key_part
            value_sum[index] += value_part

    turned_back[...] = turned(back * scale, cosine[...], -sine[...]).astype(jnp.bfloat16)
    for place in range(KVH):

        @pl.when(head == (place + 1) * group - 1)
        def _(place=place):
            for index in range(count):
                blocks_out[index, :, place * HD : (place + 1) * HD] = key_sum[index].astype(
                    jnp.bfloat16
                )
                blocks_out[index, :, (KVH + place) * HD : (KVH + place + 1) * HD] = value_sum[
                    index
                ].astype(jnp.bfloat16)


def attention_backward(heads, blocks, allowed, totals, gradient, cosine, sine):
    rows, count = heads.shape[0], len(blocks)
    one = pl.BlockSpec((rows, HD), lambda head: (0, head))
    table = pl.BlockSpec((rows, HD), lambda head: (0, 0))
    width = 2 * KVH * HD
    return pl.pallas_call(
        attention_backward_kernel,
        grid=(H,),
        in_specs=[
            one,
            pl.BlockSpec(allowed.shape, lambda head: (0, 0)),
            one,
            pl.BlockSpec((1, rows, HD), lambda head: (head, 0, 0)),
            table,
            table,
        ]
        + [head_columns(rows, 0)] * count
        + [head_columns(rows, KVH)] * count,
        out_specs=[one, pl.BlockSpec((count, rows, width), lambda head: (0, 0, 0))],
        out_shape=[
            jax.ShapeDtypeStruct((rows, QKV), jnp.bfloat16),
            jax.ShapeDtypeStruct((count, rows, width), jnp.bfloat16),
        ],
        scratch_shapes=[
            pltpu.VMEM((rows, rows * count), jnp.float32),
            pltpu.VMEM((rows, rows * count), jnp.float32),
            pltpu.VMEM((count, rows, HD), jnp.float32),
            pltpu.VMEM((count, rows, HD), jnp.float32),
        ],
        compiler_params=pltpu.CompilerParams(vmem_limit_bytes=60 * 1024 * 1024),
        cost_estimate=pl.CostEstimate(
            flops=10 * H * HD * rows * rows * count,
            bytes_accessed=10_000_000,
            transcendentals=H * rows * rows * count,
        ),
    )(heads, allowed, gradient, totals, cosine, sine, *blocks, *blocks)


def finish_keys_kernel(*refs):
    parts, (cosine, sine, unused, out) = refs[:-4], refs[-4:]
    for place in range(2 * KVH):
        lanes = slice(place * HD, (place + 1) * HD)
        total = parts[0][:, lanes].astype(jnp.float32)
        for part in parts[1:]:
            total = total + part[:, lanes].astype(jnp.float32)
        if place < KVH:
            total = turned(total, cosine[...], -sine[...])
        out[:, lanes] = total.astype(jnp.bfloat16)


def finish_keys(parts, cosine, sine, projected):
    rows, width = parts[0].shape
    return pl.pallas_call(
        finish_keys_kernel,
        grid=(1,),
        in_specs=[pl.BlockSpec((rows, width), lambda step: (0, 0))] * len(parts)
        + [pl.BlockSpec((rows, HD), lambda step: (0, 0))] * 2
        + [pl.BlockSpec(memory_space=pl.ANY)],
        out_specs=pl.BlockSpec((rows, width), lambda step: (0, QKV // width - 1)),
        out_shape=jax.ShapeDtypeStruct(projected.shape, projected.dtype),
        input_output_aliases={len(parts) + 2: 0},
        compiler_params=pltpu.CompilerParams(vmem_limit_bytes=60 * 1024 * 1024),
        cost_estimate=pl.CostEstimate(flops=0, bytes_accessed=2_000_000, transcendentals=0),
    )(*parts, cosine, sine, projected)


def weight_grad_kernel(rows_in, grads, out):
    out[...] = dot(rows_in[...], grads[...], (0, 0)).astype(jnp.bfloat16)


def weight_grad(rows_in, grads):
    rows, width = grads.shape
    tile = D // 3
    return pl.pallas_call(
        weight_grad_kernel,
        grid=(3,),
        in_specs=[
            pl.BlockSpec((rows, tile), lambda step: (0, step)),
            pl.BlockSpec((rows, width), lambda step: (0, 0)),
        ],
        out_specs=pl.BlockSpec((tile, width), lambda step: (step, 0)),
        out_shape=jax.ShapeDtypeStruct((D, width), jnp.bfloat16),
        compiler_params=pltpu.CompilerParams(vmem_limit_bytes=60 * 1024 * 1024),
        cost_estimate=pl.CostEstimate(
            flops=2 * rows * D * width, bytes_accessed=2 * D * width, transcendentals=0
        ),
    )(rows_in, grads)


def rotate_back(gradient, cosine_table, sine_table):
    half_width = gradient.shape[-1] // 2
    first_half = gradient[..., :half_width]
    second_half = gradient[..., half_width:]
    return jnp.concatenate(
        [
            first_half * cosine_table + second_half * sine_table,
            second_half * cosine_table - first_half * sine_table,
        ],
        axis=-1,
    )


def plain_backward(queries, keys_all, values_all, allowed, totals, grad_attended):
    group_size = H // KVH
    score_scale = HD ** (-0.5)
    grad_queries = []
    grad_keys = []
    grad_values = []
    for head_group in range(KVH):
        query_part = queries[:, head_group * group_size : (head_group + 1) * group_size, :]
        grad_part = grad_attended[:, head_group * group_size : (head_group + 1) * group_size, :]
        keys_part = keys_all[:, head_group, :]
        scores = (
            jnp.einsum("tjd,kd->jtk", query_part, keys_part, preferred_element_type=jnp.float32)
            * score_scale
        )
        probabilities = jnp.where(allowed[None], jnp.exp(scores - totals[head_group]), 0.0)
        grad_probs = jnp.einsum(
            "tjd,kd->jtk",
            grad_part,
            values_all[:, head_group, :],
            preferred_element_type=jnp.float32,
        )
        grad_scores = probabilities * (
            grad_probs - jnp.sum(probabilities * grad_probs, axis=-1, keepdims=True)
        )
        grad_scores = grad_scores.astype(jnp.bfloat16)
        grad_queries.append(
            jnp.einsum("jtk,kd->tjd", grad_scores, keys_part, preferred_element_type=jnp.float32)
            * score_scale
        )
        grad_keys.append(
            jnp.einsum("jtk,tjd->kd", grad_scores, query_part, preferred_element_type=jnp.float32)
            * score_scale
        )
        grad_values.append(
            jnp.einsum(
                "jtk,tjd->kd",
                probabilities.astype(jnp.bfloat16),
                grad_part,
                preferred_element_type=jnp.float32,
            )
        )
    return (
        jnp.concatenate(grad_queries, axis=1),
        jnp.stack(grad_keys, axis=1),
        jnp.stack(grad_values, axis=1),
    )


def layer_forward(stream, attn_w, expert_w, ahead, tables, allowed, cosine_table, sine_table):
    qkv_w, out_w, gain_full = attn_w
    attn_in, heads = project(stream, gain_full[0], qkv_w, cosine_table, sine_table)
    own = heads[:, H * HD :]
    blocks = [send(own, CTX, offsets) for offsets in offsets_of(CTX)]
    attended, totals = attention_forward(heads, blocks, allowed)
    middle_stream = stream + jnp.dot(attended, out_w, preferred_element_type=jnp.float32)
    normed_two, scale_two = normalize(middle_stream, gain_full[1])
    expert_in = normed_two.astype(jnp.bfloat16)
    merged, kept, gathered = moe_forward(expert_in, tables, expert_w, ahead)
    record = {
        "stream": stream,
        "attn_in": attn_in,
        "heads": heads,
        "blocks": blocks,
        "totals": totals,
        "attended": attended,
        "middle": middle_stream,
        "scale_two": scale_two,
        "kept": kept,
    }
    return (record, middle_stream + merged, gathered)


def layer_backward(gradient, record, attn_w, expert_w, tables, allowed, cosine_table, sine_table):
    qkv_w, out_w, gain_full = attn_w
    grad_normed, grad_up, grad_down = moe_backward(gradient, tables, expert_w, record["kept"])
    grad_in_two, grad_gain_two = normalize_back(
        grad_normed, record["middle"], record["scale_two"], gain_full[1]
    )
    grad_middle = gradient + grad_in_two
    grad_middle_low = grad_middle.astype(jnp.bfloat16)
    grad_out = weight_grad(record["attended"], grad_middle_low)
    grad_attended = jnp.dot(grad_middle_low, out_w.T, preferred_element_type=jnp.float32)
    keys_all = jnp.concatenate(record["blocks"], axis=0).reshape(-1, 2 * KVH, HD)
    totals = record["totals"][:, :, :1].reshape(KVH, H // KVH, -1, 1)
    row_count = gradient.shape[0]
    grad_queries, grad_keys_all, grad_values_all = plain_backward(
        record["heads"][:, : H * HD].reshape(-1, H, HD),
        keys_all[:, :KVH],
        keys_all[:, KVH:],
        allowed > 0,
        [totals[0], totals[1]],
        grad_attended.astype(jnp.bfloat16).reshape(-1, H, HD),
    )
    both_all = jnp.concatenate([grad_keys_all, grad_values_all], axis=1)
    both = None
    for place, offsets in enumerate(offsets_of(CTX)):
        part = both_all[place * row_count : (place + 1) * row_count]
        if offsets != (0, 0):
            part = send(part.astype(jnp.bfloat16), CTX, offsets, back=True).astype(jnp.float32)
        both = part if both is None else both + part
    grad_keys, grad_values = both[:, :KVH], both[:, KVH:]
    ct, st = cosine_table[:, None, : HD // 2], sine_table[:, None, HD // 2 :]
    grad_projected = jnp.concatenate(
        [
            rotate_back(grad_queries, ct, st).reshape(row_count, H * HD),
            rotate_back(grad_keys, ct, st).reshape(row_count, KVH * HD),
            grad_values.reshape(row_count, KVH * HD),
        ],
        axis=1,
    ).astype(jnp.bfloat16)
    grad_qkv = weight_grad(record["attn_in"], grad_projected)
    grad_normed_one = jnp.dot(grad_projected, qkv_w.T, preferred_element_type=jnp.float32)
    unused, scale_one = normalize(record["stream"], gain_full[0])
    grad_in_one, grad_gain_one = normalize_back(
        grad_normed_one, record["stream"], scale_one, gain_full[0]
    )
    grad_gains = jnp.stack([grad_gain_one, grad_gain_two])
    return (grad_middle + grad_in_one, (grad_qkv, grad_out, grad_up, grad_down, grad_gains))


def on_device(
    tokens,
    cotangent,
    routes,
    gate_weights,
    lengths,
    block_map,
    w_qkv,
    w_out,
    w_gateup,
    w_down,
    gains,
    m_qkv,
    v_qkv,
    m_out,
    v_out,
    m_gateup,
    v_gateup,
    m_down,
    v_down,
    m_gains,
    v_gains,
):
    row_count = tokens.shape[1]
    block_rows = row_count // 2
    own_pos, own_doc = positions_docs(block_map, lengths[0], flat_index(CTX), block_rows)
    places = [
        positions_docs(block_map, lengths[0], source_index(CTX, offsets), block_rows)
        for offsets in offsets_of(CTX)
    ]
    key_pos = jnp.concatenate([place[0] for place in places])
    key_doc = jnp.concatenate([place[1] for place in places])
    allowed = (own_doc[:, None] == key_doc[None, :]) & (key_pos[None, :] <= own_pos[:, None])
    allowed = allowed.astype(jnp.float32)
    cosine_table, sine_table = rope_tables(own_pos)
    own_tables = jnp.stack(
        [dispatch_tables(routes[layer, 0], gate_weights[layer, 0]) for layer in range(LAYERS)]
    )
    core = lax.axis_index("core")
    group_tables = []
    for offsets in offsets_of(GROUP):
        theirs = lax.dynamic_slice_in_dim(own_tables, 2 * target_index(GROUP, offsets), 2, axis=1)
        theirs = jnp.where(core == 0, theirs, theirs[:, ::-1])
        group_tables.append(send(theirs, GROUP, offsets))
    group_tables = jnp.stack(group_tables, axis=1)
    stream = tokens[0].astype(jnp.float32)
    records = []
    shards = [attention_shards(w_qkv, w_out, gains, layer) for layer in range(LAYERS)]
    parts = [expert_parts(w_gateup, w_down, layer) for layer in range(LAYERS)]
    first = gather(0, shards[0], [])
    parts[0], first = lax.optimization_barrier((parts[0], first))
    second = gather(1, shards[1], parts[0])
    cut = ATTENTION_PARTS
    attn_w = [attention_matrices(*first), attention_matrices(*second[:cut])]
    expert_w = [expert_matrices(*second[cut:]), None]
    for layer_index in range(LAYERS):
        ahead = [] if layer_index else parts[1]
        record, stream, gathered = layer_forward(
            stream,
            attn_w[layer_index],
            expert_w[layer_index],
            ahead,
            group_tables[layer_index],
            allowed,
            cosine_table,
            sine_table,
        )
        records.append(record)
        if ahead:
            expert_w[1] = gathered
    output = stream.astype(jnp.bfloat16)[None]
    gradient = cotangent[0].astype(jnp.float32)
    rates = (D ** (-0.5), 0.5, D ** (-0.5), (F // 8) ** (-0.5), 1.0)
    decays = (DECAY, DECAY, DECAY, DECAY, 0.0)
    params = (w_qkv, w_out, w_gateup, w_down, gains)
    firsts = (m_qkv, m_out, m_gateup, m_down, m_gains)
    seconds = (v_qkv, v_out, v_gateup, v_down, v_gains)
    sums = [None] * LAYERS
    for layer_index in reversed(range(LAYERS)):
        gradient, layer_grads = layer_backward(
            gradient,
            records[layer_index],
            attn_w[layer_index],
            expert_w[layer_index],
            group_tables[layer_index],
            allowed,
            cosine_table,
            sine_table,
        )
        sums[layer_index] = layer_sums(*layer_grads)
    updated = []
    for which in range(5):
        total = jnp.stack([sums[layer][which] for layer in range(LAYERS)]).astype(jnp.float32)
        updated.extend(
            adamw(
                params[which], firsts[which], seconds[which], total, rates[which], decays[which]
            )
        )
    return (output, gradient[None], *updated)


def solution(mesh):
    ctx_size, shard_size = mesh.shape["ctx"], mesh.shape["shard"]
    fine = Mesh(mesh.devices.reshape(ctx_size // 2, 2, shard_size // 4, 2, 2), ALL)
    tokens = P(SHARD, CTX, None)
    routed = P(None, SHARD, CTX, None)
    rows_two = P(None, ALL, None)
    rows_three = P(None, None, ALL, None)
    gain = P(None, None, ALL)
    weights = (rows_two, rows_two, rows_three, rows_three, gain)
    states = tuple(spec for spec in weights for which in range(2))
    return jax.shard_map(
        on_device,
        mesh=fine,
        in_specs=(tokens, tokens, routed, routed, P(SHARD, None), P()) + weights + states,
        out_specs=(tokens, tokens) + tuple(spec for spec in weights for which in range(3)),
        check_vma=False,
    )
```

```python
import functools

import jax
import jax.numpy as jnp
from jax import lax
from jax.experimental import pallas as pl
from jax.experimental.pallas import tpu as pltpu
from jax.sharding import Mesh
from jax.sharding import PartitionSpec as P

D = 1536
H = 12
KVH = 2
HD = 128
F = 768
TOP = 4
EXPERTS = 8
LAYERS = 2
STEP = 10
CAP = 160


NORM_EPS = 1e-06
ROPE_BASE = 1000000.0
BETA_ONE = 0.9
BETA_TWO = 0.95
ADAM_EPS = 1e-08
DECAY = 0.1
MASKED = -1e30


def rope_tables(positions):
    half_width = HD // 2
    frequency = ROPE_BASE ** (-(jnp.arange(half_width, dtype=jnp.float32) * 2.0 / HD))
    angles = positions.astype(jnp.float32)[:, None] * frequency[None, :]
    cosine, sine = jnp.cos(angles), jnp.sin(angles)
    return jnp.concatenate([cosine, cosine], axis=1), jnp.concatenate([-sine, sine], axis=1)


def normalize(values, gain_row):
    row_scale = lax.rsqrt(jnp.mean(values * values, axis=-1, keepdims=True) + NORM_EPS)
    return (values * row_scale * gain_row, row_scale)


def normalize_back(gradient, values, row_scale, gain_row):
    unit_rows = values * row_scale
    inner_grad = gradient * gain_row
    input_grad = row_scale * (
        inner_grad - unit_rows * jnp.mean(inner_grad * unit_rows, axis=-1, keepdims=True)
    )
    return (input_grad, jnp.sum(gradient * unit_rows, axis=0))


def adamw(parameter, moment, second, gradient, step_rate, decay_rate):
    moment = BETA_ONE * moment + (1.0 - BETA_ONE) * gradient
    second = BETA_TWO * second + (1.0 - BETA_TWO) * gradient * gradient
    direction = (
        moment / (1.0 - BETA_ONE**STEP) / (jnp.sqrt(second / (1.0 - BETA_TWO**STEP)) + ADAM_EPS)
    )
    return (parameter - step_rate * (direction + decay_rate * parameter), moment, second)


CTX = ("yo", "xi")
SHARD = ("zo", "zi", "core")
ALL = CTX + SHARD
GROUP = ("xi", "zi")
REPLICAS = ("yo", "zo", "core")


def flat_index(axes):
    index = 0
    for axis in axes:
        index = index * lax.axis_size(axis) + lax.axis_index(axis)
    return index


def shift_permutation(axes, offsets, back=False):
    sizes = [lax.axis_size(axis) for axis in axes]
    pairs = []
    for first in range(sizes[0]):
        for second in range(sizes[1]):
            target = ((first + offsets[0]) % sizes[0], (second + offsets[1]) % sizes[1])
            here = first * sizes[1] + second
            there = target[0] * sizes[1] + target[1]
            pairs.append((there, here) if back else (here, there))
    return pairs


def offsets_of(axes):
    sizes = [lax.axis_size(axis) for axis in axes]
    return [(a, b) for a in range(sizes[0]) for b in range(sizes[1])]


def send(value, axes, offsets, back=False):
    if offsets == (0, 0):
        return value
    return lax.ppermute(value, axes, shift_permutation(axes, offsets, back))


def source_index(axes, offsets):
    sizes = [lax.axis_size(axis) for axis in axes]
    return lax.rem(lax.axis_index(axes[0]) - offsets[0] + sizes[0], sizes[0]) * sizes[1] + lax.rem(
        lax.axis_index(axes[1]) - offsets[1] + sizes[1], sizes[1]
    )


def target_index(axes, offsets):
    sizes = [lax.axis_size(axis) for axis in axes]
    return lax.rem(lax.axis_index(axes[0]) + offsets[0], sizes[0]) * sizes[1] + lax.rem(
        lax.axis_index(axes[1]) + offsets[1], sizes[1]
    )


def positions_docs(block_map, lengths_row, ctx_index, block_rows):
    blocks = lax.dynamic_slice_in_dim(block_map, 2 * ctx_index, 2)
    offsets = jnp.arange(block_rows, dtype=jnp.int32)
    positions = (blocks[:, None] * block_rows + offsets[None, :]).reshape(-1)
    bounds = jnp.cumsum(lengths_row)
    documents = jnp.sum((positions[:, None] >= bounds[None, :]).astype(jnp.int32), axis=1)
    return (positions, documents)


def dispatch_tables(routes, gates):
    rows = routes.shape[0]
    hits = (routes[None] == jnp.arange(EXPERTS, dtype=jnp.int32)[:, None, None]).astype(jnp.float32)
    member = jnp.sum(hits, axis=-1)
    gate = jnp.sum(hits * gates[None], axis=-1)
    before = (jnp.arange(rows)[:, None] < jnp.arange(rows)[None, :]).astype(jnp.float32)
    rank = jnp.dot(member, before, preferred_element_type=jnp.float32)
    return jnp.stack([jnp.where(member > 0, rank, -1.0), gate], axis=1)


MESH = pl.DeviceIdType.MESH
QKV = (H + 2 * KVH) * HD


class Place:
    def __init__(self, sizes):
        self.yo_size, self.zo_size = sizes
        self.yo, self.xi, self.zo, self.zi, self.core = [lax.axis_index(axis) for axis in ALL]
        self.y_steps = range(1, self.yo_size)
        self.z_steps = range(1, self.zo_size)
        self.column = [(a, b) for a in range(self.zo_size) for b in range(2)]

    def at(self, y=0, x=0, z=0, w=0, core=0):
        return (
            lax.rem(self.yo + y, self.yo_size),
            1 - self.xi if x else self.xi,
            lax.rem(self.zo + z, self.zo_size),
            1 - self.zi if w else self.zi,
            1 - self.core if core else self.core,
        )

    def chip(self, y=0, x=0, z=0, w=0):
        yo, xi, zo, zi, core = self.at(y, x, z, w)
        return ((yo * 2 + xi) * self.zo_size + zo) * 2 + zi

    def back_y(self, y):
        return (self.yo_size - y) % self.yo_size

    def back_z(self, z):
        return (self.zo_size - z) % self.zo_size


class Wires:
    def __init__(self, send_sems, recv_sems):
        self.send_sems, self.recv_sems = send_sems, recv_sems
        self.started = []

    def send(self, source, target, name, device):
        copy = pltpu.make_async_remote_copy(
            src_ref=source,
            dst_ref=target,
            send_sem=self.send_sems.at[len(self.started)],
            recv_sem=self.recv_sems.at[name],
            device_id=device,
            device_id_type=MESH,
        )
        copy.start()
        self.started.append(copy)

    def arrive(self, target, name, device):
        pltpu.make_async_remote_copy(
            src_ref=target,
            dst_ref=target,
            send_sem=self.send_sems.at[0],
            recv_sem=self.recv_sems.at[name],
            device_id=device,
            device_id_type=MESH,
        ).wait_recv()

    def drain(self):
        for copy in self.started:
            copy.wait_send()


def greet(partners):
    barrier = pltpu.get_barrier_semaphore()
    for partner in partners:
        pl.semaphore_signal(barrier, inc=1, device_id=partner, device_id_type=MESH)
    pl.semaphore_wait(barrier, len(partners))


def mesh_sizes():
    return lax.axis_size("yo"), lax.axis_size("zo")


def add_rows(target, *parts):
    size = 16 if target.shape[0] % 16 == 0 else target.shape[0]

    def step(index, carry):
        rows = pl.ds(pl.multiple_of(index * size, size), size)
        total = target[rows, :].astype(jnp.float32)
        for part in parts:
            total = total + part[rows, :].astype(jnp.float32)
        target[rows, :] = total.astype(target.dtype)
        return carry

    lax.fori_loop(0, target.shape[0] // size, step, 0)


def together(*steps):
    alive = list(steps)
    while alive:
        for one in list(alive):
            try:
                next(one)
            except StopIteration:
                alive.remove(one)


def greet_layer(here):
    greet(
        [here.at(z=z, w=w) for z, w in here.column if (z, w) != (0, 0)]
        + [here.at(x=1), here.at(x=1, w=1), here.at(core=1)]
        + [here.at(y=y) for y in here.y_steps]
    )


def gather_attention_steps(here, wires, shards, wholes, even):
    count = len(shards)
    far = [offset for offset in here.column if offset != (0, 0)]
    mine = here.chip() * 2 + here.core
    other = here.at(core=1)

    def block(**offsets):
        return here.chip(**offsets) * 2 + here.core

    def name(kind, y, x, z, w, part):
        spot = (((kind * here.yo_size + y) * 2 + x) * here.zo_size + z) * 2 + w
        return spot * count + part

    for z, w in far:
        for part in range(count):
            wires.send(
                shards[part],
                wholes[part].at[mine],
                name(0, 0, 0, here.back_z(z), w, part),
                here.at(z=z, w=w),
            )

    def pass_on(source, y, x, z, w, part, to_x, to_y):
        target = wholes[part].at[block(y=y, x=x, z=z, w=w)]
        if to_x:
            wires.send(source, target, name(0, y, 1 - x, z, w, part), here.at(x=1))
        for step in here.y_steps if to_y else ():
            back = (y + here.back_y(step)) % here.yo_size
            wires.send(source, target, name(0, back, x, z, w, part), here.at(y=step))
        wires.send(source, target, name(1, y, x, z, w, part), other)

    for z, w in here.column:
        for part in range(count):
            if (z, w) == (0, 0):
                pass_on(shards[part], 0, 0, 0, 0, part, True, True)
                wholes[part][mine] = shards[part][...]
            else:
                source = wholes[part].at[block(z=z, w=w)]
                wires.arrive(source, name(0, 0, 0, z, w, part), other)
                pass_on(source, 0, 0, z, w, part, True, True)
        yield
    for z, w in here.column:
        for part in range(count):
            for y in here.y_steps:
                source = wholes[part].at[block(y=y, z=z, w=w)]
                wires.arrive(source, name(0, y, 0, z, w, part), other)
                pass_on(source, y, 0, z, w, part, not even or part % 2 == 0, False)
        yield
    for z, w in here.column:
        for part in range(count):
            source = wholes[part].at[block(x=1, z=z, w=w)]
            wires.arrive(source, name(0, 0, 1, z, w, part), other)
            pass_on(source, 0, 1, z, w, part, False, even and part % 2 == 1)
        yield
    for z, w in here.column:
        for part in range(count):
            for y in here.y_steps:
                source = wholes[part].at[block(y=y, x=1, z=z, w=w)]
                wires.arrive(source, name(0, y, 1, z, w, part), other)
                pass_on(source, y, 1, z, w, part, False, False)
        yield
    for y in range(here.yo_size):
        for x in range(2):
            for z, w in here.column:
                for part in range(count):
                    index = here.chip(y=y, x=x, z=z, w=w) * 2 + 1 - here.core
                    wires.arrive(wholes[part].at[index], name(1, y, x, z, w, part), other)


def gather_experts_steps(here, wires, shards, wholes):
    count = len(shards)
    group = offsets_of(GROUP)
    other = here.at(core=1)

    def name(kind, y, x, z, w, part):
        spot = (((kind * here.yo_size + y) * 2 + x) * here.zo_size + z) * 2 + w
        return spot * count + part

    def member(x, w):
        yo, xi, zo, zi, core = here.at(x=x, w=w)
        return xi * 2 + zi

    for x, w in group[1:]:
        for part in range(count):
            wires.send(
                shards[part].at[member(x, w)],
                wholes[part].at[0, here.chip()],
                name(0, 0, x, 0, w, part),
                here.at(x=x, w=w),
            )

    def pass_on(source, y, x, z, w, part, to_z, to_y):
        index = here.chip(y=y, x=x, z=z, w=w)
        for step in here.z_steps if to_z else ():
            back = (z + here.back_z(step)) % here.zo_size
            wires.send(
                source, wholes[part].at[0, index], name(0, y, x, back, w, part), here.at(z=step)
            )
        for step in here.y_steps if to_y else ():
            back = (y + here.back_y(step)) % here.yo_size
            wires.send(
                source, wholes[part].at[0, index], name(0, back, x, z, w, part), here.at(y=step)
            )
        wires.send(source, wholes[part].at[1, index], name(1, y, x, z, w, part), other)

    for x, w in group:
        for part in range(count):
            if (x, w) == (0, 0):
                pass_on(shards[part].at[member(0, 0)], 0, 0, 0, 0, part, True, True)
                wholes[part][0, here.chip()] = shards[part][member(0, 0)]
            else:
                source = wholes[part].at[0, here.chip(x=x, w=w)]
                wires.arrive(source, name(0, 0, x, 0, w, part), other)
                pass_on(source, 0, x, 0, w, part, True, True)
        yield
    for x, w in group:
        for part in range(count):
            for z in here.z_steps:
                source = wholes[part].at[0, here.chip(x=x, w=w, z=z)]
                wires.arrive(source, name(0, 0, x, z, w, part), other)
                pass_on(source, 0, x, z, w, part, False, True)
        yield
    for z in range(here.zo_size):
        for x, w in group:
            for part in range(count):
                for y in here.y_steps:
                    source = wholes[part].at[0, here.chip(y=y, x=x, w=w, z=z)]
                    wires.arrive(source, name(0, y, x, z, w, part), other)
                    pass_on(source, y, x, z, w, part, False, False)
            yield
    for y in range(here.yo_size):
        for z in range(here.zo_size):
            for x, w in group:
                for part in range(count):
                    target = wholes[part].at[1, here.chip(y=y, x=x, w=w, z=z)]
                    wires.arrive(target, name(1, y, x, z, w, part), other)


ATTENTION_PARTS = 3
EXPERT_PARTS = 2


def greet_experts(here):
    greet(
        [here.at(x=x, w=w) for x, w in offsets_of(GROUP)[1:]]
        + [here.at(z=z) for z in here.z_steps]
        + [here.at(y=y) for y in here.y_steps]
        + [here.at(core=1)]
    )


def greet_attention(here):
    greet(
        [here.at(z=z, w=w) for z, w in here.column if (z, w) != (0, 0)]
        + [here.at(x=1), here.at(core=1)]
        + [here.at(y=y) for y in here.y_steps]
    )


def gather_kernel(sizes, count, *refs):
    ins, outs, sems = refs[:count], refs[count : 2 * count], refs[2 * count :]
    here = Place(sizes)
    cut = ATTENTION_PARTS
    wires = [Wires(*sems[:2])]
    steps = [gather_attention_steps(here, wires[0], ins[:cut], outs[:cut], count == cut)]
    if count > cut:
        greet_layer(here)
        wires.append(Wires(*sems[2:]))
        steps.append(gather_experts_steps(here, wires[1], ins[cut:], outs[cut:]))
    else:
        greet_attention(here)
    together(*steps)
    for one in wires:
        one.drain()


def expert_sems(sizes):
    chips = sizes[0] * sizes[1] * 4
    sends = 3 + 4 * (sizes[0] + sizes[1]) + 4 * sizes[1] * sizes[0] + chips
    return [
        pltpu.SemaphoreType.DMA((EXPERT_PARTS * sends,)),
        pltpu.SemaphoreType.DMA((2 * chips * EXPERT_PARTS,)),
    ]


def gather(identity, attention_shards, expert_parts):
    sizes = mesh_sizes()
    chips = sizes[0] * sizes[1] * 4
    columns = sizes[1] * 2
    sends = ATTENTION_PARTS * ((columns - 1) + chips + columns * (2 * sizes[0] + 1) + chips)
    in_vmem = pl.BlockSpec(memory_space=pltpu.VMEM)
    count = len(attention_shards) + len(expert_parts)
    return pl.pallas_call(
        functools.partial(gather_kernel, sizes, count),
        out_shape=[
            jax.ShapeDtypeStruct((2 * chips,) + shard.shape, shard.dtype)
            for shard in attention_shards
        ]
        + [
            jax.ShapeDtypeStruct((2, chips) + part.shape[1:], part.dtype) for part in expert_parts
        ],
        in_specs=[in_vmem] * count,
        out_specs=[in_vmem] * count,
        scratch_shapes=[
            pltpu.SemaphoreType.DMA((sends,)),
            pltpu.SemaphoreType.DMA((2 * chips * ATTENTION_PARTS,)),
        ]
        + (expert_sems(sizes) if expert_parts else []),
        compiler_params=pltpu.CompilerParams(
            collective_id=identity, has_side_effects=True, vmem_limit_bytes=58 * 1024 * 1024
        ),
    )(*attention_shards, *expert_parts)


def sum_experts_steps(here, wires, whole, outs, first, second, third):
    count = len(whole)
    group = offsets_of(GROUP)
    other = here.at(core=1)
    chips = here.yo_size * here.zo_size * 4

    def place(y, z, member):
        return (y * here.zo_size + z) * 4 + member

    def name(kind, index, part):
        return (kind * chips + index) * count + part

    order = [
        (y, z, member)
        for y in list(here.y_steps) + [0]
        for z in list(here.z_steps) + [0]
        for member in (1, 2, 3, 0)
    ]
    for y, z, member in order:
        x, w = group[member]
        index = here.chip(y=y, x=x, z=z, w=w)
        spot = place(y, z, member)
        for part in range(count):
            wires.send(
                whole[part].at[1, index], first[part].at[spot], name(0, spot, part), other
            )
        if member == 0:
            yield
    for y, z, member in order:
        x, w = group[member]
        index = here.chip(y=y, x=x, z=z, w=w)
        spot = place(y, z, member)
        for part in range(count):
            total = first[part].at[spot]
            wires.arrive(total, name(0, spot, part), other)
            parts = [whole[part].at[0, index]]
            if y:
                add_rows(total, *parts)
                landing = place(here.back_y(y), z, member)
                wires.send(
                    total, second[part].at[landing - 4 * here.zo_size], name(1, landing, part), here.at(y=y)
                )
                continue
            for step in here.y_steps:
                spot_in = place(step, z, member)
                arrived = second[part].at[spot_in - 4 * here.zo_size]
                wires.arrive(arrived, name(1, spot_in, part), other)
                parts.append(arrived)
            if z:
                add_rows(total, *parts)
                landing = here.back_z(z) * 4 + member
                wires.send(
                    total, third[part].at[landing - 4], name(2, landing, part), here.at(z=z)
                )
                continue
            for step in here.z_steps:
                arrived = third[part].at[step * 4 + member - 4]
                wires.arrive(arrived, name(2, step * 4 + member, part), other)
                parts.append(arrived)
            add_rows(total, *parts)
            slot = here.xi * 2 + here.zi
            if member:
                wires.send(total, outs[part].at[slot], name(3, member, part), here.at(x=x, w=w))
            else:
                outs[part][slot] = total[...]
        yield
    for member in range(1, 4):
        x, w = group[member]
        yo, xi, zo, zi, core = here.at(x=x, w=w)
        for part in range(count):
            wires.arrive(outs[part].at[xi * 2 + zi], name(3, member, part), other)


def sum_attention_steps(here, wires, whole, outs, first, second, third, fourth):
    count = len(whole)
    columns = here.column
    other = here.at(core=1)
    width = len(columns)
    chips = here.yo_size * 2 * width

    def place(y, x, column):
        return (y * 2 + x) * width + column

    def name(kind, index, part):
        return (kind * chips + index) * count + part

    rounds = [
        (y, x, (column + 1) % width, part)
        for y, x in [(y, 1) for y in here.y_steps] + [(0, 1)] + [(y, 0) for y in here.y_steps] + [(0, 0)]
        for column in range(width)
        for part in range(count)
    ]
    for y, x, column, part in rounds:
        z, w = columns[column]
        spot = place(y, x, column)
        wires.send(
            whole[part].at[here.chip(y=y, x=x, z=z, w=w), 1 - here.core],
            first[part].at[spot],
            name(0, spot, part),
            other,
        )
        if (column, part) == (0, count - 1):
            yield
    for y, x, column, part in rounds:
        z, w = columns[column]
        spot = place(y, x, column)
        total = first[part].at[spot]
        wires.arrive(total, name(0, spot, part), other)
        parts = [whole[part].at[here.chip(y=y, x=x, z=z, w=w), here.core]]

        def take_in(buffer, kind, index, offset=0):
            arrived = buffer[part].at[index - offset]
            wires.arrive(arrived, name(kind, index, part), other)
            parts.append(arrived)

        def give(buffer, kind, index, device, offset=0):
            add_rows(total, *parts)
            wires.send(total, buffer[part].at[index - offset], name(kind, index, part), device)

        if x:
            give(second, 1, y * width + column, here.at(x=1))
            if part == count - 1:
                yield
            continue
        take_in(second, 1, y * width + column)
        if y:
            give(third, 2, here.back_y(y) * width + column, here.at(y=y), width)
            if part == count - 1:
                yield
            continue
        for step in here.y_steps:
            take_in(third, 2, step * width + column, width)
        if column:
            landing = columns.index((here.back_z(z), w))
            give(fourth, 3, landing, here.at(z=z, w=w), 1)
            if part == count - 1:
                yield
            continue
        for step in range(1, width):
            take_in(fourth, 3, step, 1)
        add_rows(total, *parts)
        outs[part][...] = total[...]


def sum_layer_kernel(sizes, *refs):
    both = ATTENTION_PARTS + EXPERT_PARTS
    cut = ATTENTION_PARTS
    ins, outs, rest = refs[:both], refs[both : 2 * both], refs[2 * both :]
    buffers, sems = rest[:-4], rest[-4:]
    attention = [buffers[level * cut : (level + 1) * cut] for level in range(4)]
    buffers = buffers[4 * cut :]
    experts = [buffers[level * EXPERT_PARTS : (level + 1) * EXPERT_PARTS] for level in range(3)]
    here = Place(sizes)
    wires = Wires(*sems[:2]), Wires(*sems[2:])
    greet_layer(here)
    together(
        sum_experts_steps(here, wires[1], ins[cut:], outs[cut:], *experts),
        sum_attention_steps(here, wires[0], ins[:cut], outs[:cut], *attention),
    )
    for one in wires:
        one.drain()


def sum_layer(attention_grads, expert_grads):
    sizes = mesh_sizes()
    chips = sizes[0] * sizes[1] * 4
    column = sizes[1] * 2
    attention = [grads.reshape(chips, 2, -1, grads.shape[1]) for grads in attention_grads]
    experts = [grads.reshape(2, chips, -1, D) for grads in expert_grads]
    in_vmem = pl.BlockSpec(memory_space=pltpu.VMEM)
    count = ATTENTION_PARTS + EXPERT_PARTS

    def held(blocks, sizes_of):
        return [
            pltpu.VMEM((sizes_of(part),) + block.shape[2:], jnp.bfloat16)
            for part, block in enumerate(blocks)
        ]

    return pl.pallas_call(
        functools.partial(sum_layer_kernel, sizes),
        out_shape=[jax.ShapeDtypeStruct(block.shape[2:], jnp.bfloat16) for block in attention]
        + [jax.ShapeDtypeStruct((4,) + block.shape[2:], jnp.bfloat16) for block in experts],
        in_specs=[in_vmem] * count,
        out_specs=[in_vmem] * count,
        scratch_shapes=held(attention, lambda part: chips)
        + held(attention, lambda part: sizes[0] * column)
        + held(attention, lambda part: (sizes[0] - 1) * column)
        + held(attention, lambda part: column - 1)
        + held(experts, lambda part: chips)
        + held(experts, lambda part: (sizes[0] - 1) * sizes[1] * 4)
        + held(experts, lambda part: (sizes[1] - 1) * 4)
        + [
            pltpu.SemaphoreType.DMA((3 * chips * ATTENTION_PARTS,)),
            pltpu.SemaphoreType.DMA((4 * chips * ATTENTION_PARTS,)),
            pltpu.SemaphoreType.DMA((3 * chips * EXPERT_PARTS,)),
            pltpu.SemaphoreType.DMA((4 * chips * EXPERT_PARTS,)),
        ],
        compiler_params=pltpu.CompilerParams(
            collective_id=5, has_side_effects=True, vmem_limit_bytes=62 * 1024 * 1024
        ),
    )(*attention, *experts)


def swap(value, axis):
    return lax.ppermute(value, axis, [(0, 1), (1, 0)])


def pick(value, index, axis=0):
    return lax.dynamic_index_in_dim(value, index, axis, keepdims=False)


def by_core(mine, theirs, axis):
    core = lax.axis_index("core")
    return jnp.where(
        core == 0, jnp.stack([mine, theirs], axis), jnp.stack([theirs, mine], axis)
    )


def gain_columns(gains):
    gains = gains.astype(jnp.bfloat16).T
    return jnp.pad(gains, ((0, 0), (0, 128 - gains.shape[1])))


def attention_shards(w_qkv, w_out, gains, layer):
    return [
        w_qkv[layer].astype(jnp.bfloat16),
        w_out[layer].astype(jnp.bfloat16),
        gain_columns(gains[layer]),
    ]


def expert_parts(w_gateup, w_down, layer):
    core = lax.axis_index("core")
    parts = []
    for shard in (w_gateup[layer], w_down[layer]):
        shard = shard.reshape((4, 2) + shard.shape[1:])
        theirs = swap(pick(shard, 1 - core, 1).astype(jnp.bfloat16), "core").astype(jnp.float32)
        pair = by_core(pick(shard, core, 1), theirs, 1).reshape(4, -1, D)
        parts.append(pair.astype(jnp.bfloat16))
    return parts


def attention_matrices(qkv, out, gain):
    gain = gain.reshape(D, 128)[:, :2].T.astype(jnp.float32)
    return qkv.reshape(D, QKV), out.reshape(D, D), gain


def expert_matrices(up, down):
    return up.reshape(2, D, 2 * F), down.reshape(2, F, D)


def layer_sums(grad_qkv, grad_out, grad_up, grad_down, grad_gains):
    core = lax.axis_index("core")
    attention = [
        grad_qkv.astype(jnp.bfloat16),
        grad_out.astype(jnp.bfloat16),
        gain_columns(grad_gains),
    ]
    qkv, out, gain, up, down = sum_layer(attention, [grad_up, grad_down])
    result = [qkv, out]
    for part in (up, down):
        part = part.astype(jnp.float32).reshape(4, 2, -1, D)
        theirs = swap(pick(part, 1 - core, 1).astype(jnp.bfloat16), "core").astype(jnp.float32)
        pair = by_core(pick(part, core, 1), theirs, 1)
        result.append(pair.reshape(EXPERTS, -1, D))
    return result + [gain[:, :2].T]


SQRT_HALF = 0.7071067811865476
PDF_SCALE = 0.3989422804014327
TILE = 384
TILES = F // TILE


def selections(table, columns):
    rows = table.shape[1]
    slots = lax.broadcasted_iota(jnp.int32, (CAP, rows), 0).astype(jnp.float32)
    take = (table[0:1, :] == slots).astype(jnp.bfloat16)
    slots = lax.broadcasted_iota(jnp.int32, (rows, CAP), 1).astype(jnp.float32)
    spread = (columns[:, 0:1] == slots).astype(jnp.bfloat16)
    return take, spread, columns[:, 1:2]


def dot(left, right, contract=(1, 0)):
    return lax.dot_general(
        left,
        right,
        (((contract[0],), (contract[1],)), ((), ())),
        preferred_element_type=jnp.float32,
    )


WAVES = ((0,), (3,), (1, 2))
TURNS = ((0, 2), (1, 1), (2, 2))


def moe_forward_kernel(sizes, background, *refs):
    tokens, tables, columns, up_w, down_w = refs[:5]
    extra = EXPERT_PARTS if background else 0
    shards, refs = refs[5 : 5 + extra], refs[5 + extra :]
    merged, slot_out, gate_out, up_out, active_out = refs[:5]
    wholes, refs = refs[5 : 5 + extra], refs[5 + extra :]
    chunks, leaving, coming, slot_in, result, total = refs[:6]
    sems = refs[6:]
    here = Place(sizes)
    wires = Wires(*sems[:2])
    partners = [here.at(x=x, w=w) for x, w in offsets_of(GROUP)]
    if background:
        greet_experts(here)
        other_wires = Wires(*sems[2:])
        steps = gather_experts_steps(here, other_wires, shards, wholes)
    else:
        greet(partners[1:])
        steps = iter(())
    for place in (3, 1, 2):
        wires.send(tokens, chunks.at[place - 1], place - 1, partners[place])
    next(steps, None)
    for wave, turns in zip(WAVES, TURNS):
        sources = []
        for place in wave:
            source = tokens if place == 0 else chunks.at[place - 1]
            if place:
                wires.arrive(source, place - 1, partners[place])
            sources.append(source)
        count = CAP * len(wave)
        rows = pl.ds(wave[0] * CAP, count)
        for expert in range(2):
            picks = [selections(tables[place, expert], columns[place, expert]) for place in wave]
            for index, source in enumerate(sources):
                chosen = dot(picks[index][0], source[...]).astype(jnp.bfloat16)
                slot_in[index * CAP : (index + 1) * CAP] = chosen
            slot_out[expert, rows, :] = slot_in[:count]

            def step(tile, carry, expert=expert, count=count, rows=rows):
                at_gate = pl.ds(pl.multiple_of(tile * TILE, TILE), TILE)
                at_up = pl.ds(pl.multiple_of(F + tile * TILE, TILE), TILE)
                gate = dot(slot_in[:count], up_w[expert, :, at_gate])
                up = dot(slot_in[:count], up_w[expert, :, at_up])
                active = (0.5 * gate * (1.0 + lax.erf(gate * SQRT_HALF)) * up).astype(jnp.bfloat16)
                gate_out[expert, rows, at_gate] = gate.astype(jnp.bfloat16)
                up_out[expert, rows, at_gate] = up.astype(jnp.bfloat16)
                active_out[expert, rows, at_gate] = active
                return carry

            lax.fori_loop(0, TILES, step, 0)

            def finish(tile, carry, expert=expert, count=count, rows=rows):
                lanes = pl.ds(pl.multiple_of(tile * 2 * TILE, TILE), 2 * TILE)
                result[:count, lanes] = dot(
                    active_out[expert, rows, :], down_w[expert, :, lanes]
                ).astype(jnp.bfloat16)
                return carry

            lax.fori_loop(0, D // (2 * TILE), finish, 0)
            for index in range(len(wave)):
                take, spread, gates = picks[index]
                share = dot(spread, result[index * CAP : (index + 1) * CAP]) * gates
                if expert == 0:
                    total[index] = share
                else:
                    total[index] += share
            for turn in range(turns[expert]):
                next(steps, None)
        for index, place in enumerate(wave):
            if place == 0:
                merged[...] = total[index]
            else:
                leaving[place - 1] = total[index].astype(jnp.bfloat16)
                wires.send(
                    leaving.at[place - 1], coming.at[place - 1], place + 2, partners[place]
                )
    for one in steps:
        pass
    for place in range(1, 4):
        wires.arrive(coming.at[place - 1], place + 2, partners[place])
        merged[...] += coming[place - 1].astype(jnp.float32)
    wires.drain()
    if background:
        other_wires.drain()


STAGES = 6


def moe_backward_kernel(sizes, *refs):
    gradient, tables, columns, up_w, down_w, slot_in, gate_in, up_in, active = refs[:9]
    merged, up_grads, down_grads = refs[9:12]
    chunks, leaving, coming, slot_grad, slots, total = refs[12:18]
    slot_out, gate_out, up_out, up_stage, down_stage = refs[18:23]
    here = Place(sizes)
    wires = Wires(*refs[23:25])
    stage_sems = refs[25]
    partners = [here.at(x=x, w=w) for x, w in offsets_of(GROUP)]
    greet(partners[1:])
    leaving[3] = gradient[...].astype(jnp.bfloat16)
    for place in (3, 1, 2):
        wires.send(leaving.at[3], chunks.at[place - 1], place - 1, partners[place])
    for wave in WAVES:
        sources = []
        for place in wave:
            source = gradient if place == 0 else chunks.at[place - 1]
            if place:
                wires.arrive(source, place - 1, partners[place])
            sources.append(source)
        count = CAP * len(wave)
        rows = pl.ds(wave[0] * CAP, count)
        for expert in range(2):
            picks = [selections(tables[place, expert], columns[place, expert]) for place in wave]
            for index, source in enumerate(sources):
                take, spread, gates = picks[index]
                weighted = (gates * source[...].astype(jnp.float32)).astype(jnp.bfloat16)
                slot_grad[index * CAP : (index + 1) * CAP] = dot(take, weighted).astype(jnp.bfloat16)
            slot_out[expert, rows, :] = slot_grad[:count]

            def step(tile, carry, expert=expert, count=count, rows=rows):
                at_gate = pl.ds(pl.multiple_of(tile * TILE, TILE), TILE)
                grad_act = dot(slot_grad[:count], down_w[expert, at_gate, :], (1, 1))
                gate = gate_in[expert, rows, at_gate].astype(jnp.float32)
                up = up_in[expert, rows, at_gate].astype(jnp.float32)
                below = 0.5 * (1.0 + lax.erf(gate * SQRT_HALF))
                slope = below + gate * PDF_SCALE * jnp.exp(-0.5 * gate * gate)
                gate_out[expert, rows, at_gate] = (grad_act * up * slope).astype(jnp.bfloat16)
                up_out[expert, rows, at_gate] = (grad_act * gate * below).astype(jnp.bfloat16)
                return carry

            lax.fori_loop(0, TILES, step, 0)

            def finish(tile, carry, expert=expert, count=count, rows=rows):
                lanes = pl.ds(pl.multiple_of(tile * 2 * TILE, TILE), 2 * TILE)
                part = dot(gate_out[expert, rows, :], up_w[expert, lanes, :F], (1, 1))
                part = part + dot(up_out[expert, rows, :], up_w[expert, lanes, F:], (1, 1))
                slots[:count, lanes] = part.astype(jnp.bfloat16)
                return carry

            lax.fori_loop(0, D // (2 * TILE), finish, 0)
            for index in range(len(wave)):
                share = dot(picks[index][1], slots[index * CAP : (index + 1) * CAP])
                if expert == 0:
                    total[index] = share
                else:
                    total[index] += share
        for index, place in enumerate(wave):
            if place == 0:
                merged[...] = total[index]
            else:
                leaving[place - 1] = total[index].astype(jnp.bfloat16)
                wires.send(
                    leaving.at[place - 1], coming.at[place - 1], place + 2, partners[place]
                )

    def copies(index):
        expert, tile, slot = lax.div(index, STAGES), lax.rem(index, STAGES), lax.rem(index, 2)
        up_rows = pl.ds(pl.multiple_of(tile * (D // STAGES), D // STAGES), D // STAGES)
        down_rows = pl.ds(pl.multiple_of(tile * (F // STAGES), F // STAGES), F // STAGES)
        pair = (
            pltpu.make_async_copy(
                up_stage.at[slot], up_grads.at[expert, up_rows], stage_sems.at[slot, 0]
            ),
            pltpu.make_async_copy(
                down_stage.at[slot], down_grads.at[expert, down_rows], stage_sems.at[slot, 1]
            ),
        )
        return expert, slot, up_rows, down_rows, pair

    def weight_step(index, carry):
        expert, slot, up_rows, down_rows, pair = copies(index)

        @pl.when(index >= 2)
        def _():
            for copy in copies(index - 2)[-1]:
                copy.wait()

        taken = slot_in[expert, :, up_rows]
        up_stage[slot, :, :F] = dot(taken, gate_out[expert], (0, 0)).astype(jnp.bfloat16)
        up_stage[slot, :, F:] = dot(taken, up_out[expert], (0, 0)).astype(jnp.bfloat16)
        down_stage[slot] = dot(active[expert, :, down_rows], slot_out[expert], (0, 0)).astype(
            jnp.bfloat16
        )
        for copy in pair:
            copy.start()
        return carry

    lax.fori_loop(0, 2 * STAGES, weight_step, 0)
    for index in range(2 * STAGES - 2, 2 * STAGES):
        for copy in copies(index)[-1]:
            copy.wait()
    for place in range(1, 4):
        wires.arrive(coming.at[place - 1], place + 2, partners[place])
        merged[...] += coming[place - 1].astype(jnp.float32)
    wires.drain()


def moe_call(kernel, identity, rows_in, tables, weights, extra, kinds, background=()):
    rows = rows_in.shape[0]
    slots = 4 * CAP
    sizes = mesh_sizes()
    chips = sizes[0] * sizes[1] * 4
    operands = [rows_in, tables, jnp.swapaxes(tables, 2, 3), *weights, *extra, *background]
    in_vmem = pl.BlockSpec(memory_space=pltpu.VMEM)
    more_sems = expert_sems(sizes) if background else []
    return pl.pallas_call(
        functools.partial(kernel, sizes, bool(background)),
        in_specs=[in_vmem] * len(operands),
        out_specs=[in_vmem] * (1 + len(kinds) + len(background)),
        out_shape=[jax.ShapeDtypeStruct((rows, D), jnp.float32)]
        + [jax.ShapeDtypeStruct((2, slots, width), jnp.bfloat16) for width in kinds]
        + [jax.ShapeDtypeStruct((2, chips) + part.shape[1:], part.dtype) for part in background],
        scratch_shapes=[
            pltpu.VMEM((3, rows, D), jnp.bfloat16),
            pltpu.VMEM((4, rows, D), jnp.bfloat16),
            pltpu.VMEM((3, rows, D), jnp.bfloat16),
            pltpu.VMEM((2 * CAP, D), jnp.bfloat16),
            pltpu.VMEM((2 * CAP, D), jnp.bfloat16),
            pltpu.VMEM((2, rows, D), jnp.float32),
            pltpu.SemaphoreType.DMA((6,)),
            pltpu.SemaphoreType.DMA((6,)),
        ]
        + more_sems,
        compiler_params=pltpu.CompilerParams(
            collective_id=identity, has_side_effects=True, vmem_limit_bytes=62 * 1024 * 1024
        ),
        cost_estimate=pl.CostEstimate(
            flops=48 * CAP * D * F, bytes_accessed=40_000_000, transcendentals=8 * CAP * F
        ),
    )(*operands)


def moe_forward(expert_in, tables, weights, background):
    merged, *kept = moe_call(
        moe_forward_kernel,
        2 if background else 3,
        expert_in,
        tables,
        weights,
        [],
        (D, F, F, F),
        background,
    )
    return merged, kept[:4], expert_matrices(*kept[4:]) if background else None


def moe_backward(gradient, tables, weights, kept):
    rows = gradient.shape[0]
    slots = 4 * CAP
    operands = [gradient, tables, jnp.swapaxes(tables, 2, 3), *weights, *kept]
    in_vmem, anywhere = pl.BlockSpec(memory_space=pltpu.VMEM), pl.BlockSpec(memory_space=pl.ANY)
    low = jnp.bfloat16
    return pl.pallas_call(
        functools.partial(moe_backward_kernel, mesh_sizes()),
        in_specs=[in_vmem] * len(operands),
        out_specs=[in_vmem, anywhere, anywhere],
        out_shape=[
            jax.ShapeDtypeStruct((rows, D), jnp.float32),
            jax.ShapeDtypeStruct((2, D, 2 * F), low),
            jax.ShapeDtypeStruct((2, F, D), low),
        ],
        scratch_shapes=[
            pltpu.VMEM((3, rows, D), low),
            pltpu.VMEM((4, rows, D), low),
            pltpu.VMEM((3, rows, D), low),
            pltpu.VMEM((2 * CAP, D), low),
            pltpu.VMEM((2 * CAP, D), low),
            pltpu.VMEM((2, rows, D), jnp.float32),
            pltpu.VMEM((2, slots, D), low),
            pltpu.VMEM((2, slots, F), low),
            pltpu.VMEM((2, slots, F), low),
            pltpu.VMEM((2, D // STAGES, 2 * F), low),
            pltpu.VMEM((2, F // STAGES, D), low),
            pltpu.SemaphoreType.DMA((6,)),
            pltpu.SemaphoreType.DMA((6,)),
            pltpu.SemaphoreType.DMA((2, 2)),
        ],
        compiler_params=pltpu.CompilerParams(
            collective_id=4, has_side_effects=True, vmem_limit_bytes=62 * 1024 * 1024
        ),
        cost_estimate=pl.CostEstimate(
            flops=96 * CAP * D * F, bytes_accessed=40_000_000, transcendentals=8 * CAP * F
        ),
    )(*operands)


def turned(vectors, cosine, sine):
    return vectors * cosine + pltpu.roll(vectors, HD // 2, 1) * sine


def project_kernel(stream, gain, weight, cosine, sine, normed, heads):
    tile = pl.program_id(0)

    @pl.when(tile == 0)
    def _():
        values = stream[...]
        scale = lax.rsqrt(jnp.mean(values * values, axis=-1, keepdims=True) + NORM_EPS)
        normed[...] = (values * scale * gain[...]).astype(jnp.bfloat16)

    result = dot(normed[...], weight[...])
    heads_here = result.shape[1] // HD
    for head in range(heads_here):
        lanes = slice(head * HD, (head + 1) * HD)

        @pl.when(tile * heads_here + head < H + KVH)
        def _(lanes=lanes):
            heads[:, lanes] = turned(result[:, lanes], cosine[...], sine[...]).astype(jnp.bfloat16)

        @pl.when(tile * heads_here + head >= H + KVH)
        def _(lanes=lanes):
            heads[:, lanes] = result[:, lanes].astype(jnp.bfloat16)


def project(stream, gain, weight, cosine, sine):
    rows, width = stream.shape[0], 4 * HD

    def same(shape):
        return pl.BlockSpec(shape, lambda tile: (0, 0))

    return pl.pallas_call(
        project_kernel,
        grid=(QKV // width,),
        in_specs=[
            same((rows, D)),
            same((1, D)),
            pl.BlockSpec((D, width), lambda tile: (0, tile)),
            same((rows, HD)),
            same((rows, HD)),
        ],
        out_specs=[
            same((rows, D)),
            pl.BlockSpec((rows, width), lambda tile: (0, tile)),
        ],
        out_shape=[
            jax.ShapeDtypeStruct((rows, D), jnp.bfloat16),
            jax.ShapeDtypeStruct((rows, QKV), jnp.bfloat16),
        ],
        compiler_params=pltpu.CompilerParams(vmem_limit_bytes=60 * 1024 * 1024),
        cost_estimate=pl.CostEstimate(
            flops=2 * rows * D * QKV, bytes_accessed=12_000_000, transcendentals=rows
        ),
    )(stream, gain[None], weight, cosine, sine)


def head_columns(rows, offset):
    return pl.BlockSpec((rows, HD), lambda head: (0, offset + head // (H // KVH)))


def attention_kernel(*refs):
    query, allowed = refs[:2]
    attended, total = refs[-3:-1]
    scores = refs[-1]
    count = (len(refs) - 5) // 2
    keys, values = refs[2 : 2 + count], refs[2 + count : 2 + 2 * count]
    rows = query.shape[0]
    for index, key in enumerate(keys):
        lanes = slice(index * rows, (index + 1) * rows)
        part = dot(query[...], key[...], (1, 1)) * HD ** (-0.5)
        scores[:, lanes] = jnp.where(allowed[:, lanes] > 0, part, MASKED)
    row_max = jnp.max(scores[...], axis=-1, keepdims=True)
    exponent = jnp.exp(scores[...] - row_max)
    row_total = jnp.sum(exponent, axis=-1, keepdims=True)
    probabilities = (exponent * (1.0 / row_total)).astype(jnp.bfloat16)
    result = None
    for index, value in enumerate(values):
        part = dot(probabilities[:, index * rows : (index + 1) * rows], value[...])
        result = part if result is None else result + part
    attended[...] = result.astype(jnp.bfloat16)
    total[0] = jnp.broadcast_to(row_max + jnp.log(row_total), total.shape[1:])


def attention_forward(heads, blocks, allowed):
    rows, count = heads.shape[0], len(blocks)
    one = pl.BlockSpec((rows, HD), lambda head: (0, head))
    return pl.pallas_call(
        attention_kernel,
        grid=(H,),
        in_specs=[one, pl.BlockSpec(allowed.shape, lambda head: (0, 0))]
        + [head_columns(rows, 0)] * count
        + [head_columns(rows, KVH)] * count,
        out_specs=[one, pl.BlockSpec((1, rows, HD), lambda head: (head, 0, 0))],
        out_shape=[
            jax.ShapeDtypeStruct((rows, H * HD), jnp.bfloat16),
            jax.ShapeDtypeStruct((H, rows, HD), jnp.float32),
        ],
        scratch_shapes=[pltpu.VMEM((rows, rows * count), jnp.float32)],
        compiler_params=pltpu.CompilerParams(vmem_limit_bytes=60 * 1024 * 1024),
        cost_estimate=pl.CostEstimate(
            flops=4 * H * HD * rows * rows * count,
            bytes_accessed=8_000_000,
            transcendentals=H * rows * rows * count,
        ),
    )(heads, allowed, *blocks, *blocks)


def weight_grad_kernel(rows_in, grads, out):
    out[...] = dot(rows_in[...], grads[...], (0, 0)).astype(jnp.bfloat16)


def weight_grad(rows_in, grads):
    rows, width = grads.shape
    tile = D // 3
    return pl.pallas_call(
        weight_grad_kernel,
        grid=(3,),
        in_specs=[
            pl.BlockSpec((rows, tile), lambda step: (0, step)),
            pl.BlockSpec((rows, width), lambda step: (0, 0)),
        ],
        out_specs=pl.BlockSpec((tile, width), lambda step: (step, 0)),
        out_shape=jax.ShapeDtypeStruct((D, width), jnp.bfloat16),
        compiler_params=pltpu.CompilerParams(vmem_limit_bytes=60 * 1024 * 1024),
        cost_estimate=pl.CostEstimate(
            flops=2 * rows * D * width, bytes_accessed=2 * D * width, transcendentals=0
        ),
    )(rows_in, grads)


def rotate_back(gradient, cosine_table, sine_table):
    half_width = gradient.shape[-1] // 2
    first_half = gradient[..., :half_width]
    second_half = gradient[..., half_width:]
    return jnp.concatenate(
        [
            first_half * cosine_table + second_half * sine_table,
            second_half * cosine_table - first_half * sine_table,
        ],
        axis=-1,
    )


def plain_backward(queries, keys_all, values_all, allowed, totals, grad_attended):
    group_size = H // KVH
    score_scale = HD ** (-0.5)
    grad_queries = []
    grad_keys = []
    grad_values = []
    for head_group in range(KVH):
        query_part = queries[:, head_group * group_size : (head_group + 1) * group_size, :]
        grad_part = grad_attended[:, head_group * group_size : (head_group + 1) * group_size, :]
        keys_part = keys_all[:, head_group, :]
        scores = (
            jnp.einsum("tjd,kd->jtk", query_part, keys_part, preferred_element_type=jnp.float32)
            * score_scale
        )
        probabilities = jnp.where(allowed[None], jnp.exp(scores - totals[head_group]), 0.0)
        grad_probs = jnp.einsum(
            "tjd,kd->jtk",
            grad_part,
            values_all[:, head_group, :],
            preferred_element_type=jnp.float32,
        )
        grad_scores = probabilities * (
            grad_probs - jnp.sum(probabilities * grad_probs, axis=-1, keepdims=True)
        )
        grad_scores = grad_scores.astype(jnp.bfloat16)
        grad_queries.append(
            jnp.einsum("jtk,kd->tjd", grad_scores, keys_part, preferred_element_type=jnp.float32)
            * score_scale
        )
        grad_keys.append(
            jnp.einsum("jtk,tjd->kd", grad_scores, query_part, preferred_element_type=jnp.float32)
            * score_scale
        )
        grad_values.append(
            jnp.einsum(
                "jtk,tjd->kd",
                probabilities.astype(jnp.bfloat16),
                grad_part,
                preferred_element_type=jnp.float32,
            )
        )
    return (
        jnp.concatenate(grad_queries, axis=1),
        jnp.stack(grad_keys, axis=1),
        jnp.stack(grad_values, axis=1),
    )


def layer_forward(stream, attn_w, expert_w, ahead, tables, allowed, cosine_table, sine_table):
    qkv_w, out_w, gain_full = attn_w
    attn_in, heads = project(stream, gain_full[0], qkv_w, cosine_table, sine_table)
    own = heads[:, H * HD :]
    blocks = [send(own, CTX, offsets) for offsets in offsets_of(CTX)]
    attended, totals = attention_forward(heads, blocks, allowed)
    middle_stream = stream + jnp.dot(attended, out_w, preferred_element_type=jnp.float32)
    normed_two, scale_two = normalize(middle_stream, gain_full[1])
    expert_in = normed_two.astype(jnp.bfloat16)
    merged, kept, gathered = moe_forward(expert_in, tables, expert_w, ahead)
    record = {
        "stream": stream,
        "attn_in": attn_in,
        "heads": heads,
        "blocks": blocks,
        "totals": totals,
        "attended": attended,
        "middle": middle_stream,
        "scale_two": scale_two,
        "kept": kept,
    }
    return (record, middle_stream + merged, gathered)


def layer_backward(gradient, record, attn_w, expert_w, tables, allowed, cosine_table, sine_table):
    qkv_w, out_w, gain_full = attn_w
    grad_normed, grad_up, grad_down = moe_backward(gradient, tables, expert_w, record["kept"])
    grad_in_two, grad_gain_two = normalize_back(
        grad_normed, record["middle"], record["scale_two"], gain_full[1]
    )
    grad_middle = gradient + grad_in_two
    grad_middle_low = grad_middle.astype(jnp.bfloat16)
    grad_out = weight_grad(record["attended"], grad_middle_low)
    grad_attended = jnp.dot(grad_middle_low, out_w.T, preferred_element_type=jnp.float32)
    keys_all = jnp.concatenate(record["blocks"], axis=0).reshape(-1, 2 * KVH, HD)
    totals = record["totals"][:, :, :1].reshape(KVH, H // KVH, -1, 1)
    row_count = gradient.shape[0]
    grad_queries, grad_keys_all, grad_values_all = plain_backward(
        record["heads"][:, : H * HD].reshape(-1, H, HD),
        keys_all[:, :KVH],
        keys_all[:, KVH:],
        allowed > 0,
        [totals[0], totals[1]],
        grad_attended.astype(jnp.bfloat16).reshape(-1, H, HD),
    )
    both_all = jnp.concatenate([grad_keys_all, grad_values_all], axis=1)
    both = None
    for place, offsets in enumerate(offsets_of(CTX)):
        part = both_all[place * row_count : (place + 1) * row_count]
        if offsets != (0, 0):
            part = send(part.astype(jnp.bfloat16), CTX, offsets, back=True).astype(jnp.float32)
        both = part if both is None else both + part
    grad_keys, grad_values = both[:, :KVH], both[:, KVH:]
    ct, st = cosine_table[:, None, : HD // 2], sine_table[:, None, HD // 2 :]
    grad_projected = jnp.concatenate(
        [
            rotate_back(grad_queries, ct, st).reshape(row_count, H * HD),
            rotate_back(grad_keys, ct, st).reshape(row_count, KVH * HD),
            grad_values.reshape(row_count, KVH * HD),
        ],
        axis=1,
    ).astype(jnp.bfloat16)
    grad_qkv = weight_grad(record["attn_in"], grad_projected)
    grad_normed_one = jnp.dot(grad_projected, qkv_w.T, preferred_element_type=jnp.float32)
    unused, scale_one = normalize(record["stream"], gain_full[0])
    grad_in_one, grad_gain_one = normalize_back(
        grad_normed_one, record["stream"], scale_one, gain_full[0]
    )
    grad_gains = jnp.stack([grad_gain_one, grad_gain_two])
    return (grad_middle + grad_in_one, (grad_qkv, grad_out, grad_up, grad_down, grad_gains))


def on_device(
    tokens,
    cotangent,
    routes,
    gate_weights,
    lengths,
    block_map,
    w_qkv,
    w_out,
    w_gateup,
    w_down,
    gains,
    m_qkv,
    v_qkv,
    m_out,
    v_out,
    m_gateup,
    v_gateup,
    m_down,
    v_down,
    m_gains,
    v_gains,
):
    row_count = tokens.shape[1]
    block_rows = row_count // 2
    own_pos, own_doc = positions_docs(block_map, lengths[0], flat_index(CTX), block_rows)
    places = [
        positions_docs(block_map, lengths[0], source_index(CTX, offsets), block_rows)
        for offsets in offsets_of(CTX)
    ]
    key_pos = jnp.concatenate([place[0] for place in places])
    key_doc = jnp.concatenate([place[1] for place in places])
    allowed = (own_doc[:, None] == key_doc[None, :]) & (key_pos[None, :] <= own_pos[:, None])
    allowed = allowed.astype(jnp.float32)
    cosine_table, sine_table = rope_tables(own_pos)
    own_tables = jnp.stack(
        [dispatch_tables(routes[layer, 0], gate_weights[layer, 0]) for layer in range(LAYERS)]
    )
    core = lax.axis_index("core")
    group_tables = []
    for offsets in offsets_of(GROUP):
        theirs = lax.dynamic_slice_in_dim(own_tables, 2 * target_index(GROUP, offsets), 2, axis=1)
        theirs = jnp.where(core == 0, theirs, theirs[:, ::-1])
        group_tables.append(send(theirs, GROUP, offsets))
    group_tables = jnp.stack(group_tables, axis=1)
    stream = tokens[0].astype(jnp.float32)
    records = []
    shards = [attention_shards(w_qkv, w_out, gains, layer) for layer in range(LAYERS)]
    parts = [expert_parts(w_gateup, w_down, layer) for layer in range(LAYERS)]
    first = gather(0, shards[0], [])
    parts[0], first = lax.optimization_barrier((parts[0], first))
    second = gather(1, shards[1], parts[0])
    cut = ATTENTION_PARTS
    attn_w = [attention_matrices(*first), attention_matrices(*second[:cut])]
    expert_w = [expert_matrices(*second[cut:]), None]
    for layer_index in range(LAYERS):
        ahead = [] if layer_index else parts[1]
        record, stream, gathered = layer_forward(
            stream,
            attn_w[layer_index],
            expert_w[layer_index],
            ahead,
            group_tables[layer_index],
            allowed,
            cosine_table,
            sine_table,
        )
        records.append(record)
        if ahead:
            expert_w[1] = gathered
    output = stream.astype(jnp.bfloat16)[None]
    gradient = cotangent[0].astype(jnp.float32)
    rates = (D ** (-0.5), 0.5, D ** (-0.5), (F // 8) ** (-0.5), 1.0)
    decays = (DECAY, DECAY, DECAY, DECAY, 0.0)
    params = (w_qkv, w_out, w_gateup, w_down, gains)
    firsts = (m_qkv, m_out, m_gateup, m_down, m_gains)
    seconds = (v_qkv, v_out, v_gateup, v_down, v_gains)
    sums = [None] * LAYERS
    for layer_index in reversed(range(LAYERS)):
        gradient, layer_grads = layer_backward(
            gradient,
            records[layer_index],
            attn_w[layer_index],
            expert_w[layer_index],
            group_tables[layer_index],
            allowed,
            cosine_table,
            sine_table,
        )
        sums[layer_index] = layer_sums(*layer_grads)
    updated = []
    for which in range(5):
        total = jnp.stack([sums[layer][which] for layer in range(LAYERS)]).astype(jnp.float32)
        updated.extend(
            adamw(
                params[which], firsts[which], seconds[which], total, rates[which], decays[which]
            )
        )
    return (output, gradient[None], *updated)


def solution(mesh):
    ctx_size, shard_size = mesh.shape["ctx"], mesh.shape["shard"]
    fine = Mesh(mesh.devices.reshape(ctx_size // 2, 2, shard_size // 4, 2, 2), ALL)
    tokens = P(SHARD, CTX, None)
    routed = P(None, SHARD, CTX, None)
    rows_two = P(None, ALL, None)
    rows_three = P(None, None, ALL, None)
    gain = P(None, None, ALL)
    weights = (rows_two, rows_two, rows_three, rows_three, gain)
    states = tuple(spec for spec in weights for which in range(2))
    return jax.shard_map(
        on_device,
        mesh=fine,
        in_specs=(tokens, tokens, routed, routed, P(SHARD, None), P()) + weights + states,
        out_specs=(tokens, tokens) + tuple(spec for spec in weights for which in range(3)),
        check_vma=False,
    )
```
